32 devices in a mesh: dp: 2 (over x), mp: 4 (over y, core), width: 4 (over z).
Axes of the slice: x: 2, y: 2, z: 4, core: 2. Of those that a mesh axis runs over, the one named last changes fastest.
Arguments:
- tokens: bfloat16 [16, 1024, 512], P(('dp', 'width'), 'mp'), may hold values from -6 to 6
- segments: int32 [16, 1024], P(('dp', 'width')), may hold values from -1 to 7, as said below
- cotangent: bfloat16 [16, 1024, 512], P(('dp', 'width'), 'mp'), may hold values from -6 to 6
- norm_gains: bfloat16 [2, 2, 512], P(None, None, ('dp', 'width')), may hold values from 0.5 to 1.5
- biases: bfloat16 [2, 4, 512], P(None, None, ('dp', 'width')), may hold values from -3 to 3
- w_qkv: bfloat16 [2, 512, 3, 512], P(None, ('dp', 'width'), None, 'mp'), may hold values from -0.375 to 0.375
- w_out: bfloat16 [2, 512, 512], P(None, 'mp', ('dp', 'width')), may hold values from -3 to 3
- w_gate: bfloat16 [2, 2, 512, 512], P(None, None, ('dp', 'width'), 'mp'), may hold values from -0.25 to 0.25
- w_up: bfloat16 [2, 512, 2048], P(None, ('dp', 'width'), 'mp'), may hold values from -0.25 to 0.25
- w_down: bfloat16 [2, 2048, 512], P(None, 'mp', ('dp', 'width')), may hold values from -0.125 to 0.125
Outputs:
- output: float32 [16, 1024, 512], P(('dp', 'width'), 'mp')
- d_tokens: float32 [16, 1024, 512], P(('dp', 'width'), 'mp')
- d_norm_gains: float32 [2, 2, 512], P(None, None, ('dp', 'width'))
- d_norm_biases: float32 [2, 2, 512], P(None, None, ('dp', 'width'))
- d_gate_biases: float32 [2, 2, 512], P(None, None, ('dp', 'width'))
- d_w_qkv: float32 [2, 512, 3, 512], P(None, ('dp', 'width'), None, 'mp')
- d_w_out: float32 [2, 512, 512], P(None, 'mp', ('dp', 'width'))
- d_w_gate: float32 [2, 2, 512, 512], P(None, None, ('dp', 'width'), 'mp')
- d_w_up: float32 [2, 512, 2048], P(None, ('dp', 'width'), 'mp')
- d_w_down: float32 [2, 2048, 512], P(None, 'mp', ('dp', 'width'))
The draws below stay inside these ranges and needn't reach their ends.
Inputs may be any that keep to these rules, and one draw needn't show every extreme that they name: `segments`: ids never fall along a packed row; -1 marks padding, which fills the end of a row. Of the 2 rows of one index of dp and width, one, chosen by the seed, is a single sequence of 1024 positions; every other row holds sequences 0 to 7, each of 32 to 64 positions, then padding.
All inputs are finite; a program needn't handle non-finite values.
Results may differ from the reference program's by a relative error of at most 0.025.
Values may be sent and summed in bfloat16 or wider, within the bound.
No kernel may reach another device: no remote copies, remote signals or barrier semaphores. Data moves between devices by JAX's collectives and lax.ppermute only.
A program may use at most 192 MiB of HBM per device.

```python
import jax
import jax.numpy as jnp
from jax import lax

D = 512
HEADS = 8
HEAD_DIM = 64
FF = 2048
PACK = 1024
LAYERS = 2
MICRO = 2
ROWS = 16


def draw_segments(key, part):
    key = jax.random.fold_in(key, 11)
    key_full, key_len = jax.random.split(key, 2)
    groups = ROWS // MICRO
    chosen = jax.random.randint(key_full, (groups, 1), 0, MICRO)
    full_row = (jnp.arange(MICRO)[None, :] == chosen).reshape(ROWS)
    shortest = max(2, PACK // 32)
    longest = max(shortest + 1, PACK // 16)
    lengths = jax.random.randint(key_len, (ROWS, 8), shortest, longest + 1)
    ends = jnp.cumsum(lengths, axis=1)
    positions = jnp.arange(PACK)
    seg_ids = jnp.sum((ends[:, None, :] <= positions[None, :, None]).astype(jnp.int32), axis=2)
    seg_ids = jnp.where(positions[None, :] < ends[:, 7:8], seg_ids, -1)
    return jnp.where(full_row[:, None], 0, seg_ids).astype(jnp.int32)


def spiked(drawn, stream_key, source, target, shards_of, factor):
    def block_of(axis_at):
        return (jnp.arange(drawn.shape[axis_at]) // (drawn.shape[axis_at] // shards_of)).reshape((-1,) + (1,) * (drawn.ndim - 1 - axis_at))

    near = jax.random.permutation(stream_key, shards_of)[block_of(target)]
    far = (block_of(target) + shards_of // 2) % shards_of
    return jnp.where((block_of(source) == near) | (block_of(source) == far), factor * drawn, drawn)


def block_levels(rng, shape, shards, least, largest):
    def one(position, blocks):
        heights = jax.random.uniform(jax.random.fold_in(jax.random.fold_in(rng, 6), position), (blocks,), jnp.float32, least / len(shards), largest / len(shards))
        return jnp.repeat(jnp.exp(heights), shape[position] // blocks).reshape((-1,) + (1,) * (len(shape) - position - 1))

    factor_of = one(*shards[0])
    for cut in shards[1:]:
        factor_of = factor_of * one(*cut)
    return factor_of


def gaussian(stream_key, dims, width, most, cuts=(), dtype=jnp.bfloat16):
    values = width * jax.random.normal(stream_key, dims, jnp.float32)
    if cuts:
        values = values * block_levels(stream_key, dims, cuts, -0.22, 0.18)
    return jnp.clip(values, -most, most).astype(dtype)


def heavy_noise(stream_key, dims, deviation, bound, shards, heavy, held_as=jnp.bfloat16):
    entries = deviation * jax.random.normal(stream_key, dims, jnp.float32)
    if shards:
        entries = entries * block_levels(stream_key, dims, shards, -0.22, 0.18)
    return jnp.clip(spiked(entries, jax.random.fold_in(stream_key, 3), *heavy), -bound, bound).astype(held_as)


def setup_inputs(seed: int = 0) -> dict:
    key_of = jax.random.split(jax.random.key(seed), 11)
    return {
        "tokens": gaussian(key_of[0], (ROWS, PACK, D), 1.0, 6.0, ((0, 8), (1, 4))),
        "segments": draw_segments(jax.random.fold_in(key_of[10], 71), 0),
        "cotangent": heavy_noise(key_of[2], (ROWS, PACK, D), 1.0, 6.0, ((0, 8), (1, 4)), (0, 2, 8, 2.0)),
        "norm_gains": jnp.clip(1.0 + 0.1 * jax.random.normal(key_of[3], (LAYERS, 2, D), jnp.float32), 0.5, 1.5).astype(jnp.bfloat16),
        "biases": gaussian(key_of[4], (LAYERS, 4, D), 0.5, 3.0, ((2, 8),)),
        "w_qkv": gaussian(key_of[5], (LAYERS, D, 3, D), (D // 2) ** -0.5, 0.375, ((1, 8), (3, 4))),
        "w_out": gaussian(key_of[6], (LAYERS, D, D), (max(2, D // 128)) ** -0.5, 3.0, ((1, 4), (2, 8))),
        "w_gate": gaussian(key_of[7], (LAYERS, 2, D, D), D ** -0.5, 0.25, ((2, 8), (3, 4))),
        "w_up": gaussian(key_of[8], (LAYERS, D, FF), D ** -0.5, 0.25, ((1, 8), (2, 4))),
        "w_down": gaussian(key_of[9], (LAYERS, FF, D), FF ** -0.5, 0.125, ((1, 4), (2, 8))),
    }


norm_eps = 1e-05

@jax.custom_vjp
def low(v):
    return lax.optimization_barrier(v.astype(jnp.bfloat16)).astype(jnp.float32)

@jax.custom_vjp
def low_back(v):
    return v

def low_keep(v):
    return (low(v), None)

def low_pass(kept, grad):
    return (grad,)

def back_keep(v):
    return (v, None)

def back_low(kept, grad):
    return (low(grad),)
low.defvjp(low_keep, low_pass)
low_back.defvjp(back_keep, back_low)

def layer_norm(values, gain_row, bias_row):
    mean_val = lax.optimization_barrier(jnp.mean(values, axis=-1, keepdims=True))
    centred = values - mean_val
    spread = lax.optimization_barrier(jnp.mean(centred * centred, axis=-1, keepdims=True))
    return centred * lax.rsqrt(spread + norm_eps) * gain_row + bias_row

def mat_mul(left_mat, right_mat):
    return jnp.einsum('rpd,df->rpf', left_mat, right_mat, precision=lax.Precision.HIGHEST)

def attend_row(row_args):
    queries, key_rows, value_rows, seg_row = row_args
    positions = jnp.arange(PACK)
    allowed = (seg_row[:, None] == seg_row[None, :]) & (positions[None, :] <= positions[:, None])
    scores = jnp.einsum('qhd,khd->hqk', queries, key_rows, precision=lax.Precision.HIGHEST) * HEAD_DIM ** (-0.5)
    scores = low_back(scores)
    scores = jnp.where(allowed[None], scores, -1e+30)
    top_score = lax.optimization_barrier(jnp.max(scores, axis=-1, keepdims=True))
    exp_scores = jnp.exp(scores - top_score)
    probs_row = low(exp_scores / lax.optimization_barrier(jnp.sum(exp_scores, axis=-1, keepdims=True)))
    return jnp.einsum('hqk,khd->qhd', probs_row, value_rows, precision=lax.Precision.HIGHEST)

def run_layers(tokens, norm_gains, biases, w_qkv, w_out, w_gate, w_up, w_down, segments):
    row_count = tokens.shape[0]
    heads_shape = (row_count, PACK, HEADS, HEAD_DIM)
    residual = tokens
    for layer_index in range(LAYERS):
        normed = low(layer_norm(residual, norm_gains[layer_index, 0], biases[layer_index, 0]))
        mixed_qkv = jnp.einsum('rpd,dcf->rpcf', normed, w_qkv[layer_index], precision=lax.Precision.HIGHEST)
        mixed_qkv = low(low_back(mixed_qkv))
        attended = lax.map(jax.checkpoint(attend_row), (mixed_qkv[:, :, 0].reshape(heads_shape), mixed_qkv[:, :, 1].reshape(heads_shape), mixed_qkv[:, :, 2].reshape(heads_shape), segments))
        attended = low(low_back(attended.reshape(row_count, PACK, D)))
        gate_pre = low_back(mat_mul(normed, w_gate[layer_index, 0]) + biases[layer_index, 1])
        branch_sum = low_back(mat_mul(attended, w_out[layer_index]) + jax.nn.sigmoid(gate_pre) * normed)
        middle = residual + branch_sum
        normed_two = low(layer_norm(middle, norm_gains[layer_index, 1], biases[layer_index, 2]))
        hidden = low_back(mat_mul(normed_two, w_up[layer_index]))
        active = low(jax.nn.gelu(hidden, approximate=True))
        gate_two = low_back(mat_mul(normed_two, w_gate[layer_index, 1]) + biases[layer_index, 3])
        branch_two = low_back(mat_mul(active, w_down[layer_index]) + jax.nn.sigmoid(gate_two) * normed_two)
        residual = middle + branch_two
    return residual

def reference(tokens, segments, cotangent, norm_gains, biases, w_qkv, w_out, w_gate, w_up, w_down):
    floats = tuple((array.astype(jnp.float32) for array in (tokens, norm_gains, biases, w_qkv, w_out, w_gate, w_up, w_down)))

    def forward(*params):
        return run_layers(*params, segments)
    output, pull_back = jax.vjp(forward, *floats)
    valid_rows = (segments >= 0).astype(jnp.float32)
    grad_terms = pull_back(cotangent.astype(jnp.float32) * valid_rows[:, :, None])
    bias_grads = grad_terms[2]
    return (output, grad_terms[0], grad_terms[1], bias_grads[:, 0::2], bias_grads[:, 1::2], grad_terms[3], grad_terms[4], grad_terms[5], grad_terms[6], grad_terms[7])
```

```python
import functools

import jax
import jax.numpy as jnp
from jax import lax
from jax.experimental import pallas as pl
from jax.experimental.pallas import tpu as pltpu
from jax.sharding import PartitionSpec as P

HEAD_DIM = 64
LANE = 128
NORM_EPS = 1e-05
SPAN = 256

F32 = jnp.float32
BF16 = jnp.bfloat16


def nn(a, b):
    return jnp.dot(a, b, preferred_element_type=F32)


def nt(a, b):
    return lax.dot_general(a, b, (((1,), (1,)), ((), ())), preferred_element_type=F32)


def tn(a, b):
    return lax.dot_general(a, b, (((0,), (0,)), ((), ())), preferred_element_type=F32)


def sds(shape, dtype):
    return jax.ShapeDtypeStruct(shape, dtype)


def call(body, name, out_shape, args, smem=0, scratch=(), flops=0):
    specs = [pl.BlockSpec(memory_space=pltpu.SMEM)] * smem
    specs += [pl.BlockSpec(memory_space=pltpu.VMEM)] * (len(args) - smem)
    nbytes = sum(a.size * a.dtype.itemsize for a in args)
    nbytes += sum(o.size * o.dtype.itemsize for o in jax.tree.leaves(out_shape))
    return pl.pallas_call(
        body,
        name=name,
        out_shape=out_shape,
        in_specs=specs,
        out_specs=jax.tree.map(lambda _: pl.BlockSpec(memory_space=pltpu.VMEM), out_shape),
        scratch_shapes=list(scratch),
        cost_estimate=pl.CostEstimate(flops=flops, bytes_accessed=nbytes, transcendentals=0),
        compiler_params=pltpu.CompilerParams(vmem_limit_bytes=56 * 2**20),
    )(*args)


def col(start):
    return pl.multiple_of(start, LANE)


def unpack_body(order, plan, per, me_ref, *refs):
    parts, outs = refs[: len(order)], refs[len(order) :]
    me_m, me_d = me_ref[0], me_ref[1]
    for ref, slots in zip(parts, order):
        for at, (mx, dx) in enumerate(slots):
            m = jnp.bitwise_xor(me_m, mx)
            rows = pl.ds(pl.multiple_of(jnp.bitwise_xor(me_d, dx) * per, per), per)
            for b, (which, stride, offset) in enumerate(plan):
                block = ref[at, b * per : (b + 1) * per, :]
                if stride is None:
                    if mx == 0:
                        outs[which][rows, :] = block
                else:
                    outs[which][rows, pl.ds(col(m * stride + offset), LANE)] = block


PLAN_Q = [(0, 512, 0), (0, 512, 128), (0, 512, 256), (0, 512, 384), (1, None, 0)]
PLAN_U = [(0, 128, 0), (1, 512, 0), (1, 512, 128), (1, 512, 256), (1, 512, 384)]
PLAN_D = PLAN_U


def unpack(parts, order, plan, per, me, model, mp_size):
    widths = {}
    for which, stride, _ in plan:
        widths[which] = LANE if stride is None else stride * mp_size
    shapes = [sds((model, widths[w]), BF16) for w in sorted(widths)]
    return call(
        functools.partial(unpack_body, order, plan, per),
        "unpack",
        shapes,
        [me] + parts,
        smem=1,
    )


def norm_parts(x):
    mean = jnp.mean(x, axis=1, keepdims=True)
    centred = x - mean
    rstd = lax.rsqrt(jnp.mean(centred * centred, axis=1, keepdims=True) + NORM_EPS)
    return centred * rstd, rstd


def sigmoid(v):
    return 1.0 / (1.0 + jnp.exp(-v))


def first_body(mp_size, me_ref, x_ref, par_ref, wq_ref, n_ref, s1_ref, par_t_ref, *a_refs):
    me_m = me_ref[0]
    par_t = par_ref[...].astype(F32).T[:8]
    par_t_ref[...] = par_t
    xhat, _ = norm_parts(x_ref[...].astype(F32))
    n = (xhat * par_t[0:1] + par_t[2:3]).astype(BF16)
    n_ref[...] = n
    for mx in range(mp_size):
        m = jnp.bitwise_xor(me_m, mx)
        y = nn(n_ref[...], wq_ref[:, pl.ds(col(m * 512), 512)])
        a_refs[mx][...] = y[:, :384].astype(BF16)
        cols = pl.ds(col(m * LANE), LANE)
        s1_ref[:, cols] = sigmoid(y[:, 384:] + par_t_ref[3:4, cols])


def first(me, x, par, wq, mp_size):
    rows, model = x.shape
    out = [sds((rows, model), BF16), sds((rows, model), F32), sds((8, model), F32)]
    out += [sds((rows, 384), BF16)] * mp_size
    return call(
        functools.partial(first_body, mp_size),
        "first",
        out,
        [me, x, par, wq],
        smem=1,
        flops=2 * rows * wq.size,
    )


def seg_bounds(seg_ref, row, q_at, q_spans):
    first_id = seg_ref[row, q_at * SPAN]
    first_id = jnp.where(first_id < 0, 1 << 20, first_id)
    low = jnp.int32(0)
    for kb in range(q_spans - 1):
        last_id = seg_ref[row, (kb + 1) * SPAN - 1]
        last_id = jnp.where(last_id < 0, 1 << 20, last_id)
        low += jnp.where((kb < q_at) & (last_id < first_id), 1, 0)
    return low


def allowed_t(segc_ref, segr_ref, row, k0, q0, spans):
    keys = spans * SPAN
    seg_k = segc_ref[row, pl.ds(k0, keys), :]
    seg_q = segr_ref[row, :, pl.ds(q0, SPAN)]
    same = jnp.concatenate([seg_k == seg_q[:, :LANE], seg_k == seg_q[:, LANE:]], axis=1)
    tri = lax.broadcasted_iota(jnp.int32, (keys, SPAN), 0) - (keys - SPAN) <= (
        lax.broadcasted_iota(jnp.int32, (keys, SPAN), 1)
    )
    return same & tri


def attend_body(mp_size, me_ref, seg_ref, segc_ref, segr_ref, *refs):
    a_refs = refs[:mp_size]
    qkv_ref, lse_ref = refs[mp_size : mp_size + 2]
    o_refs = refs[mp_size + 2 : 2 * mp_size + 2]
    o_scr = refs[-1]
    rows = qkv_ref.shape[0]
    part = a_refs[0].shape[0] // rows
    me_m = me_ref[0]
    for mx in range(mp_size):
        at = pl.multiple_of(jnp.bitwise_xor(me_m, mx) * part, part)
        for r in range(rows):
            qkv_ref[r, pl.ds(at, part), :] = a_refs[mx][r * part : (r + 1) * part, :]
    q_spans = qkv_ref.shape[1] // SPAN

    def step(i, carry):
        r, q_at = i // q_spans, i % q_spans
        low = seg_bounds(seg_ref, r, q_at, q_spans)
        q0 = pl.multiple_of(q_at * SPAN, SPAN)
        k0 = pl.multiple_of(low * SPAN, SPAN)
        for spans in range(1, q_spans + 1):

            @pl.when(q_at - low + 1 == spans)
            def _():
                keys = spans * SPAN
                mask = allowed_t(segc_ref, segr_ref, r, k0, q0, spans)
                outs = []
                for h in range(2):
                    lo = h * HEAD_DIM
                    q = qkv_ref[r, pl.ds(q0, SPAN), lo : lo + HEAD_DIM] * jnp.asarray(
                        HEAD_DIM**-0.5, BF16
                    )
                    k = qkv_ref[r, pl.ds(k0, keys), 128 + lo : 128 + lo + HEAD_DIM]
                    v = qkv_ref[r, pl.ds(k0, keys), 256 + lo : 256 + lo + HEAD_DIM]
                    s = jnp.where(mask, nt(k, q), -1e30)
                    top = jnp.max(s, axis=0, keepdims=True)
                    p = jnp.exp(s - top)
                    total = jnp.sum(p, axis=0, keepdims=True)
                    lse_ref[r * 2 + h, :, pl.ds(q0, SPAN)] = top + jnp.log(total)
                    outs.append(tn(v, p.astype(BF16)) / total)
                o_scr[pl.ds(pl.multiple_of(i * SPAN, SPAN), SPAN), :] = (
                    jnp.concatenate(outs, axis=0).T.astype(BF16)
                )

        return carry

    lax.fori_loop(0, rows * q_spans, step, 0)
    length = qkv_ref.shape[1]
    for mx in range(mp_size):
        for r in range(rows):
            at = pl.multiple_of(r * length + jnp.bitwise_xor(me_m, mx) * part, part)
            o_refs[mx][r * part : (r + 1) * part, :] = o_scr[pl.ds(at, part), :]


def attend(me, seg, segc, segr, a_parts):
    mp_size = len(a_parts)
    rows, length = seg.shape
    local = a_parts[0].shape[0]
    out = [sds((rows, length, 384), BF16), sds((rows * 2, 1, length), F32)]
    out += [sds((local, LANE), BF16)] * mp_size
    return call(
        functools.partial(attend_body, mp_size),
        "attend",
        out,
        [me, seg, segc, segr] + a_parts,
        smem=2,
        scratch=[pltpu.VMEM((rows * length, LANE), BF16)],
        flops=rows * 2 * length * length * HEAD_DIM * 4,
    )


def second_body(
    mp_size, me_ref, x_ref, n_ref, s1_ref, par_ref, wo_ref, wg_ref, wu_ref, wd_ref, *refs
):
    t_refs = refs[:mp_size]
    att_ref, mid_ref, n2_ref, s2_ref, act_ref, slope_ref, out_ref = refs[mp_size:]
    me_m = me_ref[0]
    for mx in range(mp_size):
        m = jnp.bitwise_xor(me_m, mx)
        att_ref[:, pl.ds(col(m * LANE), LANE)] = t_refs[mx][...]
    mid = (
        x_ref[...].astype(F32)
        + nt(att_ref[...], wo_ref[...])
        + s1_ref[...] * n_ref[...].astype(F32)
    )
    mid_ref[...] = mid
    xhat, _ = norm_parts(mid)
    n2_ref[...] = (xhat * par_ref[1:2] + par_ref[4:5]).astype(BF16)
    s2_ref[...] = sigmoid(nn(n2_ref[...], wg_ref[...]) + par_ref[5:6])
    step_cols = 256

    def step(j, carry):
        cols = pl.ds(pl.multiple_of(j * step_cols, step_cols), step_cols)
        hidden = nn(n2_ref[...], wu_ref[:, cols])
        square = hidden * hidden
        th = jnp.tanh(0.7978845608 * hidden * (1.0 + 0.044715 * square))
        half = 0.5 * (1.0 + th)
        act_ref[:, cols] = (hidden * half).astype(BF16)
        inner = 0.7978845608 * (1.0 + 3 * 0.044715 * square)
        slope_ref[:, cols] = (half + 0.5 * hidden * (1.0 - th * th) * inner).astype(BF16)
        return carry

    lax.fori_loop(0, wu_ref.shape[1] // step_cols, step, 0)
    for j in range(2):
        half_cols = wo_ref.shape[0] // 2
        cols = slice(j * half_cols, (j + 1) * half_cols)
        out_ref[:, cols] = (
            mid_ref[:, cols]
            + s2_ref[:, cols] * n2_ref[:, cols].astype(F32)
            + nt(act_ref[...], wd_ref[cols, :])
        )


def second(me, x, n, s1, par_t, wo, wg, wu, wd, t_parts):
    rows, model = x.shape
    ff = wu.shape[1]
    out = [
        sds((rows, model), BF16),
        sds((rows, model), F32),
        sds((rows, model), BF16),
        sds((rows, model), F32),
        sds((rows, ff), BF16),
        sds((rows, ff), BF16),
        sds((rows, model), F32),
    ]
    return call(
        functools.partial(second_body, len(t_parts)),
        "second",
        out,
        [me, x, n, s1, par_t, wo, wg, wu, wd] + t_parts,
        smem=1,
        flops=2 * rows * (wo.size + wg.size + wu.size + wd.size),
    )


def norm_back(x, gain, d_normed):
    xhat, rstd = norm_parts(x)
    e = d_normed * gain
    mean_e = jnp.mean(e, axis=1, keepdims=True)
    mean_ex = jnp.mean(e * xhat, axis=1, keepdims=True)
    d_gain = jnp.sum(d_normed * xhat, axis=0, keepdims=True)
    d_bias = jnp.sum(d_normed, axis=0, keepdims=True)
    return (e - mean_e - xhat * mean_ex) * rstd, d_gain, d_bias


def second_back_body(
    mp_size,
    me_ref,
    g_ref,
    mid_ref,
    n2_ref,
    s2_ref,
    slope_ref,
    par_ref,
    wo_ref,
    wg_ref,
    wu_ref,
    wd_ref,
    b2_ref,
    dcomb_ref,
    gmid_ref,
    b1_ref,
    sums_ref,
    *d_refs,
):
    ff = wu_ref.shape[1]
    model = wo_ref.shape[0]
    ff_m = ff // mp_size
    stride = LANE + ff_m
    me_m = me_ref[0]
    b2_ref[...] = g_ref[...].astype(BF16)
    s2 = s2_ref[...]
    b2f = b2_ref[...].astype(F32)
    d_z2 = (b2f * n2_ref[...].astype(F32) * s2 * (1.0 - s2)).astype(BF16)
    d_n2 = b2f * s2 + nt(d_z2, wg_ref[...])
    sums_ref[2:3, :] = jnp.sum(d_z2.astype(F32), axis=0, keepdims=True)
    gmid_ref[...] = d_n2
    for m in range(mp_size):
        dcomb_ref[:, m * stride : m * stride + LANE] = d_z2[:, m * LANE : (m + 1) * LANE]
        cols = slice(m * ff_m, (m + 1) * ff_m)
        d_hidden = (nn(b2_ref[...], wd_ref[:, cols]) * slope_ref[:, cols].astype(F32)).astype(BF16)
        dcomb_ref[:, m * stride + LANE : (m + 1) * stride] = d_hidden
        gmid_ref[...] += nt(d_hidden, wu_ref[:, cols])
    d_mid, d_gain, d_bias = norm_back(mid_ref[...], par_ref[1:2], gmid_ref[...])
    sums_ref[0:1, :] = d_gain
    sums_ref[1:2, :] = d_bias
    sums_ref[3:8, :] = jnp.zeros((5, model), F32)
    g_mid = g_ref[...] + d_mid
    gmid_ref[...] = g_mid
    b1_ref[...] = g_mid.astype(BF16)
    for mx in range(mp_size):
        m = jnp.bitwise_xor(me_m, mx)
        d_refs[mx][...] = nn(b1_ref[...], wo_ref[:, pl.ds(col(m * LANE), LANE)]).astype(BF16)


def second_back(me, g, mid, n2, s2, slope, par_t, wo, wg, wu, wd, mp_size):
    rows, model = g.shape
    ff = wu.shape[1]
    out = [
        sds((rows, model), BF16),
        sds((rows, ff + LANE * mp_size), BF16),
        sds((rows, model), F32),
        sds((rows, model), BF16),
        sds((8, model), F32),
    ]
    out += [sds((rows, LANE), BF16)] * mp_size
    return call(
        functools.partial(second_back_body, mp_size),
        "second_back",
        out,
        [me, g, mid, n2, s2, slope, par_t, wo, wg, wu, wd],
        smem=1,
        flops=2 * rows * (wo.size + wg.size + wu.size + wd.size),
    )


def attend_back_body(mp_size, me_ref, seg_ref, segc_ref, segr_ref, qkv_ref, lse_ref, *refs):
    d_in = refs[:mp_size]
    d_out = refs[mp_size : 2 * mp_size]
    do_scr, dq_scr, dk_scr, dv_scr = refs[2 * mp_size :]
    rows, length = qkv_ref.shape[0], qkv_ref.shape[1]
    part = d_in[0].shape[0] // rows
    me_m = me_ref[0]
    for mx in range(mp_size):
        for r in range(rows):
            at = pl.multiple_of(r * length + jnp.bitwise_xor(me_m, mx) * part, part)
            do_scr[pl.ds(at, part), :] = d_in[mx][r * part : (r + 1) * part, :]
    dq_scr[...] = jnp.zeros_like(dq_scr)
    dk_scr[...] = jnp.zeros_like(dk_scr)
    dv_scr[...] = jnp.zeros_like(dv_scr)
    q_spans = length // SPAN

    def step(i, carry):
        r, q_at = i // q_spans, i % q_spans
        low = seg_bounds(seg_ref, r, q_at, q_spans)
        real = seg_ref[r, q_at * SPAN] >= 0
        q0 = pl.multiple_of(q_at * SPAN, SPAN)
        k0 = pl.multiple_of(low * SPAN, SPAN)
        q_abs = pl.multiple_of(i * SPAN, SPAN)
        k_abs = pl.multiple_of(r * length + low * SPAN, SPAN)
        for spans in range(1, q_spans + 1):

            @pl.when(real & (q_at - low + 1 == spans))
            def _():
                keys = spans * SPAN
                mask = allowed_t(segc_ref, segr_ref, r, k0, q0, spans)
                dqs, dks, dvs = [], [], []
                for h in range(2):
                    lo = h * HEAD_DIM
                    q = qkv_ref[r, pl.ds(q0, SPAN), lo : lo + HEAD_DIM] * jnp.asarray(
                        HEAD_DIM**-0.5, BF16
                    )
                    k = qkv_ref[r, pl.ds(k0, keys), 128 + lo : 128 + lo + HEAD_DIM]
                    v = qkv_ref[r, pl.ds(k0, keys), 256 + lo : 256 + lo + HEAD_DIM]
                    do = do_scr[pl.ds(q_abs, SPAN), lo : lo + HEAD_DIM]
                    lse = lse_ref[r * 2 + h, :, pl.ds(q0, SPAN)]
                    p = jnp.where(mask, jnp.exp(nt(k, q) - lse), 0.0)
                    dvs.append(nn(p.astype(BF16), do))
                    dp = nt(v, do)
                    delta = jnp.sum(p * dp, axis=0, keepdims=True)
                    ds = (p * (dp - delta)).astype(BF16)
                    dks.append(nn(ds, q))
                    dqs.append(tn(k, ds))
                dq_scr[pl.ds(q_abs, SPAN), :] = (
                    jnp.concatenate(dqs, axis=0).T * HEAD_DIM**-0.5
                ).astype(BF16)
                dk_scr[pl.ds(k_abs, keys), :] += jnp.concatenate(dks, axis=1)
                dv_scr[pl.ds(k_abs, keys), :] += jnp.concatenate(dvs, axis=1)

        return carry

    lax.fori_loop(0, rows * q_spans, step, 0)
    for mx in range(mp_size):
        for r in range(rows):
            at = pl.multiple_of(r * length + jnp.bitwise_xor(me_m, mx) * part, part)
            here = slice(r * part, (r + 1) * part)
            d_out[mx][here, 0:128] = dq_scr[pl.ds(at, part), :]
            d_out[mx][here, 128:256] = dk_scr[pl.ds(at, part), :].astype(BF16)
            d_out[mx][here, 256:384] = dv_scr[pl.ds(at, part), :].astype(BF16)


def attend_back(me, seg, segc, segr, qkv, lse, d_parts):
    mp_size = len(d_parts)
    rows, length = seg.shape
    local = d_parts[0].shape[0]
    return call(
        functools.partial(attend_back_body, mp_size),
        "attend_back",
        [sds((local, 384), BF16)] * mp_size,
        [me, seg, segc, segr, qkv, lse] + d_parts,
        smem=2,
        scratch=[
            pltpu.VMEM((rows * length, LANE), BF16),
            pltpu.VMEM((rows * length, LANE), BF16),
            pltpu.VMEM((rows * length, LANE), F32),
            pltpu.VMEM((rows * length, LANE), F32),
        ],
        flops=rows * 2 * length * length * HEAD_DIM * 10,
    )


def first_back_body(
    mp_size, me_ref, x_ref, gmid_ref, n_ref, s1_ref, par_ref, sums2_ref, wq_ref, *refs
):
    d_refs = refs[:mp_size]
    dcomb_ref, g_ref, sums_ref = refs[mp_size:]
    me_m = me_ref[0]
    gmid = gmid_ref[...]
    b1f = gmid.astype(BF16).astype(F32)
    s1 = s1_ref[...]
    d_z1 = (b1f * n_ref[...].astype(F32) * s1 * (1.0 - s1)).astype(BF16)
    for m in range(mp_size):
        dcomb_ref[:, m * 512 + 384 : (m + 1) * 512] = d_z1[:, m * LANE : (m + 1) * LANE]
    for mx in range(mp_size):
        m = jnp.bitwise_xor(me_m, mx)
        dcomb_ref[:, pl.ds(col(m * 512), 384)] = d_refs[mx][...]
    d_n = b1f * s1 + nt(dcomb_ref[...], wq_ref[...])
    d_x, d_gain, d_bias = norm_back(x_ref[...].astype(F32), par_ref[0:1], d_n)
    g_ref[...] = gmid + d_x
    sums_ref[0:1, :] = d_gain
    sums_ref[1:2, :] = sums2_ref[0:1, :]
    sums_ref[2:3, :] = d_bias
    sums_ref[3:4, :] = jnp.sum(d_z1.astype(F32), axis=0, keepdims=True)
    sums_ref[4:5, :] = sums2_ref[1:2, :]
    sums_ref[5:6, :] = sums2_ref[2:3, :]
    sums_ref[6:8, :] = sums2_ref[6:8, :]


def first_back(me, x, gmid, n, s1, par_t, sums2, wq, d_parts):
    rows, model = x.shape
    out = [sds((rows, wq.shape[1]), BF16), sds((rows, model), F32), sds((8, model), F32)]
    return call(
        functools.partial(first_back_body, len(d_parts)),
        "first_back",
        out,
        [me, x, gmid, n, s1, par_t, sums2, wq] + d_parts,
        smem=1,
        flops=2 * rows * wq.size,
    )


def pack_grad_body(mp_size, chunks, left_of, columns, has_sums, me_ref, *refs):
    lefts = sorted(set(left_of))
    ins, refs = refs[: len(lefts)], refs[len(lefts) :]
    rights = refs[: len(columns)]
    refs = refs[len(columns) :]
    if has_sums:
        sums_ref, refs = refs[0], refs[1:]
    outs, scr = refs[:2], refs[2:]
    model = ins[0].shape[1]
    per = model // chunks
    me_m, me_d = me_ref[0], me_ref[1]
    half = mp_size // 2
    turn = scr[0]

    def ordered(values, dst):
        if chunks == 1:
            dst[...] = values
            return
        turn[:, : values.shape[1]] = values.astype(F32)
        for dx in range(chunks):
            at = pl.multiple_of(jnp.bitwise_xor(me_d, dx) * per, per)
            dst[dx * per : (dx + 1) * per, :] = turn[pl.ds(at, per), : values.shape[1]].astype(
                dst.dtype
            )

    for i, left in enumerate(ins):
        ordered(left[...].T, scr[1 + i])
    for mx in range(mp_size):
        m = jnp.bitwise_xor(me_m, mx)
        out = outs[mx % 2]
        at_block = 0
        for left, right, (stride, offset, width) in zip(left_of, rights, columns):
            res = nn(
                scr[1 + lefts.index(left)][...],
                right[:, pl.ds(col(m * stride + offset), width)],
            ).astype(BF16)
            for b in range(width // LANE):
                for dx in range(chunks):
                    out[mx // 2, dx, (at_block + b) * per : (at_block + b + 1) * per, :] = res[
                        dx * per : (dx + 1) * per, b * LANE : (b + 1) * LANE
                    ]
            at_block += width // LANE
    if has_sums:
        flat = jnp.concatenate([sums_ref[...], jnp.zeros((LANE - 8, model), F32)], axis=0).T
        last = scr[-1]
        ordered(flat, last)
        for mx in range(mp_size):
            for dx in range(chunks):
                outs[mx % 2][mx // 2, dx, at_block * per : (at_block + 1) * per, :] = last[
                    dx * per : (dx + 1) * per, :
                ].astype(BF16)


def pack_grad(me, mp_size, chunks, lefts, left_of, rights, columns, sums=None):
    rows, model = lefts[0].shape
    per = model // chunks
    blocks = sum(c[2] for c in columns) // LANE + (sums is not None)
    scratch = [pltpu.VMEM((model, model), F32)]
    scratch += [pltpu.VMEM((model, rows), BF16)] * len(lefts)
    if sums is not None:
        scratch.append(pltpu.VMEM((model, LANE), F32))
    return call(
        functools.partial(
            pack_grad_body, mp_size, chunks, left_of, columns, sums is not None
        ),
        "pack_grad",
        [sds((mp_size // 2, chunks, blocks * per, LANE), BF16)] * 2,
        [me] + lefts + rights + ([sums] if sums is not None else []),
        smem=1,
        scratch=scratch,
        flops=2 * rows * model * sum(c[2] for c in columns) * mp_size,
    )


def swap(value, axis, size, bits):
    return lax.ppermute(value, axis, [(i, i ^ bits) for i in range(size)])


def solution(mesh):
    dp_size, mp_size, width_size = (mesh.shape[a] for a in ("dp", "mp", "width"))
    all_axes = ("mp", "dp", "width")
    direct = (dp_size, mp_size, width_size) == (2, 4, 4)

    def exchange(parts):
        far3 = swap(parts[3], "mp", mp_size, 2)
        far2 = swap(parts[2], "mp", mp_size, 2)
        near = swap(parts[1], "mp", mp_size, 1)
        third = swap(far3, "mp", mp_size, 1)
        return [parts[0], near, far2, third]

    def gather_direct(shard, turn):
        steps = [shard] + [swap(shard, "width", width_size, k) for k in range(1, width_size)]
        base = jnp.stack(steps)
        got = {(0, 0): base}
        if turn:
            got[2, 0] = swap(base, "mp", mp_size, 2)
            got[0, 1] = swap(base, "dp", dp_size, 1)
            got[2, 1] = swap(got[2, 0], "dp", dp_size, 1)
        else:
            got[0, 1] = swap(base, "dp", dp_size, 1)
            got[2, 0] = swap(base, "mp", mp_size, 2)
            got[2, 1] = swap(got[0, 1], "mp", mp_size, 2)
        for m, d in list(got):
            got[m + 1, d] = swap(got[m, d], "mp", mp_size, 1)
        parts = [got[key] for key in got]
        order = [[(m, d * width_size + w) for w in range(width_size)] for m, d in got]
        return parts, order

    def scatter_direct(even, odd, turn):
        add = lambda a, b: (a.astype(F32) + b.astype(F32)).astype(BF16)
        got = swap(odd, "mp", mp_size, 1)
        shape = (2, dp_size, width_size) + even.shape[2:]
        even, got = even.reshape(shape), got.reshape(shape)
        if turn:
            even, got = jnp.swapaxes(even, 0, 1), jnp.swapaxes(got, 0, 1)
        axes = (("mp", mp_size, 2), ("dp", dp_size, 1))
        if turn:
            axes = axes[::-1]
        send = add(even[1], got[1])
        keep = add(even[0], got[0])
        got = swap(send, *axes[0])
        send = add(keep[1], got[1])
        keep = add(keep[0], got[0])
        got = swap(send, *axes[1])
        sums = [add(keep[k], got[k]) for k in range(width_size)]
        total = sums[0].astype(F32)
        for k in range(1, width_size):
            total = total + swap(sums[k], "width", width_size, k).astype(F32)
        return total

    def on_device(
        tokens, segments, cotangent, norm_gains, biases, w_qkv, w_out, w_gate, w_up, w_down
    ):
        batch, part, model = tokens.shape
        layers = w_qkv.shape[0]
        per = w_qkv.shape[1]
        chunks = model // per
        heads_cols = w_out.shape[1]
        ff_m = w_up.shape[2]
        ff_blocks = ff_m // LANE
        me_m = lax.axis_index("mp")
        me_d = lax.axis_index("dp") * width_size + lax.axis_index("width")
        me = jnp.stack([me_m, me_d]).astype(jnp.int32)
        if not direct:
            me_pack = jnp.zeros((2,), jnp.int32)
        else:
            me_pack = me

        def blocks_of(matrix):
            return jnp.swapaxes(matrix.reshape(per, -1, LANE), 0, 1).reshape(-1, LANE)

        def shards_of(l):
            params = jnp.concatenate([norm_gains[l], biases[l]], axis=0).T
            params = jnp.pad(params, ((0, 0), (0, LANE - params.shape[1])))
            return (
                jnp.concatenate(
                    [blocks_of(w_qkv[l].reshape(per, -1)), w_gate[l, 0], params], axis=0
                ),
                jnp.concatenate([w_gate[l, 1], blocks_of(w_up[l])], axis=0),
                jnp.concatenate([w_out[l].T, blocks_of(w_down[l].T)], axis=0),
            )

        def whole_weights(shard, plan, turn, offload):
            if direct and not offload:
                parts, order = gather_direct(shard, turn)
                return unpack(parts, order, plan, per, me, model, mp_size)
            full = lax.all_gather(shard, all_axes, axis=0, tiled=True)
            if direct:
                count = mp_size * chunks
                order = [[(i // chunks, i % chunks) for i in range(count)]]
                parts = [full.reshape(count, -1, LANE)]
                zero = jnp.zeros((2,), jnp.int32)
                return unpack(parts, order, plan, per, zero, model, mp_size)
            full = full.reshape(mp_size, chunks, len(plan), per, LANE)
            outs = {}
            for b, (which, stride, _) in enumerate(plan):
                outs.setdefault(which, []).append(b)
            result = []
            for which in sorted(outs):
                b = outs[which]
                if plan[b[0]][1] is None:
                    result.append(full[0, :, b[0]].reshape(model, LANE))
                else:
                    result.append(
                        jnp.transpose(full[:, :, b[0] : b[-1] + 1], (1, 3, 0, 2, 4)).reshape(
                            model, -1
                        )
                    )
            return result

        def reduce_piece(pair, turn):
            if direct:
                return scatter_direct(pair[0], pair[1], turn)
            full = jnp.stack(pair, axis=1)
            full = full.reshape(mp_size, -1, chunks, per, LANE)
            full = jnp.swapaxes(full, 1, 2).reshape(-1, LANE)
            return lax.psum_scatter(
                full.astype(F32), all_axes, scatter_dimension=0, tiled=True
            )

        pack_chunks = chunks if direct else 1
        segc = jnp.broadcast_to(segments[:, :, None], segments.shape + (LANE,))
        segr = segments[:, None, :]

        weights = []
        for l in range(layers):
            q_sh, u_sh, d_sh = shards_of(l)
            weights.append(
                (
                    whole_weights(q_sh, PLAN_Q, 0, False),
                    whole_weights(d_sh, PLAN_D, 1, False),
                    whole_weights(u_sh, PLAN_U, 0, False),
                )
            )

        x = tokens.reshape(batch * part, model)
        saved = []
        for l in range(layers):
            (wq, par), (wo, wd), (wg, wu) = weights[l]
            n, s1, par_t, *a_parts = first(me, x, par, wq, mp_size)
            a_parts = exchange(a_parts)
            qkv, lse, *o_parts = attend(me, segments, segc, segr, a_parts)
            o_parts = exchange(o_parts)
            att, mid, n2, s2, act, slope, out = second(
                me, x, n, s1, par_t, wo, wg, wu, wd, o_parts
            )
            saved.append((x, n, s1, par_t, qkv, lse, att, mid, n2, s2, act, slope))
            x = out
        output = x.reshape(batch, part, model)

        own = lax.dynamic_slice_in_dim(segments, me_m * part, part, 1)
        g = cotangent.astype(F32) * (own >= 0).astype(F32)[:, :, None]
        g = g.reshape(batch * part, model)
        reduced = [None] * layers
        for l in reversed(range(layers)):
            (wq, par), (wo, wd), (wg, wu) = weights[l]
            x, n, s1, par_t, qkv, lse, att, mid, n2, s2, act, slope = saved[l]
            b2, dcomb, gmid, b1, sums2, *d_parts = second_back(
                me, g, mid, n2, s2, slope, par_t, wo, wg, wu, wd, mp_size
            )
            d_parts = exchange(d_parts)
            stride = LANE + ff_m
            up_grad = pack_grad(
                me_pack, mp_size, pack_chunks, [n2], [0], [dcomb], [(stride, 0, stride)]
            )
            up_sum = reduce_piece(up_grad, 0)
            down_grad = pack_grad(
                me_pack,
                mp_size,
                pack_chunks,
                [b1, b2],
                [0, 1],
                [att, act],
                [(heads_cols, 0, heads_cols), (ff_m, 0, ff_m)],
            )
            down_sum = reduce_piece(down_grad, 1)
            d_parts = attend_back(me, segments, segc, segr, qkv, lse, d_parts)
            d_parts = exchange(d_parts)
            dcomb, g, sums = first_back(me, x, gmid, n, s1, par_t, sums2, wq, d_parts)
            q_grad = pack_grad(
                me_pack, mp_size, pack_chunks, [n], [0], [dcomb], [(512, 0, 512)], sums
            )
            q_sum = reduce_piece(q_grad, 0)
            reduced[l] = (q_sum, up_sum, down_sum)
        d_tokens = g.reshape(batch, part, model)

        def unblocks(rows, count):
            return jnp.swapaxes(rows.reshape(count, per, LANE), 0, 1).reshape(per, count * LANE)

        grads = []
        for q_sum, up_sum, down_sum in reduced:
            params = q_sum[4 * per :, :6].T
            grads.append(
                (
                    params[0:2],
                    params[2::2],
                    params[3::2],
                    unblocks(q_sum[: 3 * per], 3).reshape(per, 3, LANE),
                    down_sum[:per].T,
                    jnp.stack([q_sum[3 * per : 4 * per], up_sum[:per]]),
                    unblocks(up_sum[per:], ff_blocks),
                    unblocks(down_sum[per:], ff_blocks).T,
                )
            )
        stacked = [jnp.stack([grads[l][i] for l in range(layers)]) for i in range(8)]
        return (output, d_tokens, *stacked)

    placed = (
        P(("dp", "width"), "mp", None),
        P(("dp", "width"), None),
        P(("dp", "width"), "mp", None),
        P(None, None, ("dp", "width")),
        P(None, None, ("dp", "width")),
        P(None, ("dp", "width"), None, "mp"),
        P(None, "mp", ("dp", "width")),
        P(None, None, ("dp", "width"), "mp"),
        P(None, ("dp", "width"), "mp"),
        P(None, "mp", ("dp", "width")),
    )
    return jax.shard_map(
        on_device,
        mesh=mesh,
        in_specs=placed,
        out_specs=(
            placed[0],
            placed[0],
            placed[3],
            placed[3],
            placed[3],
            placed[5],
            placed[6],
            placed[7],
            placed[8],
            placed[9],
        ),
        check_vma=False,
    )
```

```python
import functools

import jax
import jax.numpy as jnp
from jax import lax
from jax.experimental import pallas as pl
from jax.experimental.pallas import tpu as pltpu
from jax.sharding import PartitionSpec as P

HEAD_DIM = 64
LANE = 128
NORM_EPS = 1e-05
SPAN = 256
CHUNK = 64

VMEM_MB = {
    "attend": 12,
    "second": 28,
    "second_back": 28,
    "attend_back": 16,
    "first_back": 10,
    "weight_grad": 24,
    "stack": 8,
    "pack": 4,
    "add": 6,
}

KERNEL_US = {
    "attend": 8,
    "second": 12,
    "second_back": 10,
    "attend_back": 9,
    "first_back": 4,
    "weight_grad": 8,
    "stack": 1,
    "add": 1,
    "pack": 1,
}

F32 = jnp.float32
BF16 = jnp.bfloat16


def nn(a, b):
    return jnp.dot(a, b, preferred_element_type=F32)


def nt(a, b):
    return lax.dot_general(a, b, (((1,), (1,)), ((), ())), preferred_element_type=F32)


def tn(a, b):
    return lax.dot_general(a, b, (((0,), (0,)), ((), ())), preferred_element_type=F32)


def sds(shape, dtype):
    return jax.ShapeDtypeStruct(shape, dtype)


class Chain:
    def __init__(self):
        self.token = None


ORDER = Chain()


def call(body, name, out_shape, args, smem=0, parts=(), scratch=(), flops=0, after=()):
    after = list(after) + ([] if ORDER.token is None else [ORDER.token])
    specs = [pl.BlockSpec(memory_space=pltpu.SMEM)] * smem
    specs += [pl.BlockSpec(memory_space=pltpu.VMEM)] * (len(args) - smem)
    specs += [pl.BlockSpec(memory_space=pltpu.HBM)] * len(parts)
    specs += [pl.BlockSpec(memory_space=pl.ANY)] * len(after)
    used = len(args) + len(parts)
    given = used + len(after)
    outs = len(out_shape)

    def inner(*refs):
        body(*refs[:used], *refs[given : given + outs], *refs[given + outs + 1 :])

    nbytes = sum(a.size * a.dtype.itemsize for a in list(args) + list(parts))
    nbytes += sum(o.size * o.dtype.itemsize for o in out_shape)
    *result, ORDER.token = pl.pallas_call(
        inner,
        name=name,
        out_shape=list(out_shape) + [sds((8, LANE), F32)],
        in_specs=specs,
        out_specs=[pl.BlockSpec(memory_space=pltpu.VMEM)] * outs
        + [pl.BlockSpec(memory_space=pl.ANY)],
        scratch_shapes=list(scratch),
        cost_estimate=pl.CostEstimate(
            flops=int(1 * KERNEL_US[name] * 1.1e9),
            bytes_accessed=int(1 * KERNEL_US[name] * 3.6e6),
            transcendentals=0,
        ),
        compiler_params=pltpu.CompilerParams(vmem_limit_bytes=VMEM_MB[name] * 2**20),
    )(*args, *parts, *after)
    return result


def col(start):
    return pl.multiple_of(start, LANE)


class Parts:
    def __init__(self, arrays, order, first_row, rows):
        self.arrays = arrays
        self.order = order
        self.first_row = first_row
        self.rows = rows

    def copies(self, refs, me_ref, dst, sem, chunks, own_only):
        me_m, me_d = me_ref[0], me_ref[1]
        rows = pl.ds(self.first_row, self.rows)
        if self.order is None:
            src = refs[0].at[:, rows, :]
            if own_only:
                src = refs[0].at[pl.ds(me_m * chunks, chunks), rows, :]
            yield pltpu.make_async_copy(src, dst, sem)
            return
        for ref, (mx, dx) in zip(refs, self.order):
            m = jnp.bitwise_xor(me_m, mx)
            for w in range(ref.shape[0]):
                at = jnp.bitwise_xor(me_d, dx + w)
                if not own_only:
                    at = m * chunks + at
                yield pltpu.make_async_copy(ref.at[w, rows, :], dst.at[at], sem)

    def start(self, refs, me_ref, dst, sem, chunks, own_only=False):
        for copy in self.copies(refs, me_ref, dst, sem, chunks, own_only):
            copy.start()

    def wait(self, dst, sem):
        pltpu.make_async_copy(dst, dst, sem).wait()


def blocks(dst, m, b, chunks, lo=0, hi=None):
    hi = chunks if hi is None else hi
    rows = pl.ds(b * CHUNK, CHUNK)
    return jnp.concatenate([dst[m * chunks + d, rows, :] for d in range(lo, hi)], axis=0)


def wide(dst, which, chunks, lo=0, hi=None):
    return jnp.concatenate([blocks(dst, m, b, chunks, lo, hi) for m, b in which], axis=1)


def param_rows(dst, first_row, layer, chunks):
    rows = slice(first_row + 8 * layer, first_row + 8 * layer + 8)
    share = LANE // CHUNK
    tiles = []
    for i in range(chunks // share):
        tile = dst[i * share, rows, :].astype(F32)
        for j in range(1, share):
            tile += dst[i * share + j, rows, :].astype(F32)
        tiles.append(tile)
    return jnp.concatenate(tiles, axis=1)


def norm_parts(x):
    mean = jnp.mean(x, axis=1, keepdims=True)
    centred = x - mean
    rstd = lax.rsqrt(jnp.mean(centred * centred, axis=1, keepdims=True) + NORM_EPS)
    return centred * rstd, rstd


def sigmoid(v):
    return 1.0 / (1.0 + jnp.exp(-v))


def seg_bounds(seg_ref, q_at, q_spans):
    first_id = seg_ref[q_at * SPAN]
    first_id = jnp.where(first_id < 0, 1 << 20, first_id)
    low = jnp.int32(0)
    for kb in range(q_spans - 1):
        last_id = seg_ref[(kb + 1) * SPAN - 1]
        last_id = jnp.where(last_id < 0, 1 << 20, last_id)
        low += jnp.where((kb < q_at) & (last_id < first_id), 1, 0)
    return low


def allowed_t(segc_ref, segr_ref, k0, q0, spans):
    keys = spans * SPAN
    seg_k = segc_ref[pl.ds(k0, keys), :]
    seg_q = segr_ref[:, pl.ds(q0, SPAN)]
    same = jnp.concatenate([seg_k == seg_q[:, :LANE], seg_k == seg_q[:, LANE:]], axis=1)
    tri = lax.broadcasted_iota(jnp.int32, (SPAN, SPAN), 0) <= (
        lax.broadcasted_iota(jnp.int32, (SPAN, SPAN), 1)
    )
    if spans == 1:
        return same & tri
    return jnp.concatenate([same[: keys - SPAN], same[keys - SPAN :] & tri], axis=0)


def attend_body(
    wq, layer, row, norm_here, mp_size, chunks, me_ref, seg_ref, segc_ref, segr_ref, *refs
):
    t_refs, refs = refs[:mp_size], refs[mp_size:]
    if norm_here:
        t_refs = [ref.at[row] for ref in t_refs]
    w_refs, refs = refs[: len(wq.arrays)], refs[len(wq.arrays) :]
    qkv_ref, lse_ref = refs[:2]
    o_refs, refs = [refs[2], refs[3], refs[4].at[0], refs[4].at[1]], refs[5:]
    if norm_here:
        par_ref, n_refs, refs = refs[0], refs[1 : 1 + mp_size], refs[1 + mp_size :]
    w_scr, o_scr, sem = refs
    part = t_refs[0].shape[0]
    me_m = me_ref[0]
    wq.start(w_refs, me_ref, w_scr, sem, chunks, own_only=True)
    wq.wait(w_scr, sem)
    if norm_here:
        for l in range(par_ref.shape[0]):
            par_ref[l] = param_rows(w_scr, 3 * CHUNK, l, chunks)
    weights = wide(w_scr, [(0, 0), (0, 1), (0, 2)], chunks)
    for mx in range(mp_size):
        at = pl.ds(pl.multiple_of(jnp.bitwise_xor(me_m, mx) * part, part), part)
        if norm_here:
            xhat, _ = norm_parts(t_refs[mx][...].astype(F32))
            n = (xhat * par_ref[layer, 0:1] + par_ref[layer, 2:3]).astype(BF16)
            n_refs[mx][...] = n
        else:
            n = t_refs[mx][...]
        qkv_ref[at, :] = nn(n, weights).astype(BF16)
    q_spans = qkv_ref.shape[0] // SPAN

    def step(q_at, carry):
        low = seg_bounds(seg_ref, q_at, q_spans)
        q0 = pl.multiple_of(q_at * SPAN, SPAN)
        k0 = pl.multiple_of(low * SPAN, SPAN)
        for spans in range(1, q_spans + 1):

            @pl.when(q_at - low + 1 == spans)
            def _():
                keys = spans * SPAN
                mask = allowed_t(segc_ref, segr_ref, k0, q0, spans)
                outs = []
                for h in range(2):
                    lo = h * HEAD_DIM
                    q = qkv_ref[pl.ds(q0, SPAN), lo : lo + HEAD_DIM] * jnp.asarray(
                        HEAD_DIM**-0.5, BF16
                    )
                    k = qkv_ref[pl.ds(k0, keys), 128 + lo : 128 + lo + HEAD_DIM]
                    v = qkv_ref[pl.ds(k0, keys), 256 + lo : 256 + lo + HEAD_DIM]
                    s = jnp.where(mask, nt(k, q), -1e30)
                    top = jnp.max(s, axis=0, keepdims=True)
                    p = jnp.exp(s - top)
                    total = jnp.sum(p, axis=0, keepdims=True)
                    lse_ref[h, :, pl.ds(q0, SPAN)] = top + jnp.log(total)
                    outs.append(tn(v, p.astype(BF16)) / total)
                o_scr[pl.ds(q0, SPAN), :] = jnp.concatenate(outs, axis=0).T.astype(BF16)

        return carry

    lax.fori_loop(0, q_spans, step, 0)
    for mx in range(mp_size):
        at = pl.multiple_of(jnp.bitwise_xor(me_m, mx) * part, part)
        o_refs[mx][...] = o_scr[pl.ds(at, part), :]


def attend(me, seg, segc, segr, t_parts, wq, layer, row, layers, norm_here, chunks, after=()):
    mp_size = len(t_parts)
    length = seg.shape[0]
    part, model = t_parts[0].shape[-2:]
    out = [sds((length, 384), BF16), sds((2, 1, length), F32)]
    out += [sds((part, LANE), BF16)] * 2 + [sds((2, part, LANE), BF16)]
    if norm_here:
        out += [sds((layers, 8, model), F32)] + [sds((part, model), BF16)] * mp_size
    return call(
        functools.partial(attend_body, wq, layer, row, norm_here, mp_size, chunks),
        "attend",
        out,
        [me, seg, segc, segr] + t_parts,
        smem=2,
        parts=wq.arrays,
        scratch=[
            pltpu.VMEM((chunks, wq.rows, LANE), BF16),
            pltpu.VMEM((length, LANE), BF16),
            pltpu.SemaphoreType.DMA,
        ],
        flops=2 * length * length * HEAD_DIM * 4 + 2 * length * model * 384,
        after=after,
    )


def second_body(
    wd, wu, layer, mp_size, chunks, batch, has_next, me_ref, x_ref, par_ref, *refs
):
    n_refs, refs = refs[:batch], refs[batch:]
    t_refs, refs = refs[: mp_size * batch], refs[mp_size * batch :]
    for r in range(batch):
        at = r * mp_size
        t_refs = (*t_refs[: at + 2], t_refs[at + 2].at[0], t_refs[at + 3].at[1], *t_refs[at + 4 :])
    d_refs, refs = refs[: len(wd.arrays)], refs[len(wd.arrays) :]
    u_refs = d_refs
    att_ref, s1_ref, mid_ref, n2_ref, s2_ref, act_ref, slope_ref, out_ref = refs[:8]
    refs = refs[8:]
    if has_next:
        next_refs, refs = refs[:batch], refs[batch:]
    d_scr, u_scr, d_sem, u_sem = refs
    wd.start(d_refs, me_ref, d_scr, d_sem, chunks)
    wu.start(u_refs, me_ref, u_scr, u_sem, chunks)
    me_m = me_ref[0]
    part = n_refs[0].shape[0]
    par = par_ref.at[layer]
    for r in range(batch):
        for mx in range(mp_size):
            m = jnp.bitwise_xor(me_m, mx)
            att_ref[r * part : (r + 1) * part, pl.ds(col(m * LANE), LANE)] = t_refs[
                r * mp_size + mx
            ][...]
    n = jnp.concatenate([ref[...] for ref in n_refs], axis=0)
    every = range(mp_size)
    wd.wait(d_scr, d_sem)
    s1 = sigmoid(nn(n, wide(d_scr, [(m, 0) for m in every], chunks)) + par[3:4])
    s1_ref[...] = s1
    mid = (
        x_ref[...].astype(F32)
        + nt(att_ref[...], wide(d_scr, [(m, 1) for m in every], chunks))
        + s1 * n.astype(F32)
    )
    mid_ref[...] = mid
    xhat, _ = norm_parts(mid)
    n2_ref[...] = (xhat * par[1:2] + par[4:5]).astype(BF16)
    wu.wait(u_scr, u_sem)
    s2_ref[...] = sigmoid(
        nn(n2_ref[...], wide(u_scr, [(m, 0) for m in every], chunks)) + par[5:6]
    )
    ff_blocks = act_ref.shape[1] // (mp_size * LANE)
    for m in every:
        for b in range(0, ff_blocks, 2):
            at = (m * ff_blocks + b) * LANE
            cols = slice(at, at + 2 * LANE)
            hidden = nn(n2_ref[...], wide(u_scr, [(m, 1 + b), (m, 2 + b)], chunks))
            square = hidden * hidden
            inner = 0.7978845608 + (0.7978845608 * 0.044715) * square
            th = jnp.tanh(hidden * inner)
            half = 0.5 + 0.5 * th
            act = hidden * half
            act_ref[:, cols] = act.astype(BF16)
            slope = half + act * (1.0 - th) * (3.0 * inner - 2 * 0.7978845608)
            slope_ref[:, cols] = slope.astype(BF16)
    share = chunks // 2
    for j in range(2):
        cols = slice(j * share * CHUNK, (j + 1) * share * CHUNK)
        down = [(m, 2 + b) for m in every for b in range(ff_blocks)]
        out_ref[:, cols] = (
            mid_ref[:, cols]
            + s2_ref[:, cols] * n2_ref[:, cols].astype(F32)
            + nt(act_ref[...], wide(d_scr, down, chunks, j * share, (j + 1) * share))
        )
    if has_next:
        xhat, _ = norm_parts(out_ref[...])
        after = (xhat * par_ref[layer + 1, 0:1] + par_ref[layer + 1, 2:3]).astype(BF16)
        for r in range(batch):
            next_refs[r][...] = after[r * part : (r + 1) * part]


def second(me, x, par, n_rows, t_parts, wd, wu, layer, chunks, ff, has_next, after=()):
    rows, model = x.shape
    mp_size = len(t_parts) // len(n_rows)
    out = [
        sds((rows, model), BF16),
        sds((rows, model), F32),
        sds((rows, model), F32),
        sds((rows, model), BF16),
        sds((rows, model), F32),
        sds((rows, ff), BF16),
        sds((rows, ff), BF16),
        sds((rows, model), F32),
    ]
    if has_next:
        out += [sds(n_rows[0].shape, BF16)] * len(n_rows)
    return call(
        functools.partial(
            second_body, wd, wu, layer, mp_size, chunks, len(n_rows), has_next
        ),
        "second",
        out,
        [me, x, par] + n_rows + t_parts,
        smem=1,
        parts=wd.arrays,
        scratch=[
            pltpu.VMEM((chunks * mp_size, wd.rows, LANE), BF16),
            pltpu.VMEM((chunks * mp_size, wu.rows, LANE), BF16),
            pltpu.SemaphoreType.DMA,
            pltpu.SemaphoreType.DMA,
        ],
        flops=2 * rows * model * (3 * model + 2 * ff),
        after=after,
    )


def norm_back(x, gain, d_normed):
    xhat, rstd = norm_parts(x)
    e = d_normed * gain
    mean_e = jnp.mean(e, axis=1, keepdims=True)
    mean_ex = jnp.mean(e * xhat, axis=1, keepdims=True)
    d_gain = jnp.sum(d_normed * xhat, axis=0, keepdims=True)
    d_bias = jnp.sum(d_normed, axis=0, keepdims=True)
    return (e - mean_e - xhat * mean_ex) * rstd, d_gain, d_bias


def second_back_body(
    wd, wu, layer, mp_size, chunks, batch, me_ref, g_ref, mid_ref, n2_ref, s2_ref, slope_ref,
    par_ref, *refs
):
    d_refs, refs = refs[: len(wd.arrays)], refs[len(wd.arrays) :]
    u_refs = d_refs
    b2_ref, dcomb_ref, gmid_ref, b1_ref, sums_ref = refs[:5]
    refs = refs[5:]
    o_refs, refs = [refs[0], refs[1], refs[2].at[0], refs[2].at[1]], refs[3:]
    d_scr, u_scr, d_sem, u_sem = refs
    wu.start(u_refs, me_ref, u_scr, u_sem, chunks)
    wd.start(d_refs, me_ref, d_scr, d_sem, chunks)
    ff = slope_ref.shape[1]
    model = g_ref.shape[1]
    ff_m = ff // mp_size
    ff_blocks = ff_m // LANE
    stride = LANE + ff_m
    part = g_ref.shape[0] // batch
    me_m = me_ref[0]
    every = range(mp_size)
    g = g_ref[...]
    b2_ref[...] = g.astype(BF16)
    s2 = s2_ref[...]
    b2f = b2_ref[...].astype(F32)
    d_z2 = (b2f * n2_ref[...].astype(F32) * s2 * (1.0 - s2)).astype(BF16)
    sums_ref[2:3, :] = jnp.sum(d_z2.astype(F32), axis=0, keepdims=True)
    for m in every:
        dcomb_ref[:, m * stride : m * stride + LANE] = d_z2[:, m * LANE : (m + 1) * LANE]
    wu.wait(u_scr, u_sem)
    wd.wait(d_scr, d_sem)
    for m in every:
        for b in range(0, ff_blocks, 2):
            at = m * ff_m + b * LANE
            d_act = nn(b2_ref[...], wide(d_scr, [(m, 2 + b), (m, 3 + b)], chunks))
            slope = slope_ref[:, at : at + 2 * LANE].astype(F32)
            at = m * stride + (1 + b) * LANE
            dcomb_ref[:, at : at + 2 * LANE] = (d_act * slope).astype(BF16)
    share = chunks // 2
    cols_of = [(m, b) for m in every for b in range(1 + ff_blocks)]
    for j in range(2):
        cols = slice(j * share * CHUNK, (j + 1) * share * CHUNK)
        gmid_ref[:, cols] = b2_ref[:, cols].astype(F32) * s2_ref[:, cols] + nt(
            dcomb_ref[...], wide(u_scr, cols_of, chunks, j * share, (j + 1) * share)
        )
    d_mid, d_gain, d_bias = norm_back(mid_ref[...], par_ref[layer, 1:2], gmid_ref[...])
    sums_ref[0:1, :] = d_gain
    sums_ref[1:2, :] = d_bias
    sums_ref[3:8, :] = jnp.zeros((5, model), F32)
    g_mid = g_ref[...] + d_mid
    gmid_ref[...] = g_mid
    b1_ref[...] = g_mid.astype(BF16)
    for mx in every:
        m = jnp.bitwise_xor(me_m, mx)
        d_att = nn(b1_ref[...], blocks(d_scr, m, 1, chunks)).astype(BF16)
        for r in range(batch):
            o_refs[mx][r] = d_att[r * part : (r + 1) * part]


def second_back(me, g, mid, n2, s2, slope, par, wd, wu, layer, mp_size, chunks, batch, after=()):
    rows, model = g.shape
    ff = slope.shape[1]
    out = [
        sds((rows, model), BF16),
        sds((rows, ff + LANE * mp_size), BF16),
        sds((rows, model), F32),
        sds((rows, model), BF16),
        sds((8, model), F32),
    ]
    out += [sds((batch, rows // batch, LANE), BF16)] * 2
    out += [sds((2, batch, rows // batch, LANE), BF16)]
    return call(
        functools.partial(second_back_body, wd, wu, layer, mp_size, chunks, batch),
        "second_back",
        out,
        [me, g, mid, n2, s2, slope, par],
        smem=1,
        parts=wd.arrays,
        scratch=[
            pltpu.VMEM((chunks * mp_size, wd.rows, LANE), BF16),
            pltpu.VMEM((chunks * mp_size, wu.rows, LANE), BF16),
            pltpu.SemaphoreType.DMA,
            pltpu.SemaphoreType.DMA,
        ],
        flops=2 * rows * model * (2 * model + 2 * ff),
        after=after,
    )


def attend_back_body(wq, row, mp_size, chunks, last, me_ref, seg_ref, segc_ref, segr_ref, *refs):
    qkv_ref, lse_ref = refs[:2]
    d_in, refs = refs[2 : 2 + mp_size], refs[2 + mp_size :]
    d_in = [d_in[0].at[row], d_in[1].at[row], d_in[2].at[0, row], d_in[3].at[1, row]]
    n_refs, refs = refs[:mp_size], refs[mp_size:]
    if last:
        before_ref, refs = refs[0], refs[1:]
    w_refs, refs = refs[: len(wq.arrays)], refs[len(wq.arrays) :]
    keep_ref, send_ref, dw_ref = refs[:3]
    w_scr, do_scr, dqkv_scr, dk_scr, dv_scr, sem = refs[3:]
    wq.start(w_refs, me_ref, w_scr, sem, chunks, own_only=True)
    length = qkv_ref.shape[0]
    part = d_in[0].shape[0]
    me_m, me_d = me_ref[0], me_ref[1]
    for mx in range(mp_size):
        at = pl.multiple_of(jnp.bitwise_xor(me_m, mx) * part, part)
        do_scr[pl.ds(at, part), :] = d_in[mx][...]
    dqkv_scr[...] = jnp.zeros_like(dqkv_scr)
    dk_scr[...] = jnp.zeros_like(dk_scr)
    dv_scr[...] = jnp.zeros_like(dv_scr)
    q_spans = length // SPAN

    def step(q_at, carry):
        low = seg_bounds(seg_ref, q_at, q_spans)
        real = seg_ref[q_at * SPAN] >= 0
        q0 = pl.multiple_of(q_at * SPAN, SPAN)
        k0 = pl.multiple_of(low * SPAN, SPAN)
        for spans in range(1, q_spans + 1):

            @pl.when(real & (q_at - low + 1 == spans))
            def _():
                keys = spans * SPAN
                mask = allowed_t(segc_ref, segr_ref, k0, q0, spans)
                dqs, dks, dvs = [], [], []
                for h in range(2):
                    lo = h * HEAD_DIM
                    q = qkv_ref[pl.ds(q0, SPAN), lo : lo + HEAD_DIM] * jnp.asarray(
                        HEAD_DIM**-0.5, BF16
                    )
                    k = qkv_ref[pl.ds(k0, keys), 128 + lo : 128 + lo + HEAD_DIM]
                    v = qkv_ref[pl.ds(k0, keys), 256 + lo : 256 + lo + HEAD_DIM]
                    do = do_scr[pl.ds(q0, SPAN), lo : lo + HEAD_DIM]
                    lse = lse_ref[h, :, pl.ds(q0, SPAN)]
                    p = jnp.where(mask, jnp.exp(nt(k, q) - lse), 0.0)
                    dvs.append(nn(p.astype(BF16), do))
                    dp = nt(v, do)
                    delta = jnp.sum(p * dp, axis=0, keepdims=True)
                    ds = (p * (dp - delta)).astype(BF16)
                    dks.append(nn(ds, q))
                    dqs.append(tn(k, ds))
                dqkv_scr[pl.ds(q0, SPAN), 0:128] = (
                    jnp.concatenate(dqs, axis=0).T * HEAD_DIM**-0.5
                ).astype(BF16)
                dk_scr[pl.ds(k0, keys), :] += jnp.concatenate(dks, axis=1)
                dv_scr[pl.ds(k0, keys), :] += jnp.concatenate(dvs, axis=1)

        return carry

    lax.fori_loop(0, q_spans, step, 0)
    dqkv_scr[:, 128:256] = dk_scr[...].astype(BF16)
    dqkv_scr[:, 256:384] = dv_scr[...].astype(BF16)
    wq.wait(w_scr, sem)
    weights = wide(w_scr, [(0, 0), (0, 1), (0, 2)], chunks)
    grad = jnp.zeros((n_refs[0].shape[1], 384), F32)
    if last:
        grad = before_ref[...]
    for mx in range(mp_size):
        at = pl.multiple_of(jnp.bitwise_xor(me_m, mx) * part, part)
        d_here = dqkv_scr[pl.ds(at, part), :]
        d_n = nt(d_here, weights).astype(BF16)
        (send_ref if mx % 2 else keep_ref)[mx // 2] = d_n
        grad += tn(n_refs[mx][...], d_here)
    if not last:
        dw_ref[...] = grad
        return
    grad = grad.astype(BF16)
    for d in range(chunks):
        for b in range(3):
            dw_ref[jnp.bitwise_xor(d, me_d), b * CHUNK : (b + 1) * CHUNK, :] = grad[
                d * CHUNK : (d + 1) * CHUNK, b * LANE : (b + 1) * LANE
            ]


def attend_back(
    me, seg, segc, segr, qkv, lse, d_parts, n_parts, wq, row, chunks, before=None, after=()
):
    mp_size = len(d_parts)
    length = seg.shape[0]
    part, model = n_parts[0].shape
    last = before is not None
    out = [sds((mp_size // 2, part, model), BF16)] * 2
    out += [sds((chunks, 3 * CHUNK, LANE), BF16) if last else sds((model, 384), F32)]
    return call(
        functools.partial(attend_back_body, wq, row, mp_size, chunks, last),
        "attend_back",
        out,
        [me, seg, segc, segr, qkv, lse] + d_parts + n_parts + ([before] if last else []),
        smem=2,
        parts=wq.arrays,
        scratch=[
            pltpu.VMEM((chunks, wq.rows, LANE), BF16),
            pltpu.VMEM((length, LANE), BF16),
            pltpu.VMEM((length, 384), BF16),
            pltpu.VMEM((length, LANE), F32),
            pltpu.VMEM((length, LANE), F32),
            pltpu.SemaphoreType.DMA,
        ],
        flops=2 * length * length * HEAD_DIM * 10 + 4 * length * model * 384,
        after=after,
    )


def first_back_body(
    layer, batch, x_ref, gmid_ref, local_ref, par_ref, sums2_ref, sums1_ref, *refs
):
    kept, got = refs[:batch], refs[batch : 2 * batch]
    g_ref, sums_ref = refs[2 * batch :]
    part = kept[0].shape[0]
    for r in range(batch):
        at = slice(r * part, (r + 1) * part)
        g_ref[at, :] = local_ref[at, :] + kept[r][...].astype(F32) + got[r][...].astype(F32)
    d_x, d_gain, d_bias = norm_back(x_ref[...].astype(F32), par_ref[layer, 0:1], g_ref[...])
    g_ref[...] = gmid_ref[...] + d_x
    sums_ref[0:1, :] = d_gain
    sums_ref[1:2, :] = sums2_ref[0:1, :]
    sums_ref[2:3, :] = d_bias
    sums_ref[3:4, :] = sums1_ref[0:1, :]
    sums_ref[4:5, :] = sums2_ref[1:2, :]
    sums_ref[5:6, :] = sums2_ref[2:3, :]
    sums_ref[6:8, :] = sums2_ref[6:8, :]


def first_back(x, gmid, local, par, sums2, sums1, kept, got, layer, after=()):
    rows, model = x.shape
    return call(
        functools.partial(first_back_body, layer, len(kept)),
        "first_back",
        [sds((rows, model), F32), sds((8, model), F32)],
        [x, gmid, local, par, sums2, sums1] + kept + got,
        after=after,
    )


def put_blocks(outs, mx, me_d, chunks, at_block, res, mp_first=False):
    half = chunks // 2
    for d in range(chunks):
        at = jnp.bitwise_xor(d, me_d)
        if mp_first:
            at = (mx // 2) * chunks + at
        else:
            at = (at // half) * chunks + (mx // 2) * half + at % half
        for b in range(res.shape[1] // LANE):
            rows = slice((at_block + b) * CHUNK, (at_block + b + 1) * CHUNK)
            outs[mx % 2][at, rows, :] = res[d * CHUNK : (d + 1) * CHUNK, b * LANE : (b + 1) * LANE]


def weight_grad_body(
    wd, mp_size, chunks, batch, mp_first, me_ref, n2_ref, dcomb_ref, b1_ref, b2_ref, att_ref,
    act_ref, s1_ref, *refs
):
    n_refs, refs = refs[:batch], refs[batch:]
    d_refs, refs = refs[: len(wd.arrays)], refs[len(wd.arrays) :]
    ups, downs, (local_ref, sums_ref), refs = refs[:2], refs[2:4], refs[4:6], refs[6:]
    w_scr, left, n_left, b1_left, z_scr, sem = refs
    wd.start(d_refs, me_ref, w_scr, sem, chunks)
    me_m, me_d = me_ref[0], me_ref[1]
    every = range(mp_size)
    left[...] = n2_ref[...].T
    stride = dcomb_ref.shape[1] // mp_size
    for mx in every:
        m = jnp.bitwise_xor(me_m, mx)
        res = nn(left[...], dcomb_ref[:, pl.ds(col(m * stride), stride)])
        put_blocks(ups, mx, me_d, chunks, 0, res.astype(BF16), mp_first)
    n = jnp.concatenate([ref[...] for ref in n_refs], axis=0)
    b1f = b1_ref[...].astype(F32)
    s1 = s1_ref[...]
    d_z1 = (b1f * n.astype(F32) * s1 * (1.0 - s1)).astype(BF16)
    z_scr[...] = d_z1
    sums_ref[0:1, :] = jnp.sum(d_z1.astype(F32), axis=0, keepdims=True)
    sums_ref[1:8, :] = jnp.zeros((7, sums_ref.shape[1]), F32)
    n_left[...] = n.T
    b1_left[...] = b1_ref[...].T
    left[...] = b2_ref[...].T
    wd.wait(w_scr, sem)
    local_ref[...] = b1f * s1 + nt(d_z1, wide(w_scr, [(m, 0) for m in every], chunks))
    ff_m = act_ref.shape[1] // mp_size
    for mx in every:
        m = jnp.bitwise_xor(me_m, mx)
        cols = pl.ds(col(m * LANE), LANE)
        put_blocks(downs, mx, me_d, chunks, 0, nn(n_left[...], z_scr[:, cols]).astype(BF16))
        put_blocks(downs, mx, me_d, chunks, 1, nn(b1_left[...], att_ref[:, cols]).astype(BF16))
        res = nn(left[...], act_ref[:, pl.ds(col(m * ff_m), ff_m)])
        put_blocks(downs, mx, me_d, chunks, 2, res.astype(BF16))


def weight_grad(
    me, n2, dcomb, b1, b2, att, act, s1, n_rows, wd, mp_size, chunks, mp_first, after=()
):
    rows, model = b1.shape
    gates = Parts(wd.arrays, wd.order, wd.first_row, CHUNK)
    height = dcomb.shape[1] // mp_size // LANE * CHUNK
    return call(
        functools.partial(weight_grad_body, gates, mp_size, chunks, len(n_rows), mp_first),
        "weight_grad",
        [sds((mp_size // 2 * chunks, height, LANE), BF16)] * 2
        + [sds((mp_size // 2 * chunks, wd.rows, LANE), BF16)] * 2
        + [sds((rows, model), F32), sds((8, model), F32)],
        [me, n2, dcomb, b1, b2, att, act, s1] + n_rows,
        smem=1,
        parts=wd.arrays,
        scratch=[pltpu.VMEM((chunks * mp_size, CHUNK, LANE), BF16)]
        + [pltpu.VMEM((model, rows), BF16)] * 3
        + [pltpu.VMEM((rows, model), BF16), pltpu.SemaphoreType.DMA],
        after=after,
    )


def swap(value, axis, size, bits):
    return lax.ppermute(value, axis, [(i, i ^ bits) for i in range(size)])


def add_body(count, *refs):
    left, right = refs[:2]
    outs = refs[2:]
    size = outs[0].shape[0]

    def step(i, carry):
        for part, out in enumerate(outs):
            at = part * size + i
            out[i] = (left[at].astype(F32) + right[at].astype(F32)).astype(BF16)
        return carry

    lax.fori_loop(0, size, step, 0)


def add(left, right, count):
    shape = (left.shape[0] // count,) + left.shape[1:]
    return call(
        functools.partial(add_body, count),
        "add",
        [sds(shape, BF16)] * count,
        [left, right],
    )


def join_body(count, has_sums, me_ref, *refs):
    pairs = [(refs[2 * i], refs[2 * i + 1]) for i in range(count)]
    refs = refs[2 * count :]
    if has_sums:
        sums_ref, refs = refs[0], refs[1:]
    for k, out in enumerate(refs):
        at = 0
        for left, right in pairs:
            rows = left.shape[1]
            out[at : at + rows, :] = (left[k].astype(F32) + right[k].astype(F32)).astype(BF16)
            at += rows
        if has_sums:
            tile = jnp.bitwise_xor(me_ref[1], k) // (LANE // CHUNK)
            out[at:, :] = sums_ref[:, pl.ds(col(tile * LANE), LANE)].astype(BF16)


def join(me, pairs, sums=None):
    width = pairs[0][0].shape[0]
    rows = sum(p[0].shape[1] for p in pairs) + (0 if sums is None else sums.shape[0])
    flat = [a for pair in pairs for a in pair]
    return call(
        functools.partial(join_body, len(pairs), sums is not None),
        "add",
        [sds((rows, LANE), BF16)] * width,
        [me] + flat + ([] if sums is None else [sums]),
        smem=1,
    )


def total_body(*refs):
    value = refs[0][...].astype(F32)
    for ref in refs[1:-1]:
        value += ref[...].astype(F32)
    refs[-1][...] = value


def total(parts):
    return call(total_body, "add", [sds(parts[0].shape, F32)], parts)[0]


def stack_body(*refs):
    for i, ref in enumerate(refs[:-1]):
        refs[-1][i] = ref[...]


def stack(arrays, after=()):
    shape = (len(arrays),) + arrays[0].shape
    return call(stack_body, "stack", [sds(shape, BF16)], arrays, after=after)[0]


def pack_body(layer, q_rows, *refs):
    if q_rows:
        refs[-1][0:q_rows, :] = refs[0][...]
    gate_ref, out_ref, up_ref, down_ref, shard_ref = refs[-5:]
    per = gate_ref.shape[2]
    at = q_rows
    for matrix in (gate_ref[layer, 0], out_ref[layer].T, None, gate_ref[layer, 1], up_ref[layer]):
        if matrix is None:
            matrix = down_ref[layer].T
        for b in range(matrix.shape[1] // LANE):
            shard_ref[at : at + per, :] = matrix[:, b * LANE : (b + 1) * LANE]
            at += per


def pack(layer, q, w_gate, w_out, w_up, w_down, after=()):
    per = w_gate.shape[2]
    rows = (2 * w_gate.shape[3] + w_out.shape[1] + w_up.shape[2] + w_down.shape[1]) // LANE * per
    q_rows = sum(a.shape[0] for a in q)
    return call(
        functools.partial(pack_body, layer, q_rows),
        "pack",
        [sds((q_rows + rows, LANE), BF16)],
        q + [w_gate, w_out, w_up, w_down],
        after=after,
    )[0]


def solution(mesh):
    dp_size, mp_size, width_size = (mesh.shape[a] for a in ("dp", "mp", "width"))
    all_axes = ("mp", "dp", "width")
    direct = (dp_size, mp_size, width_size) == (2, 4, 4)

    def mp_swap(value, bits):
        return swap(value, "mp", mp_size, bits)

    def dp_swap(value):
        return swap(value, "dp", dp_size, 1)

    def spread(value):
        far = mp_swap(value, 2)
        return [value, mp_swap(value, 1), far, mp_swap(far, 1)]

    def exchange(own, near, far):
        far = mp_swap(far, 2)
        return [own, mp_swap(near, 1), far, mp_swap(far, 1)]

    def send_width(value):
        return [value] + [swap(value, "width", width_size, k) for k in range(1, width_size)]

    def swap_width(values):
        return [values[0]] + [
            swap(values[k], "width", width_size, k) for k in range(1, width_size)
        ]

    def on_device(
        tokens, segments, cotangent, norm_gains, biases, w_qkv, w_out, w_gate, w_up, w_down
    ):
        ORDER.token = None
        batch, part, model = tokens.shape
        layers = w_qkv.shape[0]
        per = w_qkv.shape[1]
        chunks = model // CHUNK
        half = chunks // 2
        ff_m = w_up.shape[2]
        ff_blocks = ff_m // LANE
        ff = ff_m * mp_size
        me_m = lax.axis_index("mp")
        me_d = lax.axis_index("dp") * width_size + lax.axis_index("width")
        me = jnp.stack([me_m, me_d]).astype(jnp.int32)
        me_pack = me if direct else me * 0
        me_att = me if direct else jnp.stack([me_m, 0]).astype(jnp.int32)

        def blocks_of(matrix):
            return jnp.swapaxes(matrix.reshape(per, -1, LANE), 0, 1).reshape(-1, LANE)

        def param_block():
            rows = jnp.concatenate([norm_gains, biases], axis=1)
            rows = jnp.pad(rows, ((0, 0), (0, 2), (0, 0))).reshape(layers * 8, per)
            rows = jnp.concatenate([rows] * (LANE // per), axis=1)
            share = lax.broadcasted_iota(jnp.int32, rows.shape, 1) // per
            return jnp.where(share == me_d % (LANE // per), rows, 0)

        q_rows, d_rows, u_rows = 3 * CHUNK, (2 + ff_blocks) * CHUNK, (1 + ff_blocks) * CHUNK

        def q_shard(l):
            return blocks_of(w_qkv[l].reshape(per, -1))

        def shard(l, q, after=()):
            if direct:
                return pack(l, q, w_gate, w_out, w_up, w_down, after)
            mats = [w_gate[l, 0], w_out[l].T, blocks_of(w_down[l].T), w_gate[l, 1]]
            return jnp.concatenate(q + mats + [blocks_of(w_up[l])], axis=0)

        def gather_whole(shard, extra):
            full = lax.all_gather(shard, all_axes, axis=0, tiled=False)
            if per == CHUNK:
                return full
            count = (shard.shape[0] - extra) // per
            full = full.reshape(mp_size, chunks, CHUNK // per, shard.shape[0], LANE)
            mats = full[:, :, :, : count * per]
            mats = mats.reshape(mp_size, chunks, CHUNK // per, count, per, LANE)
            mats = jnp.swapaxes(mats, 2, 3).reshape(mp_size * chunks, count * CHUNK, LANE)
            if not extra:
                return mats
            pars = jnp.sum(full[:, :, :, count * per :].astype(F32), axis=2).astype(BF16)
            return jnp.concatenate([mats, pars.reshape(mp_size * chunks, extra, LANE)], axis=1)

        def reduce_whole(even, odd):
            full = jnp.stack([even, odd], axis=1)
            full = full.reshape(2, mp_size // 2, half, 2, -1, CHUNK // per, per, LANE)
            full = jnp.transpose(full, (1, 3, 0, 2, 5, 4, 6, 7)).reshape(-1, LANE).astype(F32)
            return lax.psum_scatter(full, all_axes, scatter_dimension=0, tiled=True)

        def reduce_q_whole(grad):
            full = grad.reshape(chunks, -1, CHUNK // per, per, LANE)
            full = jnp.swapaxes(full, 1, 2).reshape(-1, LANE).astype(F32)
            return lax.psum_scatter(full, ("dp", "width"), scatter_dimension=0, tiled=True)

        segc = jnp.broadcast_to(segments[:, :, None], segments.shape + (LANE,))
        segs = [(segments[r], segc[r], segments[r : r + 1]) for r in range(batch)]

        q_all = q_rows + layers * 8
        q_sh = jnp.concatenate([q_shard(0), param_block()], axis=0)
        t_all = spread(tokens)
        weights = [None] * layers
        if direct:
            q_steps = send_width(q_sh)
            w_steps = send_width(shard(0, []))
            q_base = stack(q_steps)
            wq = Parts([q_base, dp_swap(q_base)], [(0, 0), (0, 4)], 0, q_all)
            base = stack(w_steps)
            got = {(0, 0): base, (0, 4): dp_swap(base), (2, 0): mp_swap(base, 2)}
            arrived = [got[0, 4], got[2, 0]]
        else:
            wq = Parts([gather_whole(q_sh, layers * 8)], None, 0, q_all)
            full = gather_whole(shard(0, []), 0)
            wd, wu = Parts([full], None, 0, d_rows), Parts([full], None, d_rows, u_rows)
            arrived = []

        x = tokens.reshape(batch * part, model)
        par = None
        saved = []
        t_parts = [t_all] * batch
        for l in range(layers):
            if l:
                wq, wd, wu = weights[l]
            n_parts, o_parts, kept = [], [], []
            for r in range(batch):
                qkv, lse, own, near, far, *rest = attend(
                    me, *segs[r], t_parts[r], wq, l, r, layers, l == 0, chunks
                )
                if l == 0:
                    par = rest[0]
                    n_parts.append(rest[1:])
                else:
                    n_parts.append(t_parts[r])
                kept.append((qkv, lse))
                o_parts += exchange(own, near, far)
                if l == 0 and r == 0:
                    for k in range(1, layers):
                        full = gather_whole(shard(k, [q_shard(k)], arrived), 0)
                        weights[k] = (
                            Parts([full], None, 0, q_rows),
                            Parts([full], None, q_rows, d_rows),
                            Parts([full], None, q_rows + d_rows, u_rows),
                        )
            if l == 0:
                if direct:
                    got[2, 4] = dp_swap(got[2, 0])
                    for m, d in list(got):
                        got[m + 1, d] = mp_swap(got[m, d], 1)
                    arrays, order = list(got.values()), list(got)
                    wd, wu = Parts(arrays, order, 0, d_rows), Parts(arrays, order, d_rows, u_rows)
                weights[0] = (wq, wd, wu)
            n_rows = [n_parts[r][0] for r in range(batch)]
            att, s1, mid, n2, s2, act, slope, out, *following = second(
                me, x, par, n_rows, o_parts, wd, wu, l, chunks, ff, l + 1 < layers
            )
            saved.append((x, n_parts, kept, att, s1, mid, n2, s2, act, slope))
            x = out
            if following:
                t_parts = [spread(n) for n in following]
        output = x.reshape(batch, part, model)

        own = lax.dynamic_slice_in_dim(segments, me_m * part, part, 1)
        g = cotangent.astype(F32) * (own >= 0).astype(F32)[:, :, None]
        g = g.reshape(batch * part, model)
        reduced = [None] * layers
        all_sums = [None] * layers
        moving = {}

        def reduce_2(name, mp_first=False):
            if name in moving:
                keep, send = add(*moving[name], 2)
                moving[name] = (keep, mp_swap(send, 2) if mp_first else dp_swap(send))

        def reduce_3(name, mp_first=False):
            if name in moving:
                keep, send = add(*moving[name], 2)
                moving[name] = (keep, dp_swap(send) if mp_first else mp_swap(send, 2))

        def reduce_4(names, sums=None):
            if direct:
                pairs = [moving.pop(name) for name in names]
                moving[names[0]] = swap_width(join(me, pairs, sums))

        def reduce_5(name):
            return total(moving.pop(name)) if direct else None

        for l in reversed(range(layers)):
            wq, wd, wu = weights[l]
            x, n_parts, kept, att, s1, mid, n2, s2, act, slope = saved[l]
            n_rows = [n_parts[r][0] for r in range(batch)]
            final, first_of_two = l == 0, l + 1 < layers
            b2, dcomb, gmid, b1, sums2, *o_parts = second_back(
                me, g, mid, n2, s2, slope, par, wd, wu, l, mp_size, chunks, batch
            )
            d_parts = exchange(*o_parts)
            reduce_3(("d", l + 1))
            *grads, local, sums1 = weight_grad(
                me_pack, n2, dcomb, b1, b2, att, act, s1, n_rows, wd, mp_size, chunks,
                final and direct,
            )
            if direct:
                moving["u", l] = (grads[0], mp_swap(grads[1], 1))
                moving["d", l] = (grads[2], mp_swap(grads[3], 1))
            keeps, gots = [], []
            q_grad = None
            for r in range(batch):
                keep, send, q_grad = attend_back(
                    me_att, *segs[r], *kept[r], d_parts, n_parts[r], wq, r, chunks, q_grad
                )
                if r == 0:
                    reduce_2(("d", l))
                    reduce_2(("u", l), final)
                else:
                    reduce_3(("u", l), final)
                    if final:
                        reduce_3(("d", l))
                keep, send = add(keep, mp_swap(send, 1), 2)
                keeps.append(keep.reshape(keep.shape[1:]))
                gots.append(mp_swap(send, 2).reshape(keep.shape[1:]))
            if direct:
                moving["q", l] = (q_grad[:half], dp_swap(q_grad[half:]))
                if first_of_two:
                    reduce_4([("q", l + 1), ("u", l + 1), ("d", l + 1)])
            g, all_sums[l] = first_back(x, gmid, local, par, sums2, sums1, keeps, gots, l)
            if direct and first_of_two:
                reduced[l + 1] = reduce_5(("q", l + 1))
            if not direct:
                reduced[l] = (reduce_q_whole(q_grad), reduce_whole(*grads[:2]), reduce_whole(*grads[2:]))
        d_tokens = g.reshape(batch, part, model)
        sums = jnp.concatenate(all_sums, axis=0)
        if direct:
            sums = sums + mp_swap(sums, 1)
            sums = sums + mp_swap(sums, 2)
            sums = sums + dp_swap(sums)
            reduce_4([("u", 0)])
            reduce_4([("q", 0), ("d", 0)], sums)
            u_sum = reduce_5(("u", 0))
            rest = reduce_5(("q", 0))
            reduced[0] = jnp.concatenate(
                [rest[:q_rows], u_sum, rest[q_rows : q_rows + d_rows]], axis=0
            )
            rest = rest[q_rows + d_rows :]
            params = jnp.where(me_d % 2 == 0, rest[:, :CHUNK], rest[:, CHUNK:])
            reduced = [
                (a[:q_rows], a[q_rows : q_rows + u_rows], a[q_rows + u_rows :]) for a in reduced
            ]
        else:
            params = lax.dynamic_slice_in_dim(lax.psum(sums, all_axes), me_d * per, per, 1)
        params = params.reshape(layers, 8, per)

        def unblocks(rows, count):
            return jnp.swapaxes(rows.reshape(count, per, LANE), 0, 1).reshape(per, count * LANE)

        grads = []
        for q_sum, up_sum, down_sum in reduced:
            grads.append(
                (
                    unblocks(q_sum, 3).reshape(per, 3, LANE),
                    down_sum[per : 2 * per].T,
                    jnp.stack([down_sum[:per], up_sum[:per]]),
                    unblocks(up_sum[per:], ff_blocks),
                    unblocks(down_sum[2 * per :], ff_blocks).T,
                )
            )
        stacked = [jnp.stack([grads[l][i] for l in range(layers)]) for i in range(5)]
        return (
            output,
            d_tokens,
            params[:, 0:2],
            params[:, 2:6:2],
            params[:, 3:6:2],
            *stacked,
        )

    placed = (
        P(("dp", "width"), "mp", None),
        P(("dp", "width"), None),
        P(("dp", "width"), "mp", None),
        P(None, None, ("dp", "width")),
        P(None, None, ("dp", "width")),
        P(None, ("dp", "width"), None, "mp"),
        P(None, "mp", ("dp", "width")),
        P(None, None, ("dp", "width"), "mp"),
        P(None, ("dp", "width"), "mp"),
        P(None, "mp", ("dp", "width")),
    )
    return jax.shard_map(
        on_device,
        mesh=mesh,
        in_specs=placed,
        out_specs=(
            placed[0],
            placed[0],
            placed[3],
            placed[3],
            placed[3],
            placed[5],
            placed[6],
            placed[7],
            placed[8],
            placed[9],
        ),
        check_vma=False,
    )
```

```python
import functools

import jax
import jax.numpy as jnp
from jax import lax
from jax.experimental import pallas as pl
from jax.experimental.pallas import tpu as pltpu
from jax.sharding import PartitionSpec as P

HEAD_DIM = 64
LANE = 128
NORM_EPS = 1e-05
SPAN = 256
CHUNK = 64

VALUES_MB = {
    "attend": 6,
    "second": 10,
    "second_back": 10,
    "attend_back": 8,
    "first_back": 6,
    "weight_grad": 8,
    "stack": 2,
    "add": 2,
    "pack": 2,
    "finish": 4,
}

KERNEL_US = {
    "attend": 8,
    "second": 12,
    "second_back": 10,
    "attend_back": 9,
    "first_back": 4,
    "weight_grad": 8,
    "stack": 1,
    "add": 1,
    "pack": 1,
    "finish": 2,
}

F32 = jnp.float32
BF16 = jnp.bfloat16


def nn(a, b):
    return jnp.dot(a, b, preferred_element_type=F32)


def nt(a, b):
    return lax.dot_general(a, b, (((1,), (1,)), ((), ())), preferred_element_type=F32)


def tn(a, b):
    return lax.dot_general(a, b, (((0,), (0,)), ((), ())), preferred_element_type=F32)


def sds(shape, dtype):
    return jax.ShapeDtypeStruct(shape, dtype)


class Late:
    def __init__(self, array):
        self.array = array


class Copies:
    def __init__(self, pairs, first_out, sems):
        self.first_out = first_out
        self.all = [
            (ref, pltpu.make_async_copy(*pair, sems.at[i]))
            for i, (ref, *pair) in enumerate(pairs)
        ]
        self.waiting = []
        self.unsent = list(self.all[first_out:])
        for ref, copy in self.all[:first_out]:
            copy.start()
            self.waiting.append((ref, copy))

    def need(self, *refs):
        for ref in refs:
            for i, entry in enumerate(self.waiting):
                if entry[0] is ref:
                    entry[1].wait()
                    del self.waiting[i]
                    break

    def send(self, *refs):
        for ref in refs:
            for i, entry in enumerate(self.unsent):
                if entry[0] is ref:
                    entry[1].start()
                    del self.unsent[i]
                    break

    def finish(self):
        for _, copy in self.waiting:
            copy.wait()
        for _, copy in self.unsent:
            copy.start()
        for _, copy in self.all[self.first_out :]:
            copy.wait()


class Chain:
    def __init__(self):
        self.token = None
        self.copies = None


ORDER = Chain()


def need(*refs):
    ORDER.copies.need(*refs)


def send(*refs):
    ORDER.copies.send(*refs)


def in_hbm(a):
    return pltpu.with_memory_space_constraint(a, pltpu.HBM)


def size_of(a):
    return a.size * a.dtype.itemsize


def call(body, name, out_shape, args, smem=0, parts=(), scratch=(), after=()):
    after = list(after) + ([] if ORDER.token is None else [ORDER.token])
    late_in = [i for i, a in enumerate(args) if isinstance(a, Late)]
    late_out = [i for i, o in enumerate(out_shape) if isinstance(o, Late)]
    args = [in_hbm(a.array) if isinstance(a, Late) else a for a in args]
    out_shape = [o.array if isinstance(o, Late) else o for o in out_shape]
    parts = [in_hbm(a) for a in parts]
    hbm, vmem = (pl.BlockSpec(memory_space=space) for space in (pltpu.HBM, pltpu.VMEM))
    specs = [pl.BlockSpec(memory_space=pltpu.SMEM)] * smem
    specs += [hbm if i in late_in else vmem for i in range(smem, len(args))]
    specs += [hbm] * len(parts)
    specs += [pl.BlockSpec(memory_space=pl.ANY)] * len(after)
    used = len(args) + len(parts)
    given = used + len(after)
    outs = len(out_shape)
    late = [args[i] for i in late_in] + [out_shape[i] for i in late_out]
    room = [pltpu.VMEM(a.shape, a.dtype) for a in late]
    sems = [pltpu.SemaphoreType.DMA((len(late),))] if late else []

    def inner(*refs):
        ins, results = list(refs[:used]), list(refs[given : given + outs])
        rest = refs[given + outs + 1 :]
        own = rest[: len(scratch)]
        places = rest[len(scratch) : len(scratch) + len(late)]
        pairs = []
        for i, place in zip(late_in, places):
            pairs.append((place, ins[i], place))
            ins[i] = place
        for i, place in zip(late_out, places[len(late_in) :]):
            pairs.append((place, place, results[i]))
            results[i] = place
        copies = ORDER.copies = Copies(pairs, len(late_in), rest[-1] if late else None)
        body(*ins, *results, *own)
        copies.finish()

    nbytes = sum(size_of(a) for a in args + out_shape)
    for s in scratch:
        if hasattr(s, "shape") and len(s.shape) > 1:
            nbytes += size_of(jax.ShapeDtypeStruct(s.shape, s.dtype))
    *result, ORDER.token = pl.pallas_call(
        inner,
        name=name,
        out_shape=[
            pltpu.HBM(o.shape, o.dtype) if i in late_out else o for i, o in enumerate(out_shape)
        ]
        + [sds((8, LANE), F32)],
        in_specs=specs,
        out_specs=[hbm if i in late_out else vmem for i in range(outs)]
        + [pl.BlockSpec(memory_space=pl.ANY)],
        scratch_shapes=list(scratch) + room + sems,
        cost_estimate=pl.CostEstimate(
            flops=int(0.2 * KERNEL_US[name] * 1.1e9),
            bytes_accessed=int(0.2 * KERNEL_US[name] * 3.6e6),
            transcendentals=0,
        ),
        compiler_params=pltpu.CompilerParams(
            vmem_limit_bytes=int(1.02 * nbytes) + VALUES_MB[name] * 2**20
        ),
    )(*args, *parts, *after)
    return result


def col(start):
    return pl.multiple_of(start, LANE)


class Parts:
    def __init__(self, arrays, order, first_row, rows):
        self.arrays = arrays
        self.order = order
        self.first_row = first_row
        self.rows = rows

    def open(self, refs, me_ref, dst, sem, chunks, own_only=False):
        rows = pl.ds(self.first_row, self.rows)
        if self.order is None:
            src = refs[0].at[:, rows, :]
            if own_only:
                src = refs[0].at[pl.ds(me_ref[0] * chunks, chunks), rows, :]
            pltpu.make_async_copy(src, dst, sem).start()
            return Blocks(dst, sem, chunks, 0, 0)
        for ref, (mx, dx) in zip(refs, self.order):
            at = pl.ds((0 if own_only else mx * chunks) + dx, ref.shape[0])
            pltpu.make_async_copy(ref.at[:, rows, :], dst.at[at], sem).start()
        return Blocks(dst, sem, chunks, 0 if own_only else me_ref[0], me_ref[1])


class Blocks:
    def __init__(self, ref, sem, chunks, turn_m, turn_d):
        self.ref, self.sem, self.chunks = ref, sem, chunks
        self.turn_m, self.turn_d = turn_m, turn_d

    def wait(self):
        pltpu.make_async_copy(self.ref, self.ref, self.sem).wait()

    def place(self, m, d):
        if isinstance(self.turn_d, int):
            return m * self.chunks + d
        return jnp.bitwise_xor(m, self.turn_m) * self.chunks + jnp.bitwise_xor(d, self.turn_d)

    def block(self, m, b, lo=0, hi=None):
        rows = pl.ds(b * CHUNK, CHUNK)
        hi = self.chunks if hi is None else hi
        return jnp.concatenate([self.ref[self.place(m, d), rows, :] for d in range(lo, hi)], axis=0)

    def wide(self, which, lo=0, hi=None):
        return jnp.concatenate([self.block(m, b, lo, hi) for m, b in which], axis=1)

    def params(self, first_row, layer):
        rows = slice(first_row + 8 * layer, first_row + 8 * layer + 8)
        share = LANE // CHUNK
        tiles = []
        for i in range(self.chunks // share):
            tile = self.ref[self.place(0, i * share), rows, :].astype(F32)
            for j in range(1, share):
                tile += self.ref[self.place(0, i * share + j), rows, :].astype(F32)
            tiles.append(tile)
        return jnp.concatenate(tiles, axis=1)


def norm_parts(x):
    mean = jnp.mean(x, axis=1, keepdims=True)
    centred = x - mean
    rstd = lax.rsqrt(jnp.mean(centred * centred, axis=1, keepdims=True) + NORM_EPS)
    return centred * rstd, rstd


def sigmoid(v):
    return 1.0 / (1.0 + jnp.exp(-v))


def rows_at(me_ref, at, part):
    return pl.ds(pl.multiple_of(me_ref[2 + at] * part, part), part)


def seg_bounds(seg_ref, q_at, q_spans):
    first_id = seg_ref[q_at * SPAN]
    first_id = jnp.where(first_id < 0, 1 << 20, first_id)
    low = jnp.int32(0)
    for kb in range(q_spans - 1):
        last_id = seg_ref[(kb + 1) * SPAN - 1]
        last_id = jnp.where(last_id < 0, 1 << 20, last_id)
        low += jnp.where((kb < q_at) & (last_id < first_id), 1, 0)
    return low


def allowed_t(segc_ref, segr_ref, k0, q0, spans):
    keys = spans * SPAN
    seg_k = segc_ref[pl.ds(k0, keys), :]
    seg_q = segr_ref[:, pl.ds(q0, SPAN)]
    same = jnp.concatenate([seg_k == seg_q[:, :LANE], seg_k == seg_q[:, LANE:]], axis=1)
    tri = lax.broadcasted_iota(jnp.int32, (SPAN, SPAN), 0) <= (
        lax.broadcasted_iota(jnp.int32, (SPAN, SPAN), 1)
    )
    if spans == 1:
        return same & tri
    return jnp.concatenate([same[: keys - SPAN], same[keys - SPAN :] & tri], axis=0)


def attend_body(
    wq, layer, row, norm_here, mp_size, chunks, me_ref, seg_ref, segc_ref, segr_ref, *refs
):
    t_refs, refs = refs[:mp_size], refs[mp_size:]
    if norm_here:
        t_refs = [ref.at[me_ref[2 + row]] for ref in t_refs]
    w_refs, refs = refs[: len(wq.arrays)], refs[len(wq.arrays) :]
    qkv_ref, lse_ref = refs[:2]
    o_refs, refs = [refs[2], refs[3], refs[4].at[0], refs[4].at[1]], refs[5:]
    if norm_here:
        par_ref, n_refs, refs = refs[0], refs[1 : 1 + mp_size], refs[1 + mp_size :]
    w_scr, o_scr, sem = refs
    part = t_refs[0].shape[0]
    me_m = me_ref[0]
    w = wq.open(w_refs, me_ref, w_scr, sem, chunks, own_only=True)
    w.wait()
    if norm_here:
        for l in range(par_ref.shape[0]):
            par_ref[l] = w.params(3 * CHUNK, l)
    weights = w.wide([(0, 0), (0, 1), (0, 2)])
    for mx in range(mp_size):
        at = pl.ds(pl.multiple_of(jnp.bitwise_xor(me_m, mx) * part, part), part)
        if norm_here:
            xhat, _ = norm_parts(t_refs[mx][...].astype(F32))
            n = (xhat * par_ref[layer, 0:1] + par_ref[layer, 2:3]).astype(BF16)
            n_refs[mx][...] = n
            send(n_refs[mx])
        else:
            n = t_refs[mx][...]
        qkv_ref[at, :] = nn(n, weights).astype(BF16)
    send(qkv_ref)
    q_spans = qkv_ref.shape[0] // SPAN

    def step(q_at, carry):
        low = seg_bounds(seg_ref, q_at, q_spans)
        q0 = pl.multiple_of(q_at * SPAN, SPAN)
        k0 = pl.multiple_of(low * SPAN, SPAN)
        for spans in range(1, q_spans + 1):

            @pl.when(q_at - low + 1 == spans)
            def _():
                keys = spans * SPAN
                mask = allowed_t(segc_ref, segr_ref, k0, q0, spans)
                outs = []
                for h in range(2):
                    lo = h * HEAD_DIM
                    q = qkv_ref[pl.ds(q0, SPAN), lo : lo + HEAD_DIM] * jnp.asarray(
                        HEAD_DIM**-0.5, BF16
                    )
                    k = qkv_ref[pl.ds(k0, keys), 128 + lo : 128 + lo + HEAD_DIM]
                    v = qkv_ref[pl.ds(k0, keys), 256 + lo : 256 + lo + HEAD_DIM]
                    s = jnp.where(mask, nt(k, q), -1e30)
                    top = jnp.max(s, axis=0, keepdims=True)
                    p = jnp.exp(s - top)
                    total = jnp.sum(p, axis=0, keepdims=True)
                    lse_ref[h, :, pl.ds(q0, SPAN)] = top + jnp.log(total)
                    outs.append(tn(v, p.astype(BF16)) / total)
                o_scr[pl.ds(q0, SPAN), :] = jnp.concatenate(outs, axis=0).T.astype(BF16)

        return carry

    lax.fori_loop(0, q_spans, step, 0)
    for mx in range(mp_size):
        at = pl.multiple_of(jnp.bitwise_xor(me_m, mx) * part, part)
        o_refs[mx][...] = o_scr[pl.ds(at, part), :]


def attend(me, seg, segc, segr, t_parts, wq, layer, row, layers, norm_here, chunks, after=()):
    mp_size = len(t_parts)
    length = seg.shape[0]
    part, model = t_parts[0].shape[-2:]
    out = [sds((length, 384), BF16), sds((2, 1, length), F32)]
    if norm_here:
        out = [Late(o) for o in out]
    out += [sds((part, LANE), BF16)] * 2 + [sds((2, part, LANE), BF16)]
    if norm_here:
        out += [sds((layers, 8, model), F32)] + [Late(sds((part, model), BF16))] * mp_size
    return call(
        functools.partial(attend_body, wq, layer, row, norm_here, mp_size, chunks),
        "attend",
        out,
        [me, seg, segc, segr] + t_parts,
        smem=2,
        parts=wq.arrays,
        scratch=[
            pltpu.VMEM((chunks, wq.rows, LANE), BF16),
            pltpu.VMEM((length, LANE), BF16),
            pltpu.SemaphoreType.DMA,
        ],
        after=after,
    )


def second_body(
    wd, wu, layer, mp_size, chunks, batch, has_next, me_ref, x_ref, par_ref, *refs
):
    n_refs, refs = refs[:batch], refs[batch:]
    t_refs, refs = refs[: mp_size * batch], refs[mp_size * batch :]
    for r in range(batch):
        at = r * mp_size
        t_refs = (*t_refs[: at + 2], t_refs[at + 2].at[0], t_refs[at + 3].at[1], *t_refs[at + 4 :])
    d_refs, refs = refs[: len(wd.arrays)], refs[len(wd.arrays) :]
    u_refs = d_refs
    att_ref, s1_ref, mid_ref, n2_ref, s2_ref, act_ref, slope_ref, out_ref = refs[:8]
    refs = refs[8:]
    if has_next:
        next_refs, refs = refs[:batch], refs[batch:]
    n_scr, d_scr, u_scr, d_sem, u_sem = refs
    w_d = wd.open(d_refs, me_ref, d_scr, d_sem, chunks)
    w_u = wu.open(u_refs, me_ref, u_scr, u_sem, chunks)
    me_m = me_ref[0]
    part = n_refs[0].shape[0]
    par = par_ref.at[layer]
    for r in range(batch):
        for mx in range(mp_size):
            m = jnp.bitwise_xor(me_m, mx)
            att_ref[rows_at(me_ref, r, part), pl.ds(col(m * LANE), LANE)] = t_refs[
                r * mp_size + mx
            ][...]
    send(att_ref)
    need(*n_refs)
    for r in range(batch):
        n_scr[rows_at(me_ref, r, part), :] = n_refs[r][...]
    n = n_scr[...]
    every = range(mp_size)
    w_d.wait()
    s1 = sigmoid(nn(n, w_d.wide([(m, 0) for m in every])) + par[3:4])
    s1_ref[...] = s1
    send(s1_ref)
    need(x_ref)
    mid = (
        x_ref[...].astype(F32)
        + nt(att_ref[...], w_d.wide([(m, 1) for m in every]))
        + s1 * n.astype(F32)
    )
    mid_ref[...] = mid
    send(mid_ref)
    xhat, _ = norm_parts(mid)
    n2_ref[...] = (xhat * par[1:2] + par[4:5]).astype(BF16)
    send(n2_ref)
    w_u.wait()
    s2_ref[...] = sigmoid(nn(n2_ref[...], w_u.wide([(m, 0) for m in every])) + par[5:6])
    send(s2_ref)
    ff_blocks = act_ref.shape[1] // (mp_size * LANE)
    for m in every:
        for b in range(0, ff_blocks, 2):
            at = (m * ff_blocks + b) * LANE
            cols = slice(at, at + 2 * LANE)
            hidden = nn(n2_ref[...], w_u.wide([(m, 1 + b), (m, 2 + b)]))
            square = hidden * hidden
            inner = 0.7978845608 + (0.7978845608 * 0.044715) * square
            th = jnp.tanh(hidden * inner)
            half = 0.5 + 0.5 * th
            act = hidden * half
            act_ref[:, cols] = act.astype(BF16)
            slope = half + act * (1.0 - th) * (3.0 * inner - 2 * 0.7978845608)
            slope_ref[:, cols] = slope.astype(BF16)
    send(act_ref, slope_ref)
    share = chunks // 2
    for j in range(2):
        cols = slice(j * share * CHUNK, (j + 1) * share * CHUNK)
        down = [(m, 2 + b) for m in every for b in range(ff_blocks)]
        out_ref[:, cols] = (
            mid_ref[:, cols]
            + s2_ref[:, cols] * n2_ref[:, cols].astype(F32)
            + nt(act_ref[...], w_d.wide(down, j * share, (j + 1) * share))
        )
    send(out_ref)
    if has_next:
        xhat, _ = norm_parts(out_ref[...])
        n_scr[...] = (xhat * par_ref[layer + 1, 0:1] + par_ref[layer + 1, 2:3]).astype(BF16)
        for r in range(batch):
            next_refs[r][...] = n_scr[rows_at(me_ref, r, part), :]


def second(me, x, par, n_rows, t_parts, wd, wu, layer, chunks, ff, has_next, after=()):
    rows, model = x.shape
    mp_size = len(t_parts) // len(n_rows)
    out = [
        sds((rows, model), BF16),
        sds((rows, model), F32),
        sds((rows, model), F32),
        sds((rows, model), BF16),
        sds((rows, model), F32),
        sds((rows, ff), BF16),
        sds((rows, ff), BF16),
        sds((rows, model), F32),
    ]
    out = [Late(o) for o in out]
    if has_next:
        out += [sds(n_rows[0].shape, BF16)] * len(n_rows)
    return call(
        functools.partial(
            second_body, wd, wu, layer, mp_size, chunks, len(n_rows), has_next
        ),
        "second",
        out,
        [me, Late(x), par] + [Late(n) for n in n_rows] + t_parts,
        smem=1,
        parts=wd.arrays,
        scratch=[
            pltpu.VMEM((rows, model), BF16),
            pltpu.VMEM((chunks * mp_size, wd.rows, LANE), BF16),
            pltpu.VMEM((chunks * mp_size, wu.rows, LANE), BF16),
            pltpu.SemaphoreType.DMA,
            pltpu.SemaphoreType.DMA,
        ],
        after=after,
    )


def norm_back(x, gain, d_normed):
    xhat, rstd = norm_parts(x)
    e = d_normed * gain
    mean_e = jnp.mean(e, axis=1, keepdims=True)
    mean_ex = jnp.mean(e * xhat, axis=1, keepdims=True)
    d_gain = jnp.sum(d_normed * xhat, axis=0, keepdims=True)
    d_bias = jnp.sum(d_normed, axis=0, keepdims=True)
    return (e - mean_e - xhat * mean_ex) * rstd, d_gain, d_bias


def second_back_body(
    wd, wu, layer, mp_size, chunks, batch, me_ref, g_ref, mid_ref, n2_ref, s2_ref, slope_ref,
    par_ref, *refs
):
    d_refs, refs = refs[: len(wd.arrays)], refs[len(wd.arrays) :]
    u_refs = d_refs
    b2_ref, dcomb_ref, gmid_ref, b1_ref, sums_ref = refs[:5]
    refs = refs[5:]
    o_refs, refs = [refs[0], refs[1], refs[2].at[0], refs[2].at[1]], refs[3:]
    o_scr, d_scr, u_scr, d_sem, u_sem = refs
    w_d = wd.open(d_refs, me_ref, d_scr, d_sem, chunks)
    w_u = wu.open(u_refs, me_ref, u_scr, u_sem, chunks)
    ff = slope_ref.shape[1]
    model = g_ref.shape[1]
    ff_m = ff // mp_size
    ff_blocks = ff_m // LANE
    stride = LANE + ff_m
    part = g_ref.shape[0] // batch
    me_m = me_ref[0]
    every = range(mp_size)
    g = g_ref[...]
    b2_ref[...] = g.astype(BF16)
    need(n2_ref, s2_ref)
    s2 = s2_ref[...]
    b2f = b2_ref[...].astype(F32)
    d_z2 = (b2f * n2_ref[...].astype(F32) * s2 * (1.0 - s2)).astype(BF16)
    sums_ref[2:3, :] = jnp.sum(d_z2.astype(F32), axis=0, keepdims=True)
    for m in every:
        dcomb_ref[:, m * stride : m * stride + LANE] = d_z2[:, m * LANE : (m + 1) * LANE]
    w_d.wait()
    need(slope_ref)
    for m in every:
        for b in range(0, ff_blocks, 2):
            at = m * ff_m + b * LANE
            d_act = nn(b2_ref[...], w_d.wide([(m, 2 + b), (m, 3 + b)]))
            slope = slope_ref[:, at : at + 2 * LANE].astype(F32)
            at = m * stride + (1 + b) * LANE
            dcomb_ref[:, at : at + 2 * LANE] = (d_act * slope).astype(BF16)
    w_u.wait()
    share = chunks // 2
    cols_of = [(m, b) for m in every for b in range(1 + ff_blocks)]
    for j in range(2):
        cols = slice(j * share * CHUNK, (j + 1) * share * CHUNK)
        gmid_ref[:, cols] = b2_ref[:, cols].astype(F32) * s2_ref[:, cols] + nt(
            dcomb_ref[...], w_u.wide(cols_of, j * share, (j + 1) * share)
        )
    need(mid_ref)
    d_mid, d_gain, d_bias = norm_back(mid_ref[...], par_ref[layer, 1:2], gmid_ref[...])
    sums_ref[0:1, :] = d_gain
    sums_ref[1:2, :] = d_bias
    sums_ref[3:8, :] = jnp.zeros((5, model), F32)
    g_mid = g_ref[...] + d_mid
    gmid_ref[...] = g_mid
    b1_ref[...] = g_mid.astype(BF16)
    for mx in every:
        m = jnp.bitwise_xor(me_m, mx)
        o_scr[...] = nn(b1_ref[...], w_d.block(m, 1)).astype(BF16)
        for r in range(batch):
            o_refs[mx][r] = o_scr[rows_at(me_ref, r, part), :]


def second_back(me, g, mid, n2, s2, slope, par, wd, wu, layer, mp_size, chunks, batch, after=()):
    rows, model = g.shape
    ff = slope.shape[1]
    out = [
        sds((rows, model), BF16),
        sds((rows, ff + LANE * mp_size), BF16),
        sds((rows, model), F32),
        sds((rows, model), BF16),
        sds((8, model), F32),
    ]
    out += [sds((batch, rows // batch, LANE), BF16)] * 2
    out += [sds((2, batch, rows // batch, LANE), BF16)]
    return call(
        functools.partial(second_back_body, wd, wu, layer, mp_size, chunks, batch),
        "second_back",
        out,
        [me, g, Late(mid), Late(n2), Late(s2), Late(slope), par],
        smem=1,
        parts=wd.arrays,
        scratch=[
            pltpu.VMEM((rows, LANE), BF16),
            pltpu.VMEM((chunks * mp_size, wd.rows, LANE), BF16),
            pltpu.VMEM((chunks * mp_size, wu.rows, LANE), BF16),
            pltpu.SemaphoreType.DMA,
            pltpu.SemaphoreType.DMA,
        ],
        after=after,
    )


def attend_back_body(wq, row, mp_size, chunks, last, me_ref, seg_ref, segc_ref, segr_ref, *refs):
    qkv_ref, lse_ref = refs[:2]
    d_in, refs = refs[2 : 2 + mp_size], refs[2 + mp_size :]
    d_in = [d_in[0].at[row], d_in[1].at[row], d_in[2].at[0, row], d_in[3].at[1, row]]
    n_refs, refs = refs[:mp_size], refs[mp_size:]
    if last:
        before_ref, refs = refs[0], refs[1:]
    w_refs, refs = refs[: len(wq.arrays)], refs[len(wq.arrays) :]
    keep_ref, send_ref, dw_ref = refs[:3]
    w_scr, do_scr, dqkv_scr, dk_scr, dv_scr, sem = refs[3:]
    w = wq.open(w_refs, me_ref, w_scr, sem, chunks, own_only=True)
    length = qkv_ref.shape[0]
    part = d_in[0].shape[0]
    me_m, me_d = me_ref[0], me_ref[1]
    for mx in range(mp_size):
        at = pl.multiple_of(jnp.bitwise_xor(me_m, mx) * part, part)
        do_scr[pl.ds(at, part), :] = d_in[mx][...]
    dqkv_scr[...] = jnp.zeros_like(dqkv_scr)
    dk_scr[...] = jnp.zeros_like(dk_scr)
    dv_scr[...] = jnp.zeros_like(dv_scr)
    q_spans = length // SPAN
    need(qkv_ref, lse_ref)

    def step(q_at, carry):
        low = seg_bounds(seg_ref, q_at, q_spans)
        real = seg_ref[q_at * SPAN] >= 0
        q0 = pl.multiple_of(q_at * SPAN, SPAN)
        k0 = pl.multiple_of(low * SPAN, SPAN)
        for spans in range(1, q_spans + 1):

            @pl.when(real & (q_at - low + 1 == spans))
            def _():
                keys = spans * SPAN
                mask = allowed_t(segc_ref, segr_ref, k0, q0, spans)
                dqs, dks, dvs = [], [], []
                for h in range(2):
                    lo = h * HEAD_DIM
                    q = qkv_ref[pl.ds(q0, SPAN), lo : lo + HEAD_DIM] * jnp.asarray(
                        HEAD_DIM**-0.5, BF16
                    )
                    k = qkv_ref[pl.ds(k0, keys), 128 + lo : 128 + lo + HEAD_DIM]
                    v = qkv_ref[pl.ds(k0, keys), 256 + lo : 256 + lo + HEAD_DIM]
                    do = do_scr[pl.ds(q0, SPAN), lo : lo + HEAD_DIM]
                    lse = lse_ref[h, :, pl.ds(q0, SPAN)]
                    p = jnp.where(mask, jnp.exp(nt(k, q) - lse), 0.0)
                    dvs.append(nn(p.astype(BF16), do))
                    dp = nt(v, do)
                    delta = jnp.sum(p * dp, axis=0, keepdims=True)
                    ds = (p * (dp - delta)).astype(BF16)
                    dks.append(nn(ds, q))
                    dqs.append(tn(k, ds))
                dqkv_scr[pl.ds(q0, SPAN), 0:128] = (
                    jnp.concatenate(dqs, axis=0).T * HEAD_DIM**-0.5
                ).astype(BF16)
                dk_scr[pl.ds(k0, keys), :] += jnp.concatenate(dks, axis=1)
                dv_scr[pl.ds(k0, keys), :] += jnp.concatenate(dvs, axis=1)

        return carry

    lax.fori_loop(0, q_spans, step, 0)
    dqkv_scr[:, 128:256] = dk_scr[...].astype(BF16)
    dqkv_scr[:, 256:384] = dv_scr[...].astype(BF16)
    w.wait()
    weights = w.wide([(0, 0), (0, 1), (0, 2)])
    need(*n_refs)
    grad = jnp.zeros((n_refs[0].shape[1], 384), F32)
    if last:
        grad = before_ref[...]
    for mx in range(mp_size):
        at = pl.multiple_of(jnp.bitwise_xor(me_m, mx) * part, part)
        d_here = dqkv_scr[pl.ds(at, part), :]
        d_n = nt(d_here, weights).astype(BF16)
        (send_ref if mx % 2 else keep_ref)[mx // 2] = d_n
        grad += tn(n_refs[mx][...], d_here)
    if not last:
        dw_ref[...] = grad
        return
    grad = grad.astype(BF16)
    for d in range(chunks):
        for b in range(3):
            dw_ref[jnp.bitwise_xor(d, me_d), b * CHUNK : (b + 1) * CHUNK, :] = grad[
                d * CHUNK : (d + 1) * CHUNK, b * LANE : (b + 1) * LANE
            ]


def attend_back(
    me, seg, segc, segr, qkv, lse, d_parts, n_parts, wq, row, chunks, before=None, after=()
):
    mp_size = len(d_parts)
    length = seg.shape[0]
    part, model = n_parts[0].shape
    last = before is not None
    out = [sds((mp_size // 2, part, model), BF16)] * 2
    out += [sds((chunks, 3 * CHUNK, LANE), BF16) if last else sds((model, 384), F32)]
    return call(
        functools.partial(attend_back_body, wq, row, mp_size, chunks, last),
        "attend_back",
        out,
        [me, seg, segc, segr, Late(qkv), Late(lse)]
        + d_parts
        + [Late(n) for n in n_parts]
        + ([before] if last else []),
        smem=2,
        parts=wq.arrays,
        scratch=[
            pltpu.VMEM((chunks, wq.rows, LANE), BF16),
            pltpu.VMEM((length, LANE), BF16),
            pltpu.VMEM((length, 384), BF16),
            pltpu.VMEM((length, LANE), F32),
            pltpu.VMEM((length, LANE), F32),
            pltpu.SemaphoreType.DMA,
        ],
        after=after,
    )


def first_back_body(
    layer, batch, me_ref, x_ref, gmid_ref, local_ref, par_ref, sums2_ref, sums1_ref, *refs
):
    kept, got = refs[:batch], refs[batch : 2 * batch]
    g_ref, sums_ref = refs[2 * batch :]
    part = kept[0].shape[0]
    for r in range(batch):
        at = rows_at(me_ref, r, part)
        g_ref[at, :] = local_ref[at, :] + kept[r][...].astype(F32) + got[r][...].astype(F32)
    need(x_ref)
    d_x, d_gain, d_bias = norm_back(x_ref[...].astype(F32), par_ref[layer, 0:1], g_ref[...])
    g_ref[...] = gmid_ref[...] + d_x
    sums_ref[0:1, :] = d_gain
    sums_ref[1:2, :] = sums2_ref[0:1, :]
    sums_ref[2:3, :] = d_bias
    sums_ref[3:4, :] = sums1_ref[0:1, :]
    sums_ref[4:5, :] = sums2_ref[1:2, :]
    sums_ref[5:6, :] = sums2_ref[2:3, :]
    sums_ref[6:8, :] = sums2_ref[6:8, :]


def first_back(me, x, gmid, local, par, sums2, sums1, kept, got, layer, after=()):
    rows, model = x.shape
    return call(
        functools.partial(first_back_body, layer, len(kept)),
        "first_back",
        [sds((rows, model), F32), sds((8, model), F32)],
        [me, Late(x), gmid, local, par, sums2, sums1] + kept + got,
        smem=1,
        after=after,
    )


def put_blocks(outs, mx, me_d, chunks, at_block, res, mp_first=False):
    half = chunks // 2
    for d in range(chunks):
        at = jnp.bitwise_xor(d, me_d)
        if mp_first:
            at = (mx // 2) * chunks + at
        else:
            at = (at // half) * chunks + (mx // 2) * half + at % half
        for b in range(res.shape[1] // LANE):
            rows = slice((at_block + b) * CHUNK, (at_block + b + 1) * CHUNK)
            outs[mx % 2][at, rows, :] = res[d * CHUNK : (d + 1) * CHUNK, b * LANE : (b + 1) * LANE]


def weight_grad_body(
    wd, mp_size, chunks, batch, mp_first, me_ref, n2_ref, dcomb_ref, b1_ref, b2_ref, att_ref,
    act_ref, s1_ref, *refs
):
    n_refs, refs = refs[:batch], refs[batch:]
    d_refs, refs = refs[: len(wd.arrays)], refs[len(wd.arrays) :]
    ups, downs, (local_ref, sums_ref), refs = refs[:2], refs[2:4], refs[4:6], refs[6:]
    w_scr, left, n_left, b1_left, z_scr, sem = refs
    w = wd.open(d_refs, me_ref, w_scr, sem, chunks)
    me_m, me_d = me_ref[0], me_ref[1]
    every = range(mp_size)
    need(n2_ref)
    left[...] = n2_ref[...].T
    stride = dcomb_ref.shape[1] // mp_size
    for mx in every:
        m = jnp.bitwise_xor(me_m, mx)
        res = nn(left[...], dcomb_ref[:, pl.ds(col(m * stride), stride)])
        put_blocks(ups, mx, me_d, chunks, 0, res.astype(BF16), mp_first)
    need(s1_ref, *n_refs)
    for r in range(batch):
        z_scr[rows_at(me_ref, r, n_refs[r].shape[0]), :] = n_refs[r][...]
    n = z_scr[...]
    n_left[...] = n.T
    b1f = b1_ref[...].astype(F32)
    s1 = s1_ref[...]
    d_z1 = (b1f * n.astype(F32) * s1 * (1.0 - s1)).astype(BF16)
    z_scr[...] = d_z1
    sums_ref[0:1, :] = jnp.sum(d_z1.astype(F32), axis=0, keepdims=True)
    sums_ref[1:8, :] = jnp.zeros((7, sums_ref.shape[1]), F32)
    b1_left[...] = b1_ref[...].T
    left[...] = b2_ref[...].T
    w.wait()
    local_ref[...] = b1f * s1 + nt(d_z1, w.wide([(m, 0) for m in every]))
    need(att_ref, act_ref)
    ff_m = act_ref.shape[1] // mp_size
    for mx in every:
        m = jnp.bitwise_xor(me_m, mx)
        cols = pl.ds(col(m * LANE), LANE)
        put_blocks(downs, mx, me_d, chunks, 0, nn(n_left[...], z_scr[:, cols]).astype(BF16))
        put_blocks(downs, mx, me_d, chunks, 1, nn(b1_left[...], att_ref[:, cols]).astype(BF16))
        res = nn(left[...], act_ref[:, pl.ds(col(m * ff_m), ff_m)])
        put_blocks(downs, mx, me_d, chunks, 2, res.astype(BF16))


def weight_grad(
    me, n2, dcomb, b1, b2, att, act, s1, n_rows, wd, mp_size, chunks, mp_first, after=()
):
    rows, model = b1.shape
    gates = Parts(wd.arrays, wd.order, wd.first_row, CHUNK)
    height = dcomb.shape[1] // mp_size // LANE * CHUNK
    return call(
        functools.partial(weight_grad_body, gates, mp_size, chunks, len(n_rows), mp_first),
        "weight_grad",
        [sds((mp_size // 2 * chunks, height, LANE), BF16)] * 2
        + [sds((mp_size // 2 * chunks, wd.rows, LANE), BF16)] * 2
        + [sds((rows, model), F32), sds((8, model), F32)],
        [me, Late(n2), dcomb, b1, b2, Late(att), Late(act), Late(s1)]
        + [Late(n) for n in n_rows],
        smem=1,
        parts=wd.arrays,
        scratch=[pltpu.VMEM((chunks * mp_size, CHUNK, LANE), BF16)]
        + [pltpu.VMEM((model, rows), BF16)] * 3
        + [pltpu.VMEM((rows, model), BF16), pltpu.SemaphoreType.DMA],
        after=after,
    )


def swap(value, axis, size, bits):
    return lax.ppermute(value, axis, [(i, i ^ bits) for i in range(size)])


def add_body(count, *refs):
    left, right = refs[:2]
    outs = refs[2:]
    size = outs[0].shape[0]

    def step(i, carry):
        for part, out in enumerate(outs):
            at = part * size + i
            out[i] = (left[at].astype(F32) + right[at].astype(F32)).astype(BF16)
        return carry

    lax.fori_loop(0, size, step, 0)


def add(left, right, count):
    shape = (left.shape[0] // count,) + left.shape[1:]
    return call(
        functools.partial(add_body, count),
        "add",
        [sds(shape, BF16)] * count,
        [left, right],
    )


def join_body(count, has_sums, me_ref, *refs):
    pairs = [(refs[2 * i], refs[2 * i + 1]) for i in range(count)]
    refs = refs[2 * count :]
    if has_sums:
        sums_ref, refs = refs[0], refs[1:]
    for k, out in enumerate(refs):
        at = 0
        for left, right in pairs:
            rows = left.shape[1]
            out[at : at + rows, :] = (left[k].astype(F32) + right[k].astype(F32)).astype(BF16)
            at += rows
        if has_sums:
            tile = jnp.bitwise_xor(me_ref[1], k) // (LANE // CHUNK)
            out[at:, :] = sums_ref[:, pl.ds(col(tile * LANE), LANE)].astype(BF16)


def join(me, pairs, sums=None):
    width = 4
    rows = sum(p[0].shape[1] for p in pairs) + (0 if sums is None else sums.shape[0])
    flat = [a for pair in pairs for a in pair]
    return call(
        functools.partial(join_body, len(pairs), sums is not None),
        "add",
        [sds((rows, LANE), BF16)] * width,
        [me] + flat + ([] if sums is None else [sums]),
        smem=1,
    )


def total_body(*refs):
    value = refs[0][...].astype(F32)
    for ref in refs[1:-1]:
        value += ref[...].astype(F32)
    refs[-1][...] = value


def total(parts):
    return call(total_body, "add", [sds(parts[0].shape, F32)], parts)[0]


def stack_body(cuts, *refs):
    ins, outs = refs[: -len(cuts)], refs[-len(cuts) :]
    for i, ref in enumerate(ins):
        at = 0
        for out, rows in zip(outs, cuts):
            out[i] = ref[at : at + rows, :]
            at += rows


def stack(arrays, cuts=None, after=()):
    cuts = cuts or [arrays[0].shape[0]]
    return call(
        functools.partial(stack_body, cuts),
        "stack",
        [sds((len(arrays), rows, LANE), BF16) for rows in cuts],
        arrays,
        after=after,
    )


def copy_body(a_ref, b_ref):
    b_ref[...] = a_ref[...]


def copied(array):
    return call(copy_body, "stack", [sds(array.shape, array.dtype)], [array])[0]


def relay_body(*refs):
    pass


def relay(arrays):
    call(relay_body, "stack", [], [], after=arrays)


def pack_q_body(per, me_ref, qkv_ref, par_ref, out_ref):
    for c in range(3):
        out_ref[c * per : (c + 1) * per, :] = qkv_ref[c]
    rows = jnp.concatenate([par_ref[...].astype(F32)] * (LANE // per), axis=1)
    share = lax.broadcasted_iota(jnp.int32, rows.shape, 1) // per
    mine = jnp.where(share == me_ref[1] % (LANE // per), rows, 0.0)
    out_ref[3 * per :, :] = mine.astype(BF16)


def pack_q(me, qkv, params):
    per = qkv.shape[1]
    return call(
        functools.partial(pack_q_body, per),
        "pack",
        [sds((3 * per + params.shape[0], LANE), BF16)],
        [me, qkv, params],
        smem=1,
    )[0]


def pack_body(layer, with_q, qkv_ref, gate_ref, out_ref, up_ref, down_ref, shard_ref):
    per = gate_ref.shape[2]
    at = 0
    if with_q:
        for c in range(3):
            shard_ref[at : at + per, :] = qkv_ref[layer, c]
            at += per
    refs = (gate_ref.at[layer, 0], out_ref.at[layer], down_ref.at[layer])
    for ref in refs + (gate_ref.at[layer, 1], up_ref.at[layer]):
        for b in range(ref.shape[1] // LANE):
            shard_ref[at : at + per, :] = ref[:, b * LANE : (b + 1) * LANE]
            at += per


def pack(layer, with_q, w_qkv, w_gate, w_out, w_up, w_down):
    per = w_gate.shape[2]
    cols = 2 * w_gate.shape[3] + w_out.shape[2] + w_up.shape[2] + w_down.shape[2]
    rows = (cols // LANE + 3 * with_q) * per
    return call(
        functools.partial(pack_body, layer, with_q),
        "pack",
        [sds((rows, LANE), BF16)],
        [w_qkv, w_gate, w_out, w_up, w_down],
    )[0]


def finish_body(counts, names, me_ref, *refs):
    ins, outs = refs[: sum(counts)], refs[sum(counts) :]
    d_qkv, d_out, d_gate, d_up, d_down, d_par = outs
    per = CHUNK
    at = 0
    for count, pieces in zip(counts, names):
        value = ins[at][...].astype(F32)
        for ref in ins[at + 1 : at + count]:
            value += ref[...].astype(F32)
        at += count
        row = 0
        for name, l in pieces:
            if name == "p":
                low, high = value[row:, :CHUNK], value[row:, CHUNK:]
                d_par[...] = jnp.where(me_ref[1] % 2 == 0, low, high)
                continue
            blocks = {"q": 3, "u": 1 + d_up.shape[2] // LANE, "d": 2 + d_down.shape[2] // LANE}
            for b in range(blocks[name]):
                block = value[row : row + per]
                row += per
                if name == "q":
                    d_qkv[l, b] = block
                elif name == "u" and b == 0:
                    d_gate[l, 1] = block
                elif name == "u":
                    d_up[l, :, (b - 1) * LANE : b * LANE] = block
                elif b == 0:
                    d_gate[l, 0] = block
                elif b == 1:
                    d_out[l] = block
                else:
                    d_down[l, :, (b - 2) * LANE : (b - 1) * LANE] = block


def finish(me, layers, ff_m, groups):
    shapes = [(3, CHUNK, LANE), (CHUNK, LANE), (2, CHUNK, LANE), (CHUNK, ff_m), (CHUNK, ff_m)]
    out = [sds((layers,) + shape, F32) for shape in shapes] + [sds((layers * 8, CHUNK), F32)]
    return call(
        functools.partial(finish_body, [len(g[0]) for g in groups], [g[1] for g in groups]),
        "finish",
        out,
        [me] + [a for g in groups for a in g[0]],
        smem=1,
    )


def solution(mesh):
    dp_size, mp_size, width_size = (mesh.shape[a] for a in ("dp", "mp", "width"))
    all_axes = ("mp", "dp", "width")
    direct = (dp_size, mp_size, width_size) == (2, 4, 4)

    def mp_swap(value, bits):
        return swap(value, "mp", mp_size, bits)

    def dp_swap(value):
        return swap(value, "dp", dp_size, 1)

    def spread(value):
        return [value, mp_swap(value, 1), mp_swap(value, 2)]

    def spread_last(values):
        return values + [mp_swap(values[2], 1)]

    def exchange(own, near, far):
        far = mp_swap(far, 2)
        return [own, mp_swap(near, 1), far, mp_swap(far, 1)]

    def send_width(value):
        return [value] + [swap(value, "width", width_size, k) for k in range(1, width_size)]

    def swap_width(values):
        return [values[0]] + [
            swap(values[k], "width", width_size, k) for k in range(1, width_size)
        ]

    def on_device(
        tokens, segments, cotangent, norm_gains, biases, w_qkv, w_out, w_gate, w_up, w_down
    ):
        ORDER.token = None
        batch, part, model = tokens.shape
        layers = w_qkv.shape[0]
        per = w_qkv.shape[1]
        chunks = model // CHUNK
        half = chunks // 2
        ff_m = w_up.shape[2]
        ff_blocks = ff_m // LANE
        ff = ff_m * mp_size
        me_m = lax.axis_index("mp")
        me_d = lax.axis_index("dp") * width_size + lax.axis_index("width")
        rows = [jnp.where(segments[0, -1] < 0, 0, batch - 1)]
        rows += [batch - 1 - rows[0]] if batch == 2 else []
        me = jnp.stack([me_m, me_d] + rows).astype(jnp.int32)
        me_pack, me_att = me, me
        if not direct:
            me_pack = jnp.stack([0 * me_m, 0 * me_d] + rows).astype(jnp.int32)
            me_att = jnp.stack([me_m, 0 * me_d] + rows).astype(jnp.int32)

        def blocks_of(matrix):
            return jnp.swapaxes(matrix.reshape(per, -1, LANE), 0, 1).reshape(-1, LANE)

        qkv_t, out_t, down_t = (jnp.swapaxes(w, 1, 2) for w in (w_qkv, w_out, w_down))
        params = jnp.concatenate([norm_gains, biases], axis=1)
        params = jnp.pad(params, ((0, 0), (0, 2), (0, 0))).reshape(layers * 8, per)

        def param_block():
            rows = jnp.concatenate([params] * (LANE // per), axis=1)
            share = lax.broadcasted_iota(jnp.int32, rows.shape, 1) // per
            return jnp.where(share == me_d % (LANE // per), rows, 0)

        q_rows, d_rows, u_rows = 3 * CHUNK, (2 + ff_blocks) * CHUNK, (1 + ff_blocks) * CHUNK

        def shard(l, q):
            mats = [w_gate[l, 0], out_t[l], blocks_of(down_t[l]), w_gate[l, 1], blocks_of(w_up[l])]
            return jnp.concatenate(([qkv_t[l].reshape(-1, LANE)] if q else []) + mats, axis=0)

        def gather_whole(shard, extra):
            full = lax.all_gather(shard, all_axes, axis=0, tiled=False)
            if per == CHUNK:
                return full
            count = (shard.shape[0] - extra) // per
            full = full.reshape(mp_size, chunks, CHUNK // per, shard.shape[0], LANE)
            mats = full[:, :, :, : count * per]
            mats = mats.reshape(mp_size, chunks, CHUNK // per, count, per, LANE)
            mats = jnp.swapaxes(mats, 2, 3).reshape(mp_size * chunks, count * CHUNK, LANE)
            if not extra:
                return mats
            pars = jnp.sum(full[:, :, :, count * per :].astype(F32), axis=2).astype(BF16)
            return jnp.concatenate([mats, pars.reshape(mp_size * chunks, extra, LANE)], axis=1)

        def reduce_whole(even, odd):
            full = jnp.stack([even, odd], axis=1)
            full = full.reshape(2, mp_size // 2, half, 2, -1, CHUNK // per, per, LANE)
            full = jnp.transpose(full, (1, 3, 0, 2, 5, 4, 6, 7)).reshape(-1, LANE).astype(F32)
            return lax.psum_scatter(full, all_axes, scatter_dimension=0, tiled=True)

        def reduce_q_whole(grad):
            full = grad.reshape(chunks, -1, CHUNK // per, per, LANE)
            full = jnp.swapaxes(full, 1, 2).reshape(-1, LANE).astype(F32)
            return lax.psum_scatter(full, ("dp", "width"), scatter_dimension=0, tiled=True)

        segc = jnp.broadcast_to(segments[:, :, None], segments.shape + (LANE,))
        segs = []
        for row in rows:
            seg, seg_cols = (
                lax.dynamic_index_in_dim(a, row, 0, keepdims=False) for a in (segments, segc)
            )
            segs.append((seg, seg_cols, seg[None]))

        q_all = q_rows + layers * 8
        weights = [None] * layers
        if direct:
            mats = (qkv_t, w_gate, out_t, w_up, down_t)
            q_steps = send_width(pack_q(me, qkv_t[0], params))
            t_all = spread(tokens)
            w_steps = send_width(pack(0, False, *mats))
            (q_base,) = stack(q_steps)
            wq = Parts([q_base, dp_swap(q_base)], [(0, 0), (0, 4)], 0, q_all)
            t_all = t_all + [mp_swap(copied(t_all[2]), 1)]
        else:
            t_all = spread_last(spread(tokens))
            q_sh = jnp.concatenate([qkv_t[0].reshape(-1, LANE), param_block()], axis=0)
            wq = Parts([gather_whole(q_sh, layers * 8)], None, 0, q_all)
            full = gather_whole(shard(0, False), 0)
            wd, wu = Parts([full], None, 0, d_rows), Parts([full], None, d_rows, u_rows)
            for l in range(1, layers):
                full = gather_whole(shard(l, True), 0)
                weights[l] = (
                    Parts([full], None, 0, q_rows),
                    Parts([full], None, q_rows, d_rows),
                    Parts([full], None, q_rows + d_rows, u_rows),
                )

        def two_pieces(got):
            for m, d in list(got):
                last = got[m, d]
                if (m, d) == (2, 4):
                    last = copied(last)
                got[m + 1, d] = mp_swap(last, 1)
            arrays, order = list(got.values()), list(got)
            return Parts(arrays, order, 0, d_rows), Parts(arrays, order, d_rows, u_rows)

        x = tokens.reshape(batch * part, model)
        par = None
        saved = []
        t_parts = [t_all] * batch
        for l in range(layers):
            if l and direct:
                wq = wq_next
            elif l:
                wq, wd, wu = weights[l]
            n_parts, o_parts, kept = [], [], []
            for r in range(batch):
                qkv, lse, own, near, far, *rest = attend(
                    me, *segs[r], t_parts[r], wq, l, r, layers, l == 0, chunks
                )
                if l == 0:
                    par = rest[0]
                    n_parts.append(rest[1:])
                else:
                    n_parts.append(t_parts[r])
                kept.append((qkv, lse))
                o_parts += exchange(own, near, far)
                if direct and l == 0 and r == 0:
                    (base,) = stack(w_steps)
                    got = {(0, 0): base, (0, 4): dp_swap(base), (2, 0): mp_swap(base, 2)}
                    later = send_width(pack(1, True, *mats))
            if direct:
                if l == 0:
                    relay(later[1:] + [got[0, 4], got[2, 0]])
                    got[2, 4] = dp_swap(copied(got[2, 0]))
                else:
                    got[2, 4] = dp_swap(got[2, 0])
                wd, wu = two_pieces(got)
                if l == 0:
                    q_base, base = stack(later, [q_rows, d_rows + u_rows])
                    wq_next = Parts([q_base, dp_swap(q_base)], [(0, 0), (0, 4)], 0, q_rows)
                    got = {(0, 0): base, (0, 4): dp_swap(base), (2, 0): mp_swap(base, 2)}
                else:
                    wq = wq_next
                weights[l] = (wq, wd, wu)
            elif l == 0:
                weights[0] = (wq, wd, wu)
            n_rows = [n_parts[r][0] for r in range(batch)]
            att, s1, mid, n2, s2, act, slope, out, *following = second(
                me, x, par, n_rows, o_parts, wd, wu, l, chunks, ff, l + 1 < layers
            )
            saved.append((x, n_parts, kept, att, s1, mid, n2, s2, act, slope))
            x = out
            if following:
                t_parts = [spread(n) for n in following]
                if direct:
                    relay([got[0, 4], got[2, 0], wq_next.arrays[1]] + [t[2] for t in t_parts])
                t_parts = [spread_last(t) for t in t_parts]
        output = x.reshape(batch, part, model)

        own = lax.dynamic_slice_in_dim(segments, me_m * part, part, 1)
        g = cotangent.astype(F32) * (own >= 0).astype(F32)[:, :, None]
        g = g.reshape(batch * part, model)
        reduced = [None] * layers
        all_sums = [None] * layers
        moving = {}

        def reduce_2(name, mp_first=False):
            if name in moving:
                keep, send = add(*moving[name], 2)
                moving[name] = (keep, mp_swap(send, 2) if mp_first else dp_swap(send))

        def reduce_3(name, mp_first=False):
            if name in moving:
                keep, send = add(*moving[name], 2)
                moving[name] = (keep, dp_swap(send) if mp_first else mp_swap(send, 2))

        def reduce_4(names, sums=None):
            if direct:
                pairs = [moving.pop(name) for name in names]
                moving[names[0]] = swap_width(join(me, pairs, sums))

        def reduce_5(name):
            return total(moving.pop(name)) if direct else None

        for l in reversed(range(layers)):
            wq, wd, wu = weights[l]
            x, n_parts, kept, att, s1, mid, n2, s2, act, slope = saved[l]
            n_rows = [n_parts[r][0] for r in range(batch)]
            final, first_of_two = l == 0, l + 1 < layers
            b2, dcomb, gmid, b1, sums2, *o_parts = second_back(
                me, g, mid, n2, s2, slope, par, wd, wu, l, mp_size, chunks, batch
            )
            d_parts = exchange(*o_parts)
            if first_of_two:
                reduce_4([("q", l + 1), ("u", l + 1)])
            reduce_3(("d", l + 1))
            *grads, local, sums1 = weight_grad(
                me_pack, n2, dcomb, b1, b2, att, act, s1, n_rows, wd, mp_size, chunks,
                final and direct,
            )
            relay([d_parts[2]])
            if direct:
                moving["u", l] = (grads[0], mp_swap(grads[1], 1))
                moving["d", l] = (grads[2], mp_swap(grads[3], 1))
            keeps, gots = [], []
            q_grad = None
            for r in range(batch):
                keep, send, q_grad = attend_back(
                    me_att, *segs[r], *kept[r], d_parts, n_parts[r], wq, r, chunks, q_grad
                )
                if r == 0:
                    reduce_2(("d", l))
                    reduce_2(("u", l), final)
                    if first_of_two:
                        moving["q", l + 1] = [reduce_5(("q", l + 1))] if direct else None
                        reduce_4([("d", l + 1)])
                else:
                    reduce_3(("u", l), final)
                    if final:
                        reduce_3(("d", l))
                keep, send = add(keep, mp_swap(send, 1), 2)
                keeps.append(keep.reshape(keep.shape[1:]))
                gots.append(mp_swap(send, 2).reshape(keep.shape[1:]))
            if direct and first_of_two:
                moving["d", l + 1] = [reduce_5(("d", l + 1))]
            if direct:
                moving["q", l] = (q_grad[:half], dp_swap(q_grad[half:]))
                if final:
                    reduce_4([("u", l)])
                    reduce_4([("q", l), ("d", l)])
            g, all_sums[l] = first_back(me, x, gmid, local, par, sums2, sums1, keeps, gots, l)
            if not direct:
                reduced[l] = (reduce_q_whole(q_grad), reduce_whole(*grads[:2]), reduce_whole(*grads[2:]))
        d_tokens = g.reshape(batch, part, model)
        sums = jnp.concatenate(all_sums, axis=0)
        if direct:
            sums = sums + mp_swap(sums, 1)
            sums = sums + mp_swap(sums, 2)
            sums = sums + dp_swap(sums)
            moving["p", 0] = swap_width(join(me, [], sums))
            groups = [
                (moving["q", 1], [("q", 1), ("u", 1)]),
                (moving["d", 1], [("d", 1)]),
                (moving["u", 0], [("u", 0)]),
                (moving["q", 0], [("q", 0), ("d", 0)]),
                (moving["p", 0], [("p", 0)]),
            ]
            *stacked, params = finish(me, layers, ff_m, groups)
        else:
            params = lax.dynamic_slice_in_dim(lax.psum(sums, all_axes), me_d * per, per, 1)
        params = params.reshape(layers, 8, per)

        def unblocks(rows, count):
            return jnp.swapaxes(rows.reshape(count, per, LANE), 0, 1).reshape(per, count * LANE)

        if not direct:
            grads = []
            for q_sum, up_sum, down_sum in reduced:
                grads.append(
                    (
                        q_sum.reshape(3, per, LANE),
                        down_sum[per : 2 * per],
                        jnp.stack([down_sum[:per], up_sum[:per]]),
                        unblocks(up_sum[per:], ff_blocks),
                        unblocks(down_sum[2 * per :], ff_blocks),
                    )
                )
            stacked = [jnp.stack([grads[l][i] for l in range(layers)]) for i in range(5)]
        for i in (0, 1, 4):
            stacked[i] = jnp.swapaxes(stacked[i], 1, 2)
        return (
            output,
            d_tokens,
            params[:, 0:2],
            params[:, 2:6:2],
            params[:, 3:6:2],
            *stacked,
        )

    placed = (
        P(("dp", "width"), "mp", None),
        P(("dp", "width"), None),
        P(("dp", "width"), "mp", None),
        P(None, None, ("dp", "width")),
        P(None, None, ("dp", "width")),
        P(None, ("dp", "width"), None, "mp"),
        P(None, "mp", ("dp", "width")),
        P(None, None, ("dp", "width"), "mp"),
        P(None, ("dp", "width"), "mp"),
        P(None, "mp", ("dp", "width")),
    )
    return jax.shard_map(
        on_device,
        mesh=mesh,
        in_specs=placed,
        out_specs=(
            placed[0],
            placed[0],
            placed[3],
            placed[3],
            placed[3],
            placed[5],
            placed[6],
            placed[7],
            placed[8],
            placed[9],
        ),
        check_vma=False,
    )
```

```python
import functools

import jax
import jax.numpy as jnp
from jax import lax
from jax.experimental import pallas as pl
from jax.experimental.pallas import tpu as pltpu
from jax.sharding import PartitionSpec as P

HEAD_DIM = 64
LANE = 128
NORM_EPS = 1e-05
SPAN = 256
CHUNK = 64

VALUES_MB = {
    "attend": 6,
    "second": 10,
    "second_back": 10,
    "attend_back": 8,
    "first_back": 6,
    "weight_grad": 8,
    "relay": 1,
    "stack": 2,
    "add": 2,
    "pack": 2,
    "finish": 4,
}

KERNEL_US = {
    "attend": 8,
    "second": 12,
    "second_back": 10,
    "attend_back": 9,
    "first_back": 4,
    "weight_grad": 8,
    "relay": 1,
    "stack": 0.1,
    "add": 1,
    "pack": 10,
    "finish": 2,
}

F32 = jnp.float32
BF16 = jnp.bfloat16


def nn(a, b):
    return jnp.dot(a, b, preferred_element_type=F32)


def nt(a, b):
    return lax.dot_general(a, b, (((1,), (1,)), ((), ())), preferred_element_type=F32)


def tn(a, b):
    return lax.dot_general(a, b, (((0,), (0,)), ((), ())), preferred_element_type=F32)


def sds(shape, dtype):
    return jax.ShapeDtypeStruct(shape, dtype)


class Late:
    def __init__(self, array):
        self.array = array


class Copies:
    def __init__(self, pairs, first_out, sems):
        self.first_out = first_out
        self.all = [
            (ref, pltpu.make_async_copy(*pair, sems.at[i]))
            for i, (ref, *pair) in enumerate(pairs)
        ]
        self.waiting = []
        self.unsent = list(self.all[first_out:])
        for ref, copy in self.all[:first_out]:
            copy.start()
            self.waiting.append((ref, copy))

    def need(self, *refs):
        for ref in refs:
            for i, entry in enumerate(self.waiting):
                if entry[0] is ref:
                    entry[1].wait()
                    del self.waiting[i]
                    break

    def send(self, *refs):
        for ref in refs:
            for i, entry in enumerate(self.unsent):
                if entry[0] is ref:
                    entry[1].start()
                    del self.unsent[i]
                    break

    def finish(self):
        for _, copy in self.waiting:
            copy.wait()
        for _, copy in self.unsent:
            copy.start()
        for _, copy in self.all[self.first_out :]:
            copy.wait()


class Chain:
    def __init__(self):
        self.token = None
        self.copies = None


ORDER = Chain()


def need(*refs):
    ORDER.copies.need(*refs)


def send(*refs):
    ORDER.copies.send(*refs)


def in_hbm(a):
    return pltpu.with_memory_space_constraint(a, pltpu.HBM)


def size_of(a):
    return a.size * a.dtype.itemsize


def call(body, name, out_shape, args, smem=0, parts=(), scratch=(), after=()):
    after = list(after) + ([] if ORDER.token is None else [ORDER.token])
    late_in = [i for i, a in enumerate(args) if isinstance(a, Late)]
    late_out = [i for i, o in enumerate(out_shape) if isinstance(o, Late)]
    args = [in_hbm(a.array) if isinstance(a, Late) else a for a in args]
    out_shape = [o.array if isinstance(o, Late) else o for o in out_shape]
    parts = [in_hbm(a) for a in parts]
    hbm, vmem = (pl.BlockSpec(memory_space=space) for space in (pltpu.HBM, pltpu.VMEM))
    specs = [pl.BlockSpec(memory_space=pltpu.SMEM)] * smem
    specs += [hbm if i in late_in else vmem for i in range(smem, len(args))]
    specs += [hbm] * len(parts)
    specs += [pl.BlockSpec(memory_space=pl.ANY)] * len(after)
    used = len(args) + len(parts)
    given = used + len(after)
    outs = len(out_shape)
    late = [args[i] for i in late_in] + [out_shape[i] for i in late_out]
    room = [pltpu.VMEM(a.shape, a.dtype) for a in late]
    sems = [pltpu.SemaphoreType.DMA((len(late),))] if late else []

    def inner(*refs):
        ins, results = list(refs[:used]), list(refs[given : given + outs])
        rest = refs[given + outs + 1 :]
        own = rest[: len(scratch)]
        places = rest[len(scratch) : len(scratch) + len(late)]
        pairs = []
        for i, place in zip(late_in, places):
            pairs.append((place, ins[i], place))
            ins[i] = place
        for i, place in zip(late_out, places[len(late_in) :]):
            pairs.append((place, place, results[i]))
            results[i] = place
        copies = ORDER.copies = Copies(pairs, len(late_in), rest[-1] if late else None)
        body(*ins, *results, *own)
        copies.finish()

    nbytes = sum(size_of(a) for a in args + out_shape)
    for s in scratch:
        if hasattr(s, "shape") and len(s.shape) > 1:
            nbytes += size_of(jax.ShapeDtypeStruct(s.shape, s.dtype))
    *result, ORDER.token = pl.pallas_call(
        inner,
        name=name,
        out_shape=[
            pltpu.HBM(o.shape, o.dtype) if i in late_out else o for i, o in enumerate(out_shape)
        ]
        + [sds((8, LANE), F32)],
        in_specs=specs,
        out_specs=[hbm if i in late_out else vmem for i in range(outs)]
        + [pl.BlockSpec(memory_space=pl.ANY)],
        scratch_shapes=list(scratch) + room + sems,
        cost_estimate=pl.CostEstimate(
            flops=int(5 * KERNEL_US[name] * 1.1e9),
            bytes_accessed=int(5 * KERNEL_US[name] * 3.6e6),
            transcendentals=0,
        ),
        compiler_params=pltpu.CompilerParams(
            vmem_limit_bytes=int(1.02 * nbytes) + VALUES_MB[name] * 2**20
        ),
    )(*args, *parts, *after)
    return result


def col(start):
    return pl.multiple_of(start, LANE)


class Parts:
    def __init__(self, arrays, order, first_rows, rows):
        self.arrays = arrays
        self.order = order
        self.first_rows = first_rows if isinstance(first_rows, list) else [first_rows] * len(arrays)
        self.rows = rows

    def open(self, refs, me_ref, dst, sem, chunks, own_only=False):
        if self.order is None:
            rows = pl.ds(self.first_rows[0], self.rows)
            src = refs[0].at[:, rows, :]
            if own_only:
                src = refs[0].at[pl.ds(me_ref[0] * chunks, chunks), rows, :]
            pltpu.make_async_copy(src, dst, sem).start()
            return Blocks(dst, sem, chunks, 0, 0)
        for ref, first_row, (mx, dx) in zip(refs, self.first_rows, self.order):
            rows = pl.ds(first_row, self.rows)
            at = pl.ds((0 if own_only else mx * chunks) + dx, ref.shape[0])
            pltpu.make_async_copy(ref.at[:, rows, :], dst.at[at], sem).start()
        return Blocks(dst, sem, chunks, 0 if own_only else me_ref[0], me_ref[1])


def others(wd, wu):
    return [a for a in wu.arrays if not any(a is b for b in wd.arrays)]


def shared(wd, wu, d_refs, refs):
    more = iter(refs)
    found, count = [], 0
    for a in wu.arrays:
        at = [i for i, b in enumerate(wd.arrays) if a is b]
        count += not at
        found.append(d_refs[at[0]] if at else next(more))
    return found, refs[count:]


class Blocks:
    def __init__(self, ref, sem, chunks, turn_m, turn_d):
        self.ref, self.sem, self.chunks = ref, sem, chunks
        self.turn_m, self.turn_d = turn_m, turn_d

    def wait(self):
        pltpu.make_async_copy(self.ref, self.ref, self.sem).wait()

    def place(self, m, d):
        if isinstance(self.turn_d, int):
            return m * self.chunks + d
        return jnp.bitwise_xor(m, self.turn_m) * self.chunks + jnp.bitwise_xor(d, self.turn_d)

    def block(self, m, b, lo=0, hi=None):
        rows = pl.ds(b * CHUNK, CHUNK)
        hi = self.chunks if hi is None else hi
        return jnp.concatenate([self.ref[self.place(m, d), rows, :] for d in range(lo, hi)], axis=0)

    def wide(self, which, lo=0, hi=None):
        return jnp.concatenate([self.block(m, b, lo, hi) for m, b in which], axis=1)

    def params(self, first_row, layer):
        rows = slice(first_row + 8 * layer, first_row + 8 * layer + 8)
        share = LANE // CHUNK
        tiles = []
        for i in range(self.chunks // share):
            tile = self.ref[self.place(0, i * share), rows, :].astype(F32)
            for j in range(1, share):
                tile += self.ref[self.place(0, i * share + j), rows, :].astype(F32)
            tiles.append(tile)
        return jnp.concatenate(tiles, axis=1)


def norm_parts(x):
    mean = jnp.mean(x, axis=1, keepdims=True)
    centred = x - mean
    rstd = lax.rsqrt(jnp.mean(centred * centred, axis=1, keepdims=True) + NORM_EPS)
    return centred * rstd, rstd


def sigmoid(v):
    return 1.0 / (1.0 + jnp.exp(-v))


def rows_at(me_ref, at, part):
    return pl.ds(pl.multiple_of(me_ref[2 + at] * part, part), part)


def seg_bounds(seg_ref, row, q_at, q_spans):
    first_id = seg_ref[row, q_at * SPAN]
    first_id = jnp.where(first_id < 0, 1 << 20, first_id)
    low = jnp.int32(0)
    for kb in range(q_spans - 1):
        last_id = seg_ref[row, (kb + 1) * SPAN - 1]
        last_id = jnp.where(last_id < 0, 1 << 20, last_id)
        low += jnp.where((kb < q_at) & (last_id < first_id), 1, 0)
    return low


def allowed_t(segc_ref, segr_ref, row, k0, q0, spans):
    keys = spans * SPAN
    seg_k = segc_ref[pl.ds(k0, keys), :]
    seg_q = segr_ref[row, :, pl.ds(q0, SPAN)]
    same = jnp.concatenate([seg_k == seg_q[:, :LANE], seg_k == seg_q[:, LANE:]], axis=1)
    tri = lax.broadcasted_iota(jnp.int32, (SPAN, SPAN), 0) <= (
        lax.broadcasted_iota(jnp.int32, (SPAN, SPAN), 1)
    )
    if spans == 1:
        return same & tri
    return jnp.concatenate([same[: keys - SPAN], same[keys - SPAN :] & tri], axis=0)


def attend_body(
    wq, layer, norm_here, mp_size, chunks, batch, me_ref, seg_ref, segr_ref, *refs
):
    given = mp_size if norm_here else mp_size * batch
    t_refs, refs = refs[:given], refs[given:]
    w_refs, refs = refs[: len(wq.arrays)], refs[len(wq.arrays) :]
    qkv_ref, lse_ref = refs[:2]
    o_refs, refs = [refs[2], refs[3], refs[4].at[0], refs[4].at[1]], refs[5:]
    if norm_here:
        par_ref, n_refs, refs = refs[0], refs[1 : 1 + mp_size * batch], refs[1 + mp_size * batch :]
    w_scr, o_scr, segc_ref, sem = refs
    part = o_refs[0].shape[1]
    me_m = me_ref[0]
    w = wq.open(w_refs, me_ref, w_scr, sem, chunks, own_only=True)
    w.wait()
    if norm_here:
        for l in range(par_ref.shape[0]):
            par_ref[l] = w.params(3 * CHUNK, l)
    weights = w.wide([(0, 0), (0, 1), (0, 2)])
    q_spans = qkv_ref.shape[1] // SPAN
    for r in range(batch):
        for mx in range(mp_size):
            at = pl.ds(pl.multiple_of(jnp.bitwise_xor(me_m, mx) * part, part), part)
            if norm_here:
                xhat, _ = norm_parts(t_refs[mx][me_ref[2 + r]].astype(F32))
                n = (xhat * par_ref[layer, 0:1] + par_ref[layer, 2:3]).astype(BF16)
                n_refs[r * mp_size + mx][...] = n
                send(n_refs[r * mp_size + mx])
            else:
                n = t_refs[mx * batch + r][...]
            qkv_ref[r, at, :] = nn(n, weights).astype(BF16)
    send(qkv_ref)

    for r in range(batch):
        length = qkv_ref.shape[1]
        segc_ref[pl.ds(r * length, length), :] = jnp.broadcast_to(segr_ref[r], (LANE, length)).T

    def step(i, carry):
        r, q_at = i // q_spans, i % q_spans
        low = seg_bounds(seg_ref, r, q_at, q_spans)
        q0 = pl.multiple_of(q_at * SPAN, SPAN)
        k0 = pl.multiple_of(low * SPAN, SPAN)
        k_abs = pl.multiple_of((r * q_spans + low) * SPAN, SPAN)
        for spans in range(1, q_spans + 1):

            @pl.when(q_at - low + 1 == spans)
            def _():
                keys = spans * SPAN
                mask = allowed_t(segc_ref, segr_ref, r, k_abs, q0, spans)
                outs = []
                for h in range(2):
                    lo = h * HEAD_DIM
                    q = qkv_ref[r, pl.ds(q0, SPAN), lo : lo + HEAD_DIM] * jnp.asarray(
                        HEAD_DIM**-0.5, BF16
                    )
                    k = qkv_ref[r, pl.ds(k0, keys), 128 + lo : 128 + lo + HEAD_DIM]
                    v = qkv_ref[r, pl.ds(k0, keys), 256 + lo : 256 + lo + HEAD_DIM]
                    s = jnp.where(mask, nt(k, q), -1e30)
                    top = jnp.max(s, axis=0, keepdims=True)
                    p = jnp.exp(s - top)
                    total = jnp.sum(p, axis=0, keepdims=True)
                    lse_ref[r * 2 + h, :, pl.ds(q0, SPAN)] = top + jnp.log(total)
                    outs.append(tn(v, p.astype(BF16)) / total)
                o_scr[r, pl.ds(q0, SPAN), :] = jnp.concatenate(outs, axis=0).T.astype(BF16)

        return carry

    lax.fori_loop(0, batch * q_spans, step, 0)
    for mx in range(mp_size):
        at = pl.multiple_of(jnp.bitwise_xor(me_m, mx) * part, part)
        for r in range(batch):
            o_refs[mx][r] = o_scr[r, pl.ds(at, part), :]


def attend(me, segs, t_parts, wq, layer, layers, norm_here, chunks):
    seg, segr = segs
    batch, length = seg.shape
    mp_size = 4
    part, model = t_parts[0].shape[-2:]
    out = [sds((batch, length, 384), BF16), sds((batch * 2, 1, length), F32)]
    if norm_here:
        out = [Late(o) for o in out]
    out += [sds((batch, part, LANE), BF16)] * 2 + [sds((2, batch, part, LANE), BF16)]
    if norm_here:
        out += [sds((layers, 8, model), F32)] + [Late(sds((part, model), BF16))] * mp_size * batch
    return call(
        functools.partial(attend_body, wq, layer, norm_here, mp_size, chunks, batch),
        "attend",
        out,
        [me, seg, segr] + t_parts,
        smem=2,
        parts=wq.arrays,
        scratch=[
            pltpu.VMEM((chunks, wq.rows, LANE), BF16),
            pltpu.VMEM((batch, length, LANE), BF16),
            pltpu.VMEM((batch * length, LANE), F32),
            pltpu.SemaphoreType.DMA,
        ],
    )


def second_body(
    wd, wu, layer, mp_size, chunks, batch, has_next, me_ref, x_ref, par_ref, *refs
):
    n_refs, refs = refs[:batch], refs[batch:]
    t_refs, refs = refs[:mp_size], refs[mp_size:]
    t_refs = [t_refs[0], t_refs[1], t_refs[2].at[0], t_refs[3].at[1]]
    d_refs, refs = refs[: len(wd.arrays)], refs[len(wd.arrays) :]
    u_refs, refs = shared(wd, wu, d_refs, refs)
    att_ref, s1_ref, mid_ref, n2_ref, s2_ref, act_ref, slope_ref, out_ref = refs[:8]
    refs = refs[8:]
    if has_next:
        next_refs, refs = refs[:batch], refs[batch:]
    n_scr, d_scr, u_scr, d_sem, u_sem = refs
    w_d = wd.open(d_refs, me_ref, d_scr, d_sem, chunks)
    w_u = wu.open(u_refs, me_ref, u_scr, u_sem, chunks)
    me_m = me_ref[0]
    part = n_refs[0].shape[0]
    par = par_ref.at[layer]
    for r in range(batch):
        for mx in range(mp_size):
            m = jnp.bitwise_xor(me_m, mx)
            att_ref[rows_at(me_ref, r, part), pl.ds(col(m * LANE), LANE)] = t_refs[mx][r]
    send(att_ref)
    need(*n_refs)
    for r in range(batch):
        n_scr[rows_at(me_ref, r, part), :] = n_refs[r][...]
    n = n_scr[...]
    every = range(mp_size)
    w_d.wait()
    s1 = sigmoid(nn(n, w_d.wide([(m, 0) for m in every])) + par[3:4])
    s1_ref[...] = s1
    send(s1_ref)
    need(x_ref)
    mid = (
        x_ref[...].astype(F32)
        + nt(att_ref[...], w_d.wide([(m, 1) for m in every]))
        + s1 * n.astype(F32)
    )
    mid_ref[...] = mid
    send(mid_ref)
    xhat, _ = norm_parts(mid)
    n2_ref[...] = (xhat * par[1:2] + par[4:5]).astype(BF16)
    send(n2_ref)
    w_u.wait()
    s2_ref[...] = sigmoid(nn(n2_ref[...], w_u.wide([(m, 0) for m in every])) + par[5:6])
    send(s2_ref)
    ff_blocks = act_ref.shape[1] // (mp_size * LANE)
    for m in every:
        for b in range(0, ff_blocks, 2):
            at = (m * ff_blocks + b) * LANE
            cols = slice(at, at + 2 * LANE)
            hidden = nn(n2_ref[...], w_u.wide([(m, 1 + b), (m, 2 + b)]))
            square = hidden * hidden
            inner = 0.7978845608 + (0.7978845608 * 0.044715) * square
            th = jnp.tanh(hidden * inner)
            half = 0.5 + 0.5 * th
            act = hidden * half
            act_ref[:, cols] = act.astype(BF16)
            slope = half + act * (1.0 - th) * (3.0 * inner - 2 * 0.7978845608)
            slope_ref[:, cols] = slope.astype(BF16)
    send(act_ref, slope_ref)
    share = chunks // 2
    for j in range(2):
        cols = slice(j * share * CHUNK, (j + 1) * share * CHUNK)
        down = [(m, 2 + b) for m in every for b in range(ff_blocks)]
        out_ref[:, cols] = (
            mid_ref[:, cols]
            + s2_ref[:, cols] * n2_ref[:, cols].astype(F32)
            + nt(act_ref[...], w_d.wide(down, j * share, (j + 1) * share))
        )
    send(out_ref)
    if has_next:
        xhat, _ = norm_parts(out_ref[...])
        n_scr[...] = (xhat * par_ref[layer + 1, 0:1] + par_ref[layer + 1, 2:3]).astype(BF16)
        for r in range(batch):
            next_refs[r][...] = n_scr[rows_at(me_ref, r, part), :]


def second(me, x, par, n_rows, t_parts, wd, wu, layer, chunks, ff, has_next, after=()):
    rows, model = x.shape
    mp_size = len(t_parts)
    out = [
        sds((rows, model), BF16),
        sds((rows, model), F32),
        sds((rows, model), F32),
        sds((rows, model), BF16),
        sds((rows, model), F32),
        sds((rows, ff), BF16),
        sds((rows, ff), BF16),
        sds((rows, model), F32),
    ]
    out = [Late(o) for o in out]
    if has_next:
        out += [sds(n_rows[0].shape, BF16)] * len(n_rows)
    return call(
        functools.partial(
            second_body, wd, wu, layer, mp_size, chunks, len(n_rows), has_next
        ),
        "second",
        out,
        [me, Late(x), par] + [Late(n) for n in n_rows] + t_parts,
        smem=1,
        parts=wd.arrays + others(wd, wu),
        scratch=[
            pltpu.VMEM((rows, model), BF16),
            pltpu.VMEM((chunks * mp_size, wd.rows, LANE), BF16),
            pltpu.VMEM((chunks * mp_size, wu.rows, LANE), BF16),
            pltpu.SemaphoreType.DMA,
            pltpu.SemaphoreType.DMA,
        ],
        after=after,
    )


def norm_back(x, gain, d_normed):
    xhat, rstd = norm_parts(x)
    e = d_normed * gain
    mean_e = jnp.mean(e, axis=1, keepdims=True)
    mean_ex = jnp.mean(e * xhat, axis=1, keepdims=True)
    d_gain = jnp.sum(d_normed * xhat, axis=0, keepdims=True)
    d_bias = jnp.sum(d_normed, axis=0, keepdims=True)
    return (e - mean_e - xhat * mean_ex) * rstd, d_gain, d_bias


def second_back_body(
    wd, wu, layer, mp_size, chunks, batch, me_ref, g_ref, mid_ref, n2_ref, s2_ref, slope_ref,
    par_ref, *refs
):
    d_refs, refs = refs[: len(wd.arrays)], refs[len(wd.arrays) :]
    u_refs, refs = shared(wd, wu, d_refs, refs)
    b2_ref, dcomb_ref, gmid_ref, b1_ref, sums_ref = refs[:5]
    refs = refs[5:]
    o_refs, refs = [refs[0], refs[1], refs[2].at[0], refs[2].at[1]], refs[3:]
    o_scr, d_scr, u_scr, d_sem, u_sem = refs
    w_d = wd.open(d_refs, me_ref, d_scr, d_sem, chunks)
    w_u = wu.open(u_refs, me_ref, u_scr, u_sem, chunks)
    ff = slope_ref.shape[1]
    model = g_ref.shape[1]
    ff_m = ff // mp_size
    ff_blocks = ff_m // LANE
    stride = LANE + ff_m
    part = g_ref.shape[0] // batch
    me_m = me_ref[0]
    every = range(mp_size)
    g = g_ref[...]
    b2_ref[...] = g.astype(BF16)
    need(n2_ref, s2_ref)
    s2 = s2_ref[...]
    b2f = b2_ref[...].astype(F32)
    d_z2 = (b2f * n2_ref[...].astype(F32) * s2 * (1.0 - s2)).astype(BF16)
    sums_ref[2:3, :] = jnp.sum(d_z2.astype(F32), axis=0, keepdims=True)
    for m in every:
        dcomb_ref[:, m * stride : m * stride + LANE] = d_z2[:, m * LANE : (m + 1) * LANE]
    w_d.wait()
    need(slope_ref)
    for m in every:
        for b in range(0, ff_blocks, 2):
            at = m * ff_m + b * LANE
            d_act = nn(b2_ref[...], w_d.wide([(m, 2 + b), (m, 3 + b)]))
            slope = slope_ref[:, at : at + 2 * LANE].astype(F32)
            at = m * stride + (1 + b) * LANE
            dcomb_ref[:, at : at + 2 * LANE] = (d_act * slope).astype(BF16)
    w_u.wait()
    share = chunks // 2
    cols_of = [(m, b) for m in every for b in range(1 + ff_blocks)]
    for j in range(2):
        cols = slice(j * share * CHUNK, (j + 1) * share * CHUNK)
        gmid_ref[:, cols] = b2_ref[:, cols].astype(F32) * s2_ref[:, cols] + nt(
            dcomb_ref[...], w_u.wide(cols_of, j * share, (j + 1) * share)
        )
    need(mid_ref)
    d_mid, d_gain, d_bias = norm_back(mid_ref[...], par_ref[layer, 1:2], gmid_ref[...])
    sums_ref[0:1, :] = d_gain
    sums_ref[1:2, :] = d_bias
    sums_ref[3:8, :] = jnp.zeros((5, model), F32)
    g_mid = g_ref[...] + d_mid
    gmid_ref[...] = g_mid
    b1_ref[...] = g_mid.astype(BF16)
    for mx in every:
        m = jnp.bitwise_xor(me_m, mx)
        o_scr[...] = nn(b1_ref[...], w_d.block(m, 1)).astype(BF16)
        for r in range(batch):
            o_refs[mx][r] = o_scr[rows_at(me_ref, r, part), :]


def second_back(me, g, mid, n2, s2, slope, par, wd, wu, layer, mp_size, chunks, batch, after=()):
    rows, model = g.shape
    ff = slope.shape[1]
    out = [
        sds((rows, model), BF16),
        sds((rows, ff + LANE * mp_size), BF16),
        sds((rows, model), F32),
        sds((rows, model), BF16),
        sds((8, model), F32),
    ]
    out += [sds((batch, rows // batch, LANE), BF16)] * 2
    out += [sds((2, batch, rows // batch, LANE), BF16)]
    return call(
        functools.partial(second_back_body, wd, wu, layer, mp_size, chunks, batch),
        "second_back",
        out,
        [me, g, Late(mid), Late(n2), Late(s2), Late(slope), par],
        smem=1,
        parts=wd.arrays + others(wd, wu),
        scratch=[
            pltpu.VMEM((rows, LANE), BF16),
            pltpu.VMEM((chunks * mp_size, wd.rows, LANE), BF16),
            pltpu.VMEM((chunks * mp_size, wu.rows, LANE), BF16),
            pltpu.SemaphoreType.DMA,
            pltpu.SemaphoreType.DMA,
        ],
        after=after,
    )


def attend_back_body(wq, row, mp_size, chunks, last, me_ref, seg_ref, segr_ref, *refs):
    qkv_ref, lse_ref = refs[:2]
    d_in, refs = refs[2 : 2 + mp_size], refs[2 + mp_size :]
    d_in = [d_in[0].at[row], d_in[1].at[row], d_in[2].at[0, row], d_in[3].at[1, row]]
    n_refs, refs = refs[:mp_size], refs[mp_size:]
    if last:
        before_ref, refs = refs[0], refs[1:]
    w_refs, refs = refs[: len(wq.arrays)], refs[len(wq.arrays) :]
    keep_ref, send_ref, dw_ref = refs[:3]
    w_scr, do_scr, dqkv_scr, dk_scr, dv_scr, segc_ref, sem = refs[3:]
    w = wq.open(w_refs, me_ref, w_scr, sem, chunks, own_only=True)
    length = qkv_ref.shape[1]
    part = d_in[0].shape[0]
    me_m, me_d = me_ref[0], me_ref[1]
    for mx in range(mp_size):
        at = pl.multiple_of(jnp.bitwise_xor(me_m, mx) * part, part)
        do_scr[pl.ds(at, part), :] = d_in[mx][...]
    dqkv_scr[...] = jnp.zeros_like(dqkv_scr)
    dk_scr[...] = jnp.zeros_like(dk_scr)
    segc_ref[...] = jnp.broadcast_to(segr_ref[row], (LANE, length)).T
    dv_scr[...] = jnp.zeros_like(dv_scr)
    q_spans = length // SPAN

    def step(q_at, carry):
        low = seg_bounds(seg_ref, row, q_at, q_spans)
        real = seg_ref[row, q_at * SPAN] >= 0
        q0 = pl.multiple_of(q_at * SPAN, SPAN)
        k0 = pl.multiple_of(low * SPAN, SPAN)
        for spans in range(1, q_spans + 1):

            @pl.when(real & (q_at - low + 1 == spans))
            def _():
                keys = spans * SPAN
                mask = allowed_t(segc_ref, segr_ref, row, k0, q0, spans)
                dqs, dks, dvs = [], [], []
                for h in range(2):
                    lo = h * HEAD_DIM
                    q = qkv_ref[row, pl.ds(q0, SPAN), lo : lo + HEAD_DIM] * jnp.asarray(
                        HEAD_DIM**-0.5, BF16
                    )
                    k = qkv_ref[row, pl.ds(k0, keys), 128 + lo : 128 + lo + HEAD_DIM]
                    v = qkv_ref[row, pl.ds(k0, keys), 256 + lo : 256 + lo + HEAD_DIM]
                    do = do_scr[pl.ds(q0, SPAN), lo : lo + HEAD_DIM]
                    lse = lse_ref[row * 2 + h, :, pl.ds(q0, SPAN)]
                    p = jnp.where(mask, jnp.exp(nt(k, q) - lse), 0.0)
                    dvs.append(nn(p.astype(BF16), do))
                    dp = nt(v, do)
                    delta = jnp.sum(p * dp, axis=0, keepdims=True)
                    ds = (p * (dp - delta)).astype(BF16)
                    dks.append(nn(ds, q))
                    dqs.append(tn(k, ds))
                dqkv_scr[pl.ds(q0, SPAN), 0:128] = (
                    jnp.concatenate(dqs, axis=0).T * HEAD_DIM**-0.5
                ).astype(BF16)
                dk_scr[pl.ds(k0, keys), :] += jnp.concatenate(dks, axis=1)
                dv_scr[pl.ds(k0, keys), :] += jnp.concatenate(dvs, axis=1)

        return carry

    lax.fori_loop(0, q_spans, step, 0)
    dqkv_scr[:, 128:256] = dk_scr[...].astype(BF16)
    dqkv_scr[:, 256:384] = dv_scr[...].astype(BF16)
    w.wait()
    weights = w.wide([(0, 0), (0, 1), (0, 2)])
    need(*n_refs)
    grad = jnp.zeros((n_refs[0].shape[1], 384), F32)
    if last:
        grad = before_ref[...]
    for mx in range(mp_size):
        at = pl.multiple_of(jnp.bitwise_xor(me_m, mx) * part, part)
        d_here = dqkv_scr[pl.ds(at, part), :]
        d_n = nt(d_here, weights).astype(BF16)
        (send_ref if mx % 2 else keep_ref)[mx // 2] = d_n
        grad += tn(n_refs[mx][...], d_here)
    if not last:
        dw_ref[...] = grad
        return
    grad = grad.astype(BF16)
    for d in range(chunks):
        for b in range(3):
            dw_ref[jnp.bitwise_xor(d, me_d), b * CHUNK : (b + 1) * CHUNK, :] = grad[
                d * CHUNK : (d + 1) * CHUNK, b * LANE : (b + 1) * LANE
            ]


def attend_back(
    me, seg, segr, qkv, lse, d_parts, n_parts, wq, row, chunks, before=None, after=()
):
    mp_size = len(d_parts)
    length = seg.shape[1]
    part, model = n_parts[0].shape
    last = before is not None
    out = [sds((mp_size // 2, part, model), BF16)] * 2
    out += [sds((chunks, 3 * CHUNK, LANE), BF16) if last else sds((model, 384), F32)]
    return call(
        functools.partial(attend_back_body, wq, row, mp_size, chunks, last),
        "attend_back",
        out,
        [me, seg, segr, qkv, lse]
        + d_parts
        + [Late(n) for n in n_parts]
        + ([before] if last else []),
        smem=2,
        parts=wq.arrays,
        scratch=[
            pltpu.VMEM((chunks, wq.rows, LANE), BF16),
            pltpu.VMEM((length, LANE), BF16),
            pltpu.VMEM((length, 384), BF16),
            pltpu.VMEM((length, LANE), F32),
            pltpu.VMEM((length, LANE), F32),
            pltpu.VMEM((length, LANE), F32),
            pltpu.SemaphoreType.DMA,
        ],
        after=after,
    )


def first_back_body(
    layer, batch, me_ref, x_ref, gmid_ref, local_ref, par_ref, sums2_ref, sums1_ref, *refs
):
    kept, got = refs[:batch], refs[batch : 2 * batch]
    g_ref, sums_ref = refs[2 * batch :]
    part = kept[0].shape[0]
    for r in range(batch):
        at = rows_at(me_ref, r, part)
        g_ref[at, :] = local_ref[at, :] + kept[r][...].astype(F32) + got[r][...].astype(F32)
    need(x_ref)
    d_x, d_gain, d_bias = norm_back(x_ref[...].astype(F32), par_ref[layer, 0:1], g_ref[...])
    g_ref[...] = gmid_ref[...] + d_x
    sums_ref[0:1, :] = d_gain
    sums_ref[1:2, :] = sums2_ref[0:1, :]
    sums_ref[2:3, :] = d_bias
    sums_ref[3:4, :] = sums1_ref[0:1, :]
    sums_ref[4:5, :] = sums2_ref[1:2, :]
    sums_ref[5:6, :] = sums2_ref[2:3, :]
    sums_ref[6:8, :] = sums2_ref[6:8, :]


def first_back(me, x, gmid, local, par, sums2, sums1, kept, got, layer, after=()):
    rows, model = x.shape
    return call(
        functools.partial(first_back_body, layer, len(kept)),
        "first_back",
        [sds((rows, model), F32), sds((8, model), F32)],
        [me, Late(x), gmid, local, par, sums2, sums1] + kept + got,
        smem=1,
        after=after,
    )


def put_blocks(outs, mx, me_d, chunks, at_block, res, mp_first=False):
    half = chunks // 2
    for d in range(chunks):
        at = jnp.bitwise_xor(d, me_d)
        if mp_first:
            at = (mx // 2) * chunks + at
        else:
            at = (at // half) * chunks + (mx // 2) * half + at % half
        for b in range(res.shape[1] // LANE):
            rows = slice((at_block + b) * CHUNK, (at_block + b + 1) * CHUNK)
            outs[mx % 2][at, rows, :] = res[d * CHUNK : (d + 1) * CHUNK, b * LANE : (b + 1) * LANE]


def weight_grad_body(
    wd, mp_size, chunks, batch, mp_first, me_ref, n2_ref, dcomb_ref, b1_ref, b2_ref, att_ref,
    act_ref, s1_ref, *refs
):
    n_refs, refs = refs[:batch], refs[batch:]
    d_refs, refs = refs[: len(wd.arrays)], refs[len(wd.arrays) :]
    ups, downs, (local_ref, sums_ref), refs = refs[:2], refs[2:4], refs[4:6], refs[6:]
    w_scr, left, n_left, b1_left, z_scr, sem = refs
    w = wd.open(d_refs, me_ref, w_scr, sem, chunks)
    me_m, me_d = me_ref[0], me_ref[1]
    every = range(mp_size)
    need(n2_ref)
    left[...] = n2_ref[...].T
    stride = dcomb_ref.shape[1] // mp_size
    for mx in every:
        m = jnp.bitwise_xor(me_m, mx)
        res = nn(left[...], dcomb_ref[:, pl.ds(col(m * stride), stride)])
        put_blocks(ups, mx, me_d, chunks, 0, res.astype(BF16), mp_first)
    need(s1_ref, *n_refs)
    for r in range(batch):
        z_scr[rows_at(me_ref, r, n_refs[r].shape[0]), :] = n_refs[r][...]
    n = z_scr[...]
    n_left[...] = n.T
    b1f = b1_ref[...].astype(F32)
    s1 = s1_ref[...]
    d_z1 = (b1f * n.astype(F32) * s1 * (1.0 - s1)).astype(BF16)
    z_scr[...] = d_z1
    sums_ref[0:1, :] = jnp.sum(d_z1.astype(F32), axis=0, keepdims=True)
    sums_ref[1:8, :] = jnp.zeros((7, sums_ref.shape[1]), F32)
    b1_left[...] = b1_ref[...].T
    left[...] = b2_ref[...].T
    w.wait()
    local_ref[...] = b1f * s1 + nt(d_z1, w.wide([(m, 0) for m in every]))
    need(att_ref, act_ref)
    ff_m = act_ref.shape[1] // mp_size
    for mx in every:
        m = jnp.bitwise_xor(me_m, mx)
        cols = pl.ds(col(m * LANE), LANE)
        put_blocks(downs, mx, me_d, chunks, 0, nn(n_left[...], z_scr[:, cols]).astype(BF16))
        put_blocks(downs, mx, me_d, chunks, 1, nn(b1_left[...], att_ref[:, cols]).astype(BF16))
        res = nn(left[...], act_ref[:, pl.ds(col(m * ff_m), ff_m)])
        put_blocks(downs, mx, me_d, chunks, 2, res.astype(BF16))


def weight_grad(
    me, n2, dcomb, b1, b2, att, act, s1, n_rows, wd, mp_size, chunks, mp_first, after=()
):
    rows, model = b1.shape
    gates = Parts(wd.arrays, wd.order, wd.first_rows, CHUNK)
    height = dcomb.shape[1] // mp_size // LANE * CHUNK
    return call(
        functools.partial(weight_grad_body, gates, mp_size, chunks, len(n_rows), mp_first),
        "weight_grad",
        [sds((mp_size // 2 * chunks, height, LANE), BF16)] * 2
        + [sds((mp_size // 2 * chunks, wd.rows, LANE), BF16)] * 2
        + [sds((rows, model), F32), sds((8, model), F32)],
        [me, Late(n2), dcomb, b1, b2, Late(att), Late(act), Late(s1)]
        + [Late(n) for n in n_rows],
        smem=1,
        parts=wd.arrays,
        scratch=[pltpu.VMEM((chunks * mp_size, CHUNK, LANE), BF16)]
        + [pltpu.VMEM((model, rows), BF16)] * 3
        + [pltpu.VMEM((rows, model), BF16), pltpu.SemaphoreType.DMA],
        after=after,
    )


def swap(value, axis, size, bits):
    return lax.ppermute(value, axis, [(i, i ^ bits) for i in range(size)])


def add_body(count, *refs):
    left, right = refs[:2]
    outs = refs[2:]
    size = outs[0].shape[0]

    def step(i, carry):
        for part, out in enumerate(outs):
            at = part * size + i
            out[i] = (left[at].astype(F32) + right[at].astype(F32)).astype(BF16)
        return carry

    lax.fori_loop(0, size, step, 0)


def add(left, right, count):
    shape = (left.shape[0] // count,) + left.shape[1:]
    return call(
        functools.partial(add_body, count),
        "add",
        [sds(shape, BF16)] * count,
        [left, right],
    )


def join_body(count, has_sums, me_ref, *refs):
    pairs = [(refs[2 * i], refs[2 * i + 1]) for i in range(count)]
    refs = refs[2 * count :]
    if has_sums:
        sums_ref, refs = refs[0], refs[1:]
    for k, out in enumerate(refs):
        at = 0
        for left, right in pairs:
            rows = left.shape[1]
            out[at : at + rows, :] = (left[k].astype(F32) + right[k].astype(F32)).astype(BF16)
            at += rows
        if has_sums:
            tile = jnp.bitwise_xor(me_ref[1], k) // (LANE // CHUNK)
            out[at:, :] = sums_ref[:, pl.ds(col(tile * LANE), LANE)].astype(BF16)


def join(me, pairs, sums=None):
    width = 4
    rows = sum(p[0].shape[1] for p in pairs) + (0 if sums is None else sums.shape[0])
    flat = [a for pair in pairs for a in pair]
    return call(
        functools.partial(join_body, len(pairs), sums is not None),
        "add",
        [sds((rows, LANE), BF16)] * width,
        [me] + flat + ([] if sums is None else [sums]),
        smem=1,
    )


def total_body(*refs):
    value = refs[0][...].astype(F32)
    for ref in refs[1:-1]:
        value += ref[...].astype(F32)
    refs[-1][...] = value


def total(parts):
    return call(total_body, "add", [sds(parts[0].shape, F32)], parts)[0]


def stack_body(cuts, *refs):
    ins, outs = refs[: -len(cuts)], refs[-len(cuts) :]
    for i, ref in enumerate(ins):
        at = 0
        for out, rows in zip(outs, cuts):
            out[i] = ref[at : at + rows, :]
            at += rows


def stack(arrays, cuts=None, after=()):
    cuts = cuts or [arrays[0].shape[0]]
    return call(
        functools.partial(stack_body, cuts),
        "stack",
        [sds((len(arrays), rows, LANE), BF16) for rows in cuts],
        arrays,
        after=after,
    )


def copy_body(rows, *refs):
    half = len(refs) // 2
    for (first, count), a_ref, b_ref in zip(rows, refs[:half], refs[half:]):
        b_ref[...] = a_ref[:, first : first + count, :]


def copied(*pieces):
    return call(
        functools.partial(copy_body, [p[1:] for p in pieces]),
        "stack",
        [sds((a.shape[0], count, a.shape[2]), a.dtype) for a, _, count in pieces],
        [p[0] for p in pieces],
    )


def relay_body(*refs):
    pass


def relay(arrays, name="relay"):
    call(relay_body, name, [], [], after=arrays)


def pack_q_body(per, me_ref, qkv_ref, par_ref, out_ref):
    for c in range(3):
        out_ref[c * per : (c + 1) * per, :] = qkv_ref[c]
    rows = jnp.concatenate([par_ref[...].astype(F32)] * (LANE // per), axis=1)
    share = lax.broadcasted_iota(jnp.int32, rows.shape, 1) // per
    mine = jnp.where(share == me_ref[1] % (LANE // per), rows, 0.0)
    out_ref[3 * per :, :] = mine.astype(BF16)


def pack_q(me, qkv, params):
    per = qkv.shape[1]
    return call(
        functools.partial(pack_q_body, per),
        "pack",
        [sds((3 * per + params.shape[0], LANE), BF16)],
        [me, qkv, params],
        smem=1,
    )[0]


def pack_body(layer, with_q, qkv_ref, gate_ref, out_ref, up_ref, down_ref, shard_ref):
    per = gate_ref.shape[2]
    at = 0
    if with_q:
        for c in range(3):
            shard_ref[at : at + per, :] = qkv_ref[layer, c]
            at += per
    refs = (gate_ref.at[layer, 0], out_ref.at[layer], down_ref.at[layer])
    for ref in refs + (gate_ref.at[layer, 1], up_ref.at[layer]):
        for b in range(ref.shape[1] // LANE):
            shard_ref[at : at + per, :] = ref[:, b * LANE : (b + 1) * LANE]
            at += per


def pack(layer, with_q, w_qkv, w_gate, w_out, w_up, w_down):
    per = w_gate.shape[2]
    cols = 2 * w_gate.shape[3] + w_out.shape[2] + w_up.shape[2] + w_down.shape[2]
    rows = (cols // LANE + 3 * with_q) * per
    return call(
        functools.partial(pack_body, layer, with_q),
        "pack",
        [sds((rows, LANE), BF16)],
        [w_qkv, w_gate, w_out, w_up, w_down],
    )[0]


def finish_body(counts, names, me_ref, *refs):
    ins, outs = refs[: sum(counts)], refs[sum(counts) :]
    d_qkv, d_out, d_gate, d_up, d_down, d_gains, d_norm_biases, d_gate_biases = outs
    per = CHUNK
    at = 0
    for count, pieces in zip(counts, names):
        value = ins[at][...].astype(F32)
        for ref in ins[at + 1 : at + count]:
            value += ref[...].astype(F32)
        at += count
        row = 0
        for name, l in pieces:
            if name == "p":
                low, high = value[row:, :CHUNK], value[row:, CHUNK:]
                value = jnp.where(me_ref[1] % 2 == 0, low, high)
                for i in range(value.shape[0] // 8):
                    for out, first in ((d_gains, 0), (d_norm_biases, 2), (d_gate_biases, 3)):
                        step = 1 if out is d_gains else 2
                        for j in range(2):
                            at_row = 8 * i + first + j * step
                            out[i, j : j + 1, :] = value[at_row : at_row + 1]
                continue
            blocks = {"q": 3, "u": 1 + d_up.shape[2] // LANE, "d": 2 + d_down.shape[2] // LANE}
            for b in range(blocks[name]):
                block = value[row : row + per]
                row += per
                if name == "q":
                    d_qkv[l, b] = block
                elif name == "u" and b == 0:
                    d_gate[l, 1] = block
                elif name == "u":
                    d_up[l, :, (b - 1) * LANE : b * LANE] = block
                elif b == 0:
                    d_gate[l, 0] = block
                elif b == 1:
                    d_out[l] = block
                else:
                    d_down[l, :, (b - 2) * LANE : (b - 1) * LANE] = block


def finish(me, layers, ff_m, groups):
    shapes = [(3, CHUNK, LANE), (CHUNK, LANE), (2, CHUNK, LANE), (CHUNK, ff_m), (CHUNK, ff_m)]
    out = [sds((layers,) + shape, F32) for shape in shapes] + [sds((layers, 2, CHUNK), F32)] * 3
    return call(
        functools.partial(finish_body, [len(g[0]) for g in groups], [g[1] for g in groups]),
        "finish",
        out,
        [me] + [a for g in groups for a in g[0]],
        smem=1,
    )


def solution(mesh):
    dp_size, mp_size, width_size = (mesh.shape[a] for a in ("dp", "mp", "width"))
    all_axes = ("mp", "dp", "width")
    direct = (dp_size, mp_size, width_size) == (2, 4, 4)

    def mp_swap(value, bits):
        return swap(value, "mp", mp_size, bits)

    def dp_swap(value):
        return swap(value, "dp", dp_size, 1)

    def spread(value):
        return [value, mp_swap(value, 1), mp_swap(value, 2)]

    def spread_last(values):
        return values + [mp_swap(values[2], 1)]

    def exchange(own, near, far):
        far = mp_swap(far, 2)
        return [own, mp_swap(near, 1), far, mp_swap(far, 1)]

    def send_width(value):
        return [value] + [swap(value, "width", width_size, k) for k in range(1, width_size)]

    def swap_width(values):
        return [values[0]] + [
            swap(values[k], "width", width_size, k) for k in range(1, width_size)
        ]

    def on_device(
        tokens, segments, cotangent, norm_gains, biases, w_qkv, w_out, w_gate, w_up, w_down
    ):
        ORDER.token = None
        batch, part, model = tokens.shape
        layers = w_qkv.shape[0]
        per = w_qkv.shape[1]
        chunks = model // CHUNK
        half = chunks // 2
        ff_m = w_up.shape[2]
        ff_blocks = ff_m // LANE
        ff = ff_m * mp_size
        me_m = lax.axis_index("mp")
        me_d = lax.axis_index("dp") * width_size + lax.axis_index("width")
        rows = [jnp.where(segments[0, -1] < 0, 0, batch - 1)]
        rows += [batch - 1 - rows[0]] if batch == 2 else []
        me = jnp.stack([me_m, me_d] + rows).astype(jnp.int32)
        me_pack, me_att = me, me
        if not direct:
            me_pack = jnp.stack([0 * me_m, 0 * me_d] + rows).astype(jnp.int32)
            me_att = jnp.stack([me_m, 0 * me_d] + rows).astype(jnp.int32)

        def blocks_of(matrix):
            return jnp.swapaxes(matrix.reshape(per, -1, LANE), 0, 1).reshape(-1, LANE)

        qkv_t, out_t, down_t = (jnp.swapaxes(w, 1, 2) for w in (w_qkv, w_out, w_down))
        params = jnp.concatenate([norm_gains, biases], axis=1)
        params = jnp.pad(params, ((0, 0), (0, 2), (0, 0))).reshape(layers * 8, per)

        def param_block():
            rows = jnp.concatenate([params] * (LANE // per), axis=1)
            share = lax.broadcasted_iota(jnp.int32, rows.shape, 1) // per
            return jnp.where(share == me_d % (LANE // per), rows, 0)

        q_rows, d_rows, u_rows = 3 * CHUNK, (2 + ff_blocks) * CHUNK, (1 + ff_blocks) * CHUNK

        def shard(l, q):
            mats = [w_gate[l, 0], out_t[l], blocks_of(down_t[l]), w_gate[l, 1], blocks_of(w_up[l])]
            return jnp.concatenate(([qkv_t[l].reshape(-1, LANE)] if q else []) + mats, axis=0)

        def gather_whole(shard, extra):
            full = lax.all_gather(shard, all_axes, axis=0, tiled=False)
            if per == CHUNK:
                return full
            count = (shard.shape[0] - extra) // per
            full = full.reshape(mp_size, chunks, CHUNK // per, shard.shape[0], LANE)
            mats = full[:, :, :, : count * per]
            mats = mats.reshape(mp_size, chunks, CHUNK // per, count, per, LANE)
            mats = jnp.swapaxes(mats, 2, 3).reshape(mp_size * chunks, count * CHUNK, LANE)
            if not extra:
                return mats
            pars = jnp.sum(full[:, :, :, count * per :].astype(F32), axis=2).astype(BF16)
            return jnp.concatenate([mats, pars.reshape(mp_size * chunks, extra, LANE)], axis=1)

        def reduce_whole(even, odd):
            full = jnp.stack([even, odd], axis=1)
            full = full.reshape(2, mp_size // 2, half, 2, -1, CHUNK // per, per, LANE)
            full = jnp.transpose(full, (1, 3, 0, 2, 5, 4, 6, 7)).reshape(-1, LANE).astype(F32)
            return lax.psum_scatter(full, all_axes, scatter_dimension=0, tiled=True)

        def reduce_q_whole(grad):
            full = grad.reshape(chunks, -1, CHUNK // per, per, LANE)
            full = jnp.swapaxes(full, 1, 2).reshape(-1, LANE).astype(F32)
            return lax.psum_scatter(full, ("dp", "width"), scatter_dimension=0, tiled=True)

        seg = jnp.where(rows[0] == 0, segments, segments[::-1]) if batch == 2 else segments
        segs = (seg, seg[:, None, :].astype(F32))

        q_all = q_rows + layers * 8
        weights = [None] * layers
        if direct:
            mats = (qkv_t, w_gate, out_t, w_up, down_t)
            q_steps = send_width(pack_q(me, qkv_t[0], params))
            t_all = spread(tokens)
            w_steps = send_width(pack(0, False, *mats))
            relay([], "pack")
            (q_base,) = stack(q_steps)
            t_far = copied((t_all[2], 0, part))[0]
            wq = Parts([q_base, dp_swap(q_base)], [(0, 0), (0, 4)], 0, q_all)
            (base,) = stack(w_steps)
            got = {(0, 0): base, (0, 4): dp_swap(base), (2, 0): mp_swap(base, 2)}
            later = send_width(pack(1, True, *mats))
            relay([wq.arrays[1]])
            t_all = t_all + [mp_swap(t_far, 1)]
        else:
            t_all = spread_last(spread(tokens))
            q_sh = jnp.concatenate([qkv_t[0].reshape(-1, LANE), param_block()], axis=0)
            wq = Parts([gather_whole(q_sh, layers * 8)], None, 0, q_all)
            full = gather_whole(shard(0, False), 0)
            wd, wu = Parts([full], None, 0, d_rows), Parts([full], None, d_rows, u_rows)
            for l in range(1, layers):
                full = gather_whole(shard(l, True), 0)
                weights[l] = (
                    Parts([full], None, 0, q_rows),
                    Parts([full], None, q_rows, d_rows),
                    Parts([full], None, q_rows + d_rows, u_rows),
                )

        def last_step(got):
            d_last, u_last = copied((got[2, 0], 0, d_rows), (got[0, 4], d_rows, u_rows))
            return dp_swap(d_last), mp_swap(u_last, 2)

        def two_pieces(got, lasts):
            for m, d in list(got):
                got[m + 1, d] = mp_swap(got[m, d], 1)
            arrays, order = list(got.values()), list(got) + [(2, 4), (3, 4)]
            lasts = copied(*[(a, 0, a.shape[1]) for a in lasts])
            d_all, u_all = (arrays + [a, mp_swap(a, 1)] for a in lasts)
            return (
                Parts(d_all, order, 0, d_rows),
                Parts(u_all, order, [d_rows] * len(arrays) + [0, 0], u_rows),
            )

        x = tokens.reshape(batch * part, model)
        par = None
        saved = []
        t_parts = t_all
        for l in range(layers):
            if l and direct:
                wq = wq_next
            elif l:
                wq, wd, wu = weights[l]
            qkv, lse, own, near, far, *rest = attend(
                me, segs, t_parts, wq, l, layers, l == 0, chunks
            )
            kept = (qkv, lse)
            if l == 0:
                par = rest[0]
                n_parts = [rest[1 + r * mp_size : 1 + (r + 1) * mp_size] for r in range(batch)]
            else:
                n_parts = [t_parts[r::batch] for r in range(batch)]
            o_parts = exchange(own, near, far)
            if direct:
                if l == 0:
                    relay([got[0, 4], got[2, 0]] + later[1:])
                    lasts = last_step(got)
                    relay([o_parts[2]])
                wd, wu = two_pieces(got, lasts)
                if l == 0:
                    q_base, base = stack(later, [q_rows, d_rows + u_rows])
                    wq_next = Parts([q_base, dp_swap(q_base)], [(0, 0), (0, 4)], 0, q_rows)
                    got = {(0, 0): base, (0, 4): dp_swap(base), (2, 0): mp_swap(base, 2)}
                else:
                    wq = wq_next
                weights[l] = (wq, wd, wu)
            elif l == 0:
                weights[0] = (wq, wd, wu)
            n_rows = [n_parts[r][0] for r in range(batch)]
            att, s1, mid, n2, s2, act, slope, out, *following = second(
                me, x, par, n_rows, o_parts, wd, wu, l, chunks, ff, l + 1 < layers
            )
            saved.append((x, n_parts, kept, att, s1, mid, n2, s2, act, slope))
            x = out
            if following:
                t_rows = [spread(n) for n in following]
                if direct:
                    relay([got[0, 4], got[2, 0], wq_next.arrays[1]] + [t[2] for t in t_rows])
                    lasts = last_step(got)
                t_rows = [spread_last(t) for t in t_rows]
                t_parts = [t_rows[r][mx] for mx in range(mp_size) for r in range(batch)]
        output = x.reshape(batch, part, model)

        own = lax.dynamic_slice_in_dim(segments, me_m * part, part, 1)
        g = cotangent.astype(F32) * (own >= 0).astype(F32)[:, :, None]
        g = g.reshape(batch * part, model)
        reduced = [None] * layers
        all_sums = [None] * layers
        moving = {}

        def reduce_2(name, mp_first=False):
            if name in moving:
                keep, send = add(*moving[name], 2)
                moving[name] = (keep, mp_swap(send, 2) if mp_first else dp_swap(send))

        def reduce_3(name, mp_first=False):
            if name in moving:
                keep, send = add(*moving[name], 2)
                moving[name] = (keep, dp_swap(send) if mp_first else mp_swap(send, 2))

        def reduce_4(names, sums=None):
            if direct:
                pairs = [moving.pop(name) for name in names]
                moving[names[0]] = swap_width(join(me, pairs, sums))

        def reduce_5(name):
            return total(moving.pop(name)) if direct else None

        for l in reversed(range(layers)):
            wq, wd, wu = weights[l]
            x, n_parts, kept, att, s1, mid, n2, s2, act, slope = saved[l]
            n_rows = [n_parts[r][0] for r in range(batch)]
            final, first_of_two = l == 0, l + 1 < layers
            b2, dcomb, gmid, b1, sums2, *o_parts = second_back(
                me, g, mid, n2, s2, slope, par, wd, wu, l, mp_size, chunks, batch
            )
            d_parts = exchange(*o_parts)
            if first_of_two:
                reduce_4([("q", l + 1), ("u", l + 1)])
            reduce_3(("d", l + 1))
            *grads, local, sums1 = weight_grad(
                me_pack, n2, dcomb, b1, b2, att, act, s1, n_rows, wd, mp_size, chunks,
                final and direct,
            )
            relay([d_parts[2]])
            if direct:
                moving["u", l] = (grads[0], mp_swap(grads[1], 1))
                moving["d", l] = (grads[2], mp_swap(grads[3], 1))
            keeps, gots = [], []
            q_grad = None
            for r in range(batch):
                keep, send, q_grad = attend_back(
                    me_att, *segs, *kept, d_parts, n_parts[r], wq, r, chunks, q_grad
                )
                if r == 0:
                    if first_of_two:
                        reduce_4([("d", l + 1)])
                    reduce_2(("d", l))
                    reduce_2(("u", l), final)
                    if first_of_two:
                        moving["q", l + 1] = [reduce_5(("q", l + 1))] if direct else None
                else:
                    reduce_3(("u", l), final)
                    if final:
                        reduce_3(("d", l))
                keep, send = add(keep, mp_swap(send, 1), 2)
                keeps.append(keep.reshape(keep.shape[1:]))
                gots.append(mp_swap(send, 2).reshape(keep.shape[1:]))
            if direct and first_of_two:
                moving["d", l + 1] = [reduce_5(("d", l + 1))]
            if direct:
                moving["q", l] = (q_grad[:half], dp_swap(q_grad[half:]))
                if final:
                    reduce_4([("u", l)])
            g, all_sums[l] = first_back(me, x, gmid, local, par, sums2, sums1, keeps, gots, l)
            if direct and final:
                reduce_4([("q", l), ("d", l)])
                moving["u", l] = [reduce_5(("u", l))]
            if not direct:
                reduced[l] = (reduce_q_whole(q_grad), reduce_whole(*grads[:2]), reduce_whole(*grads[2:]))
        d_tokens = g.reshape(batch, part, model)
        sums = jnp.concatenate(all_sums, axis=0)
        if direct:
            sums = sums + mp_swap(sums, 1)
            sums = sums + mp_swap(sums, 2)
            sums = sums + dp_swap(sums)
            moving["p", 0] = swap_width(join(me, [], sums))
            groups = [
                (moving["q", 1], [("q", 1), ("u", 1)]),
                (moving["d", 1], [("d", 1)]),
                (moving["u", 0], [("u", 0)]),
                (moving["q", 0], [("q", 0), ("d", 0)]),
                (moving["p", 0], [("p", 0)]),
            ]
            stacked = finish(me, layers, ff_m, groups)
            stacked, small = stacked[:5], stacked[5:]
        else:
            params = lax.dynamic_slice_in_dim(lax.psum(sums, all_axes), me_d * per, per, 1)
            params = params.reshape(layers, 8, per)
            small = [params[:, 0:2], params[:, 2:6:2], params[:, 3:6:2]]

        def unblocks(rows, count):
            return jnp.swapaxes(rows.reshape(count, per, LANE), 0, 1).reshape(per, count * LANE)

        if not direct:
            grads = []
            for q_sum, up_sum, down_sum in reduced:
                grads.append(
                    (
                        q_sum.reshape(3, per, LANE),
                        down_sum[per : 2 * per],
                        jnp.stack([down_sum[:per], up_sum[:per]]),
                        unblocks(up_sum[per:], ff_blocks),
                        unblocks(down_sum[2 * per :], ff_blocks),
                    )
                )
            stacked = [jnp.stack([grads[l][i] for l in range(layers)]) for i in range(5)]
        for i in (0, 1, 4):
            stacked[i] = jnp.swapaxes(stacked[i], 1, 2)
        return (
            output,
            d_tokens,
            *small,
            *stacked,
        )

    placed = (
        P(("dp", "width"), "mp", None),
        P(("dp", "width"), None),
        P(("dp", "width"), "mp", None),
        P(None, None, ("dp", "width")),
        P(None, None, ("dp", "width")),
        P(None, ("dp", "width"), None, "mp"),
        P(None, "mp", ("dp", "width")),
        P(None, None, ("dp", "width"), "mp"),
        P(None, ("dp", "width"), "mp"),
        P(None, "mp", ("dp", "width")),
    )
    return jax.shard_map(
        on_device,
        mesh=mesh,
        in_specs=placed,
        out_specs=(
            placed[0],
            placed[0],
            placed[3],
            placed[3],
            placed[3],
            placed[5],
            placed[6],
            placed[7],
            placed[8],
            placed[9],
        ),
        check_vma=False,
    )
```

```python
import functools

import jax
import jax.numpy as jnp
from jax import lax
from jax.experimental import pallas as pl
from jax.experimental.pallas import tpu as pltpu
from jax.sharding import PartitionSpec as P

HEAD_DIM = 64
LANE = 128
NORM_EPS = 1e-05
SPAN = 256
CHUNK = 64

VALUES_MB = {
    "attend": 6,
    "second": 10,
    "second_back": 10,
    "attend_back": 8,
    "first_back": 6,
    "weight_grad": 8,
    "relay": 1,
    "sum": 2,
    "stack": 2,
    "add": 2,
    "pack": 2,
    "finish": 4,
}

KERNEL_US = {
    "attend": 8,
    "second": 12,
    "second_back": 10,
    "attend_back": 9,
    "first_back": 4,
    "weight_grad": 8,
    "relay": 1,
    "sum": 0.1,
    "stack": 0.1,
    "add": 1,
    "pack": 10,
    "finish": 2,
}

F32 = jnp.float32
BF16 = jnp.bfloat16


def nn(a, b):
    return jnp.dot(a, b, preferred_element_type=F32)


def nt(a, b):
    return lax.dot_general(a, b, (((1,), (1,)), ((), ())), preferred_element_type=F32)


def tn(a, b):
    return lax.dot_general(a, b, (((0,), (0,)), ((), ())), preferred_element_type=F32)


def sds(shape, dtype):
    return jax.ShapeDtypeStruct(shape, dtype)


class Late:
    def __init__(self, array):
        self.array = array


class Copies:
    def __init__(self, pairs, first_out, sems):
        self.first_out = first_out
        self.all = [
            (ref, pltpu.make_async_copy(*pair, sems.at[i]))
            for i, (ref, *pair) in enumerate(pairs)
        ]
        self.waiting = []
        self.unsent = list(self.all[first_out:])
        for ref, copy in self.all[:first_out]:
            copy.start()
            self.waiting.append((ref, copy))

    def need(self, *refs):
        for ref in refs:
            for i, entry in enumerate(self.waiting):
                if entry[0] is ref:
                    entry[1].wait()
                    del self.waiting[i]
                    break

    def send(self, *refs):
        for ref in refs:
            for i, entry in enumerate(self.unsent):
                if entry[0] is ref:
                    entry[1].start()
                    del self.unsent[i]
                    break

    def finish(self):
        for _, copy in self.waiting:
            copy.wait()
        for _, copy in self.unsent:
            copy.start()
        for _, copy in self.all[self.first_out :]:
            copy.wait()


class Chain:
    def __init__(self):
        self.token = None
        self.copies = None


ORDER = Chain()


def need(*refs):
    ORDER.copies.need(*refs)


def send(*refs):
    ORDER.copies.send(*refs)


def in_hbm(a):
    return pltpu.with_memory_space_constraint(a, pltpu.HBM)


def size_of(a):
    return a.size * a.dtype.itemsize


def call(body, name, out_shape, args, smem=0, parts=(), scratch=(), after=()):
    after = list(after) + ([] if ORDER.token is None else [ORDER.token])
    late_in = [i for i, a in enumerate(args) if isinstance(a, Late)]
    late_out = [i for i, o in enumerate(out_shape) if isinstance(o, Late)]
    args = [in_hbm(a.array) if isinstance(a, Late) else a for a in args]
    out_shape = [o.array if isinstance(o, Late) else o for o in out_shape]
    parts = [in_hbm(a) for a in parts]
    hbm, vmem = (pl.BlockSpec(memory_space=space) for space in (pltpu.HBM, pltpu.VMEM))
    specs = [pl.BlockSpec(memory_space=pltpu.SMEM)] * smem
    specs += [hbm if i in late_in else vmem for i in range(smem, len(args))]
    specs += [hbm] * len(parts)
    specs += [pl.BlockSpec(memory_space=pl.ANY)] * len(after)
    used = len(args) + len(parts)
    given = used + len(after)
    outs = len(out_shape)
    late = [args[i] for i in late_in] + [out_shape[i] for i in late_out]
    room = [pltpu.VMEM(a.shape, a.dtype) for a in late]
    sems = [pltpu.SemaphoreType.DMA((len(late),))] if late else []

    def inner(*refs):
        ins, results = list(refs[:used]), list(refs[given : given + outs])
        rest = refs[given + outs + 1 :]
        own = rest[: len(scratch)]
        places = rest[len(scratch) : len(scratch) + len(late)]
        pairs = []
        for i, place in zip(late_in, places):
            pairs.append((place, ins[i], place))
            ins[i] = place
        for i, place in zip(late_out, places[len(late_in) :]):
            pairs.append((place, place, results[i]))
            results[i] = place
        copies = ORDER.copies = Copies(pairs, len(late_in), rest[-1] if late else None)
        body(*ins, *results, *own)
        copies.finish()

    nbytes = sum(size_of(a) for a in args + out_shape)
    for s in scratch:
        if hasattr(s, "shape") and len(s.shape) > 1:
            nbytes += size_of(jax.ShapeDtypeStruct(s.shape, s.dtype))
    *result, ORDER.token = pl.pallas_call(
        inner,
        name=name,
        out_shape=[
            pltpu.HBM(o.shape, o.dtype) if i in late_out else o for i, o in enumerate(out_shape)
        ]
        + [sds((8, LANE), F32)],
        in_specs=specs,
        out_specs=[hbm if i in late_out else vmem for i in range(outs)]
        + [pl.BlockSpec(memory_space=pl.ANY)],
        scratch_shapes=list(scratch) + room + sems,
        cost_estimate=pl.CostEstimate(
            flops=int(5 * KERNEL_US[name] * 1.1e9),
            bytes_accessed=int(5 * KERNEL_US[name] * 3.6e6),
            transcendentals=0,
        ),
        compiler_params=pltpu.CompilerParams(
            vmem_limit_bytes=int(1.02 * nbytes) + VALUES_MB[name] * 2**20
        ),
    )(*args, *parts, *after)
    return result


def col(start):
    return pl.multiple_of(start, LANE)


class Parts:
    def __init__(self, arrays, order, first_rows, rows):
        self.arrays = arrays
        self.order = order
        self.first_rows = first_rows if isinstance(first_rows, list) else [first_rows] * len(arrays)
        self.rows = rows

    def open(self, refs, me_ref, dst, sem, chunks, own_only=False):
        if self.order is None:
            rows = pl.ds(self.first_rows[0], self.rows)
            src = refs[0].at[:, rows, :]
            if own_only:
                src = refs[0].at[pl.ds(me_ref[0] * chunks, chunks), rows, :]
            pltpu.make_async_copy(src, dst, sem).start()
            return Blocks(dst, sem, chunks, 0, 0)
        for ref, first_row, (mx, dx) in zip(refs, self.first_rows, self.order):
            rows = pl.ds(first_row, self.rows)
            at = pl.ds((0 if own_only else mx * chunks) + dx, ref.shape[0])
            pltpu.make_async_copy(ref.at[:, rows, :], dst.at[at], sem).start()
        return Blocks(dst, sem, chunks, 0 if own_only else me_ref[0], me_ref[1])


def others(wd, wu):
    return [a for a in wu.arrays if not any(a is b for b in wd.arrays)]


def shared(wd, wu, d_refs, refs):
    more = iter(refs)
    found, count = [], 0
    for a in wu.arrays:
        at = [i for i, b in enumerate(wd.arrays) if a is b]
        count += not at
        found.append(d_refs[at[0]] if at else next(more))
    return found, refs[count:]


class Blocks:
    def __init__(self, ref, sem, chunks, turn_m, turn_d):
        self.ref, self.sem, self.chunks = ref, sem, chunks
        self.turn_m, self.turn_d = turn_m, turn_d

    def wait(self):
        pltpu.make_async_copy(self.ref, self.ref, self.sem).wait()

    def place(self, m, d):
        if isinstance(self.turn_d, int):
            return m * self.chunks + d
        return jnp.bitwise_xor(m, self.turn_m) * self.chunks + jnp.bitwise_xor(d, self.turn_d)

    def block(self, m, b, lo=0, hi=None):
        rows = pl.ds(b * CHUNK, CHUNK)
        hi = self.chunks if hi is None else hi
        return jnp.concatenate([self.ref[self.place(m, d), rows, :] for d in range(lo, hi)], axis=0)

    def wide(self, which, lo=0, hi=None):
        return jnp.concatenate([self.block(m, b, lo, hi) for m, b in which], axis=1)

    def params(self, first_row, layer):
        rows = slice(first_row + 8 * layer, first_row + 8 * layer + 8)
        share = LANE // CHUNK
        tiles = []
        for i in range(self.chunks // share):
            tile = self.ref[self.place(0, i * share), rows, :].astype(F32)
            for j in range(1, share):
                tile += self.ref[self.place(0, i * share + j), rows, :].astype(F32)
            tiles.append(tile)
        return jnp.concatenate(tiles, axis=1)


def norm_parts(x):
    mean = jnp.mean(x, axis=1, keepdims=True)
    centred = x - mean
    rstd = lax.rsqrt(jnp.mean(centred * centred, axis=1, keepdims=True) + NORM_EPS)
    return centred * rstd, rstd


def sigmoid(v):
    return 1.0 / (1.0 + jnp.exp(-v))


def rows_at(me_ref, at, part):
    return pl.ds(pl.multiple_of(me_ref[2 + at] * part, part), part)


def seg_bounds(seg_ref, row, q_at, q_spans):
    first_id = seg_ref[row, q_at * SPAN]
    first_id = jnp.where(first_id < 0, 1 << 20, first_id)
    low = jnp.int32(0)
    for kb in range(q_spans - 1):
        last_id = seg_ref[row, (kb + 1) * SPAN - 1]
        last_id = jnp.where(last_id < 0, 1 << 20, last_id)
        low += jnp.where((kb < q_at) & (last_id < first_id), 1, 0)
    return low


def allowed_t(segc_ref, segr_ref, row, k0, q0, spans):
    keys = spans * SPAN
    seg_k = segc_ref[pl.ds(k0, keys), :]
    seg_q = segr_ref[row, :, pl.ds(q0, SPAN)]
    same = jnp.concatenate([seg_k == seg_q[:, :LANE], seg_k == seg_q[:, LANE:]], axis=1)
    tri = lax.broadcasted_iota(jnp.int32, (SPAN, SPAN), 0) <= (
        lax.broadcasted_iota(jnp.int32, (SPAN, SPAN), 1)
    )
    if spans == 1:
        return same & tri
    return jnp.concatenate([same[: keys - SPAN], same[keys - SPAN :] & tri], axis=0)


def attend_body(
    wq, layer, norm_here, mp_size, chunks, batch, me_ref, seg_ref, segr_ref, *refs
):
    given = mp_size if norm_here else mp_size * batch
    t_refs, refs = refs[:given], refs[given:]
    w_refs, refs = refs[: len(wq.arrays)], refs[len(wq.arrays) :]
    qkv_ref, lse_ref = refs[:2]
    o_refs, refs = [refs[2], refs[3], refs[4].at[0], refs[4].at[1]], refs[5:]
    if norm_here:
        par_ref, n_refs, refs = refs[0], refs[1 : 1 + mp_size * batch], refs[1 + mp_size * batch :]
    w_scr, o_scr, segc_ref, sem = refs
    part = o_refs[0].shape[1]
    me_m = me_ref[0]
    w = wq.open(w_refs, me_ref, w_scr, sem, chunks, own_only=True)
    w.wait()
    if norm_here:
        for l in range(par_ref.shape[0]):
            par_ref[l] = w.params(3 * CHUNK, l)
    weights = w.wide([(0, 0), (0, 1), (0, 2)])
    q_spans = qkv_ref.shape[1] // SPAN
    for r in range(batch):
        for mx in range(mp_size):
            at = pl.ds(pl.multiple_of(jnp.bitwise_xor(me_m, mx) * part, part), part)
            if norm_here:
                xhat, _ = norm_parts(t_refs[mx][me_ref[2 + r]].astype(F32))
                n = (xhat * par_ref[layer, 0:1] + par_ref[layer, 2:3]).astype(BF16)
                n_refs[r * mp_size + mx][...] = n
                send(n_refs[r * mp_size + mx])
            else:
                n = t_refs[mx * batch + r][...]
            qkv_ref[r, at, :] = nn(n, weights).astype(BF16)
    send(qkv_ref)

    for r in range(batch):
        length = qkv_ref.shape[1]
        segc_ref[pl.ds(r * length, length), :] = jnp.broadcast_to(segr_ref[r], (LANE, length)).T

    def step(i, carry):
        r, q_at = i // q_spans, i % q_spans
        low = seg_bounds(seg_ref, r, q_at, q_spans)
        q0 = pl.multiple_of(q_at * SPAN, SPAN)
        k0 = pl.multiple_of(low * SPAN, SPAN)
        k_abs = pl.multiple_of((r * q_spans + low) * SPAN, SPAN)
        for spans in range(1, q_spans + 1):

            @pl.when(q_at - low + 1 == spans)
            def _():
                keys = spans * SPAN
                mask = allowed_t(segc_ref, segr_ref, r, k_abs, q0, spans)
                outs = []
                for h in range(2):
                    lo = h * HEAD_DIM
                    q = qkv_ref[r, pl.ds(q0, SPAN), lo : lo + HEAD_DIM] * jnp.asarray(
                        HEAD_DIM**-0.5, BF16
                    )
                    k = qkv_ref[r, pl.ds(k0, keys), 128 + lo : 128 + lo + HEAD_DIM]
                    v = qkv_ref[r, pl.ds(k0, keys), 256 + lo : 256 + lo + HEAD_DIM]
                    s = jnp.where(mask, nt(k, q), -1e30)
                    top = jnp.max(s, axis=0, keepdims=True)
                    p = jnp.exp(s - top)
                    total = jnp.sum(p, axis=0, keepdims=True)
                    lse_ref[r * 2 + h, :, pl.ds(q0, SPAN)] = top + jnp.log(total)
                    outs.append(tn(v, p.astype(BF16)) / total)
                o_scr[r, pl.ds(q0, SPAN), :] = jnp.concatenate(outs, axis=0).T.astype(BF16)

        return carry

    lax.fori_loop(0, batch * q_spans, step, 0)
    for mx in range(mp_size):
        at = pl.multiple_of(jnp.bitwise_xor(me_m, mx) * part, part)
        for r in range(batch):
            o_refs[mx][r] = o_scr[r, pl.ds(at, part), :]


def attend(me, segs, t_parts, wq, layer, layers, norm_here, chunks):
    seg, segr = segs
    batch, length = seg.shape
    mp_size = 4
    part, model = t_parts[0].shape[-2:]
    out = [sds((batch, length, 384), BF16), sds((batch * 2, 1, length), F32)]
    if norm_here:
        out = [Late(o) for o in out]
    out += [sds((batch, part, LANE), BF16)] * 2 + [sds((2, batch, part, LANE), BF16)]
    if norm_here:
        out += [sds((layers, 8, model), F32)] + [Late(sds((part, model), BF16))] * mp_size * batch
    return call(
        functools.partial(attend_body, wq, layer, norm_here, mp_size, chunks, batch),
        "attend",
        out,
        [me, seg, segr] + t_parts,
        smem=2,
        parts=wq.arrays,
        scratch=[
            pltpu.VMEM((chunks, wq.rows, LANE), BF16),
            pltpu.VMEM((batch, length, LANE), BF16),
            pltpu.VMEM((batch * length, LANE), F32),
            pltpu.SemaphoreType.DMA,
        ],
    )


def second_body(
    wd, wu, layer, mp_size, chunks, batch, has_next, me_ref, x_ref, par_ref, *refs
):
    n_refs, refs = refs[:batch], refs[batch:]
    t_refs, refs = refs[:mp_size], refs[mp_size:]
    t_refs = [t_refs[0], t_refs[1], t_refs[2].at[0], t_refs[3].at[1]]
    d_refs, refs = refs[: len(wd.arrays)], refs[len(wd.arrays) :]
    u_refs, refs = shared(wd, wu, d_refs, refs)
    att_ref, s1_ref, mid_ref, n2_ref, s2_ref, act_ref, slope_ref, out_ref = refs[:8]
    refs = refs[8:]
    if has_next:
        next_refs, refs = refs[:batch], refs[batch:]
    n_scr, d_scr, u_scr, d_sem, u_sem = refs
    w_d = wd.open(d_refs, me_ref, d_scr, d_sem, chunks)
    w_u = wu.open(u_refs, me_ref, u_scr, u_sem, chunks)
    me_m = me_ref[0]
    part = n_refs[0].shape[0]
    par = par_ref.at[layer]
    for r in range(batch):
        for mx in range(mp_size):
            m = jnp.bitwise_xor(me_m, mx)
            att_ref[rows_at(me_ref, r, part), pl.ds(col(m * LANE), LANE)] = t_refs[mx][r]
    send(att_ref)
    need(*n_refs)
    for r in range(batch):
        n_scr[rows_at(me_ref, r, part), :] = n_refs[r][...]
    n = n_scr[...]
    every = range(mp_size)
    w_d.wait()
    s1 = sigmoid(nn(n, w_d.wide([(m, 0) for m in every])) + par[3:4])
    s1_ref[...] = s1
    send(s1_ref)
    need(x_ref)
    mid = (
        x_ref[...].astype(F32)
        + nt(att_ref[...], w_d.wide([(m, 1) for m in every]))
        + s1 * n.astype(F32)
    )
    mid_ref[...] = mid
    send(mid_ref)
    xhat, _ = norm_parts(mid)
    n2_ref[...] = (xhat * par[1:2] + par[4:5]).astype(BF16)
    send(n2_ref)
    w_u.wait()
    s2_ref[...] = sigmoid(nn(n2_ref[...], w_u.wide([(m, 0) for m in every])) + par[5:6])
    send(s2_ref)
    ff_blocks = act_ref.shape[1] // (mp_size * LANE)
    for m in every:
        for b in range(0, ff_blocks, 2):
            at = (m * ff_blocks + b) * LANE
            cols = slice(at, at + 2 * LANE)
            hidden = nn(n2_ref[...], w_u.wide([(m, 1 + b), (m, 2 + b)]))
            square = hidden * hidden
            inner = 0.7978845608 + (0.7978845608 * 0.044715) * square
            th = jnp.tanh(hidden * inner)
            half = 0.5 + 0.5 * th
            act = hidden * half
            act_ref[:, cols] = act.astype(BF16)
            slope = half + act * (1.0 - th) * (3.0 * inner - 2 * 0.7978845608)
            slope_ref[:, cols] = slope.astype(BF16)
    send(act_ref, slope_ref)
    share = chunks // 2
    for j in range(2):
        cols = slice(j * share * CHUNK, (j + 1) * share * CHUNK)
        down = [(m, 2 + b) for m in every for b in range(ff_blocks)]
        out_ref[:, cols] = (
            mid_ref[:, cols]
            + s2_ref[:, cols] * n2_ref[:, cols].astype(F32)
            + nt(act_ref[...], w_d.wide(down, j * share, (j + 1) * share))
        )
    send(out_ref)
    if has_next:
        xhat, _ = norm_parts(out_ref[...])
        n_scr[...] = (xhat * par_ref[layer + 1, 0:1] + par_ref[layer + 1, 2:3]).astype(BF16)
        for r in range(batch):
            next_refs[r][...] = n_scr[rows_at(me_ref, r, part), :]


def second(me, x, par, n_rows, t_parts, wd, wu, layer, chunks, ff, has_next, after=()):
    rows, model = x.shape
    mp_size = len(t_parts)
    out = [
        sds((rows, model), BF16),
        sds((rows, model), F32),
        sds((rows, model), F32),
        sds((rows, model), BF16),
        sds((rows, model), F32),
        sds((rows, ff), BF16),
        sds((rows, ff), BF16),
        sds((rows, model), F32),
    ]
    out = [Late(o) for o in out]
    if has_next:
        out += [sds(n_rows[0].shape, BF16)] * len(n_rows)
    return call(
        functools.partial(
            second_body, wd, wu, layer, mp_size, chunks, len(n_rows), has_next
        ),
        "second",
        out,
        [me, Late(x), par] + [Late(n) for n in n_rows] + t_parts,
        smem=1,
        parts=wd.arrays + others(wd, wu),
        scratch=[
            pltpu.VMEM((rows, model), BF16),
            pltpu.VMEM((chunks * mp_size, wd.rows, LANE), BF16),
            pltpu.VMEM((chunks * mp_size, wu.rows, LANE), BF16),
            pltpu.SemaphoreType.DMA,
            pltpu.SemaphoreType.DMA,
        ],
        after=after,
    )


def norm_back(x, gain, d_normed):
    xhat, rstd = norm_parts(x)
    e = d_normed * gain
    mean_e = jnp.mean(e, axis=1, keepdims=True)
    mean_ex = jnp.mean(e * xhat, axis=1, keepdims=True)
    d_gain = jnp.sum(d_normed * xhat, axis=0, keepdims=True)
    d_bias = jnp.sum(d_normed, axis=0, keepdims=True)
    return (e - mean_e - xhat * mean_ex) * rstd, d_gain, d_bias


def second_back_body(
    wd, wu, layer, mp_size, chunks, batch, me_ref, g_ref, mid_ref, n2_ref, s2_ref, slope_ref,
    par_ref, *refs
):
    d_refs, refs = refs[: len(wd.arrays)], refs[len(wd.arrays) :]
    u_refs, refs = shared(wd, wu, d_refs, refs)
    b2_ref, dcomb_ref, gmid_ref, b1_ref, sums_ref = refs[:5]
    refs = refs[5:]
    o_refs, refs = [refs[0], refs[1], refs[2].at[0], refs[2].at[1]], refs[3:]
    o_scr, d_scr, u_scr, d_sem, u_sem = refs
    w_d = wd.open(d_refs, me_ref, d_scr, d_sem, chunks)
    ff = slope_ref.shape[1]
    model = g_ref.shape[1]
    ff_m = ff // mp_size
    ff_blocks = ff_m // LANE
    stride = LANE + ff_m
    part = g_ref.shape[0] // batch
    me_m = me_ref[0]
    every = range(mp_size)
    g = g_ref[...]
    b2_ref[...] = g.astype(BF16)
    need(n2_ref, s2_ref)
    s2 = s2_ref[...]
    b2f = b2_ref[...].astype(F32)
    d_z2 = (b2f * n2_ref[...].astype(F32) * s2 * (1.0 - s2)).astype(BF16)
    sums_ref[2:3, :] = jnp.sum(d_z2.astype(F32), axis=0, keepdims=True)
    for m in every:
        dcomb_ref[:, m * stride : m * stride + LANE] = d_z2[:, m * LANE : (m + 1) * LANE]
    w_d.wait()
    w_u = wu.open(u_refs, me_ref, u_scr, u_sem, chunks)
    need(slope_ref)
    for m in every:
        for b in range(0, ff_blocks, 2):
            at = m * ff_m + b * LANE
            d_act = nn(b2_ref[...], w_d.wide([(m, 2 + b), (m, 3 + b)]))
            slope = slope_ref[:, at : at + 2 * LANE].astype(F32)
            at = m * stride + (1 + b) * LANE
            dcomb_ref[:, at : at + 2 * LANE] = (d_act * slope).astype(BF16)
    w_u.wait()
    share = chunks // 2
    cols_of = [(m, b) for m in every for b in range(1 + ff_blocks)]
    for j in range(2):
        cols = slice(j * share * CHUNK, (j + 1) * share * CHUNK)
        gmid_ref[:, cols] = b2_ref[:, cols].astype(F32) * s2_ref[:, cols] + nt(
            dcomb_ref[...], w_u.wide(cols_of, j * share, (j + 1) * share)
        )
    need(mid_ref)
    d_mid, d_gain, d_bias = norm_back(mid_ref[...], par_ref[layer, 1:2], gmid_ref[...])
    sums_ref[0:1, :] = d_gain
    sums_ref[1:2, :] = d_bias
    sums_ref[3:8, :] = jnp.zeros((5, model), F32)
    g_mid = g_ref[...] + d_mid
    gmid_ref[...] = g_mid
    b1_ref[...] = g_mid.astype(BF16)
    for mx in every:
        m = jnp.bitwise_xor(me_m, mx)
        o_scr[...] = nn(b1_ref[...], w_d.block(m, 1)).astype(BF16)
        for r in range(batch):
            o_refs[mx][r] = o_scr[rows_at(me_ref, r, part), :]


def second_back(me, g, mid, n2, s2, slope, par, wd, wu, layer, mp_size, chunks, batch, after=()):
    rows, model = g.shape
    ff = slope.shape[1]
    out = [
        sds((rows, model), BF16),
        sds((rows, ff + LANE * mp_size), BF16),
        sds((rows, model), F32),
        sds((rows, model), BF16),
        sds((8, model), F32),
    ]
    out += [sds((batch, rows // batch, LANE), BF16)] * 2
    out += [sds((2, batch, rows // batch, LANE), BF16)]
    return call(
        functools.partial(second_back_body, wd, wu, layer, mp_size, chunks, batch),
        "second_back",
        out,
        [me, g, Late(mid), Late(n2), Late(s2), Late(slope), par],
        smem=1,
        parts=wd.arrays + others(wd, wu),
        scratch=[
            pltpu.VMEM((rows, LANE), BF16),
            pltpu.VMEM((chunks * mp_size, wd.rows, LANE), BF16),
            pltpu.VMEM((chunks * mp_size, wu.rows, LANE), BF16),
            pltpu.SemaphoreType.DMA,
            pltpu.SemaphoreType.DMA,
        ],
        after=after,
    )


def attend_back_body(wq, row, mp_size, chunks, last, me_ref, seg_ref, segr_ref, *refs):
    qkv_ref, lse_ref = refs[:2]
    d_in, refs = refs[2 : 2 + mp_size], refs[2 + mp_size :]
    d_in = [d_in[0].at[row], d_in[1].at[row], d_in[2].at[0, row], d_in[3].at[1, row]]
    n_refs, refs = refs[:mp_size], refs[mp_size:]
    if last:
        before_ref, refs = refs[0], refs[1:]
    w_refs, refs = refs[: len(wq.arrays)], refs[len(wq.arrays) :]
    keep_ref, send_ref, dw_ref = refs[:3]
    w_scr, do_scr, dqkv_scr, dk_scr, dv_scr, segc_ref, sem = refs[3:]
    w = wq.open(w_refs, me_ref, w_scr, sem, chunks, own_only=True)
    length = qkv_ref.shape[1]
    part = d_in[0].shape[0]
    me_m, me_d = me_ref[0], me_ref[1]
    for mx in range(mp_size):
        at = pl.multiple_of(jnp.bitwise_xor(me_m, mx) * part, part)
        do_scr[pl.ds(at, part), :] = d_in[mx][...]
    dqkv_scr[...] = jnp.zeros_like(dqkv_scr)
    dk_scr[...] = jnp.zeros_like(dk_scr)
    segc_ref[...] = jnp.broadcast_to(segr_ref[row], (LANE, length)).T
    dv_scr[...] = jnp.zeros_like(dv_scr)
    q_spans = length // SPAN

    def step(q_at, carry):
        low = seg_bounds(seg_ref, row, q_at, q_spans)
        real = seg_ref[row, q_at * SPAN] >= 0
        q0 = pl.multiple_of(q_at * SPAN, SPAN)
        k0 = pl.multiple_of(low * SPAN, SPAN)
        for spans in range(1, q_spans + 1):

            @pl.when(real & (q_at - low + 1 == spans))
            def _():
                keys = spans * SPAN
                mask = allowed_t(segc_ref, segr_ref, row, k0, q0, spans)
                dqs, dks, dvs = [], [], []
                for h in range(2):
                    lo = h * HEAD_DIM
                    q = qkv_ref[row, pl.ds(q0, SPAN), lo : lo + HEAD_DIM] * jnp.asarray(
                        HEAD_DIM**-0.5, BF16
                    )
                    k = qkv_ref[row, pl.ds(k0, keys), 128 + lo : 128 + lo + HEAD_DIM]
                    v = qkv_ref[row, pl.ds(k0, keys), 256 + lo : 256 + lo + HEAD_DIM]
                    do = do_scr[pl.ds(q0, SPAN), lo : lo + HEAD_DIM]
                    lse = lse_ref[row * 2 + h, :, pl.ds(q0, SPAN)]
                    p = jnp.where(mask, jnp.exp(nt(k, q) - lse), 0.0)
                    dvs.append(nn(p.astype(BF16), do))
                    dp = nt(v, do)
                    delta = jnp.sum(p * dp, axis=0, keepdims=True)
                    ds = (p * (dp - delta)).astype(BF16)
                    dks.append(nn(ds, q))
                    dqs.append(tn(k, ds))
                dqkv_scr[pl.ds(q0, SPAN), 0:128] = (
                    jnp.concatenate(dqs, axis=0).T * HEAD_DIM**-0.5
                ).astype(BF16)
                dk_scr[pl.ds(k0, keys), :] += jnp.concatenate(dks, axis=1)
                dv_scr[pl.ds(k0, keys), :] += jnp.concatenate(dvs, axis=1)

        return carry

    lax.fori_loop(0, q_spans, step, 0)
    dqkv_scr[:, 128:256] = dk_scr[...].astype(BF16)
    dqkv_scr[:, 256:384] = dv_scr[...].astype(BF16)
    w.wait()
    weights = w.wide([(0, 0), (0, 1), (0, 2)])
    need(*n_refs)
    grad = jnp.zeros((n_refs[0].shape[1], 384), F32)
    if last:
        grad = before_ref[...]
    for mx in range(mp_size):
        at = pl.multiple_of(jnp.bitwise_xor(me_m, mx) * part, part)
        d_here = dqkv_scr[pl.ds(at, part), :]
        d_n = nt(d_here, weights).astype(BF16)
        (send_ref if mx % 2 else keep_ref)[mx // 2] = d_n
        grad += tn(n_refs[mx][...], d_here)
    if not last:
        dw_ref[...] = grad
        return
    grad = grad.astype(BF16)
    for d in range(chunks):
        for b in range(3):
            dw_ref[jnp.bitwise_xor(d, me_d), b * CHUNK : (b + 1) * CHUNK, :] = grad[
                d * CHUNK : (d + 1) * CHUNK, b * LANE : (b + 1) * LANE
            ]


def attend_back(
    me, seg, segr, qkv, lse, d_parts, n_parts, wq, row, chunks, before=None, after=()
):
    mp_size = len(d_parts)
    length = seg.shape[1]
    part, model = n_parts[0].shape
    last = before is not None
    out = [sds((mp_size // 2, part, model), BF16)] * 2
    out += [sds((chunks, 3 * CHUNK, LANE), BF16) if last else sds((model, 384), F32)]
    return call(
        functools.partial(attend_back_body, wq, row, mp_size, chunks, last),
        "attend_back",
        out,
        [me, seg, segr, qkv, lse]
        + d_parts
        + [Late(n) for n in n_parts]
        + ([before] if last else []),
        smem=2,
        parts=wq.arrays,
        scratch=[
            pltpu.VMEM((chunks, wq.rows, LANE), BF16),
            pltpu.VMEM((length, LANE), BF16),
            pltpu.VMEM((length, 384), BF16),
            pltpu.VMEM((length, LANE), F32),
            pltpu.VMEM((length, LANE), F32),
            pltpu.VMEM((length, LANE), F32),
            pltpu.SemaphoreType.DMA,
        ],
        after=after,
    )


def first_back_body(
    layer, batch, me_ref, x_ref, gmid_ref, local_ref, par_ref, sums2_ref, sums1_ref, *refs
):
    kept, got = refs[:batch], refs[batch : 2 * batch]
    g_ref, sums_ref = refs[2 * batch :]
    part = kept[0].shape[0]
    for r in range(batch):
        at = rows_at(me_ref, r, part)
        g_ref[at, :] = local_ref[at, :] + kept[r][...].astype(F32) + got[r][...].astype(F32)
    need(x_ref)
    d_x, d_gain, d_bias = norm_back(x_ref[...].astype(F32), par_ref[layer, 0:1], g_ref[...])
    g_ref[...] = gmid_ref[...] + d_x
    sums_ref[0:1, :] = d_gain
    sums_ref[1:2, :] = sums2_ref[0:1, :]
    sums_ref[2:3, :] = d_bias
    sums_ref[3:4, :] = sums1_ref[0:1, :]
    sums_ref[4:5, :] = sums2_ref[1:2, :]
    sums_ref[5:6, :] = sums2_ref[2:3, :]
    sums_ref[6:8, :] = sums2_ref[6:8, :]


def first_back(me, x, gmid, local, par, sums2, sums1, kept, got, layer, after=()):
    rows, model = x.shape
    return call(
        functools.partial(first_back_body, layer, len(kept)),
        "first_back",
        [sds((rows, model), F32), sds((8, model), F32)],
        [me, Late(x), gmid, local, par, sums2, sums1] + kept + got,
        smem=1,
        after=after,
    )


def put_blocks(outs, mx, me_d, chunks, at_block, res, mp_first=False):
    half = chunks // 2
    for d in range(chunks):
        at = jnp.bitwise_xor(d, me_d)
        if mp_first:
            at = (mx // 2) * chunks + at
        else:
            at = (at // half) * chunks + (mx // 2) * half + at % half
        for b in range(res.shape[1] // LANE):
            rows = slice((at_block + b) * CHUNK, (at_block + b + 1) * CHUNK)
            outs[mx % 2][at, rows, :] = res[d * CHUNK : (d + 1) * CHUNK, b * LANE : (b + 1) * LANE]


def weight_grad_body(
    wd, mp_size, chunks, batch, mp_first, me_ref, n2_ref, dcomb_ref, b1_ref, b2_ref, att_ref,
    act_ref, s1_ref, *refs
):
    n_refs, refs = refs[:batch], refs[batch:]
    d_refs, refs = refs[: len(wd.arrays)], refs[len(wd.arrays) :]
    ups, downs, (local_ref, sums_ref), refs = refs[:2], refs[2:4], refs[4:6], refs[6:]
    w_scr, left, n_left, b1_left, z_scr, sem = refs
    w = wd.open(d_refs, me_ref, w_scr, sem, chunks)
    me_m, me_d = me_ref[0], me_ref[1]
    every = range(mp_size)
    need(n2_ref)
    left[...] = n2_ref[...].T
    stride = dcomb_ref.shape[1] // mp_size
    for mx in every:
        m = jnp.bitwise_xor(me_m, mx)
        res = nn(left[...], dcomb_ref[:, pl.ds(col(m * stride), stride)])
        put_blocks(ups, mx, me_d, chunks, 0, res.astype(BF16), mp_first)
    need(s1_ref, *n_refs)
    for r in range(batch):
        z_scr[rows_at(me_ref, r, n_refs[r].shape[0]), :] = n_refs[r][...]
    n = z_scr[...]
    n_left[...] = n.T
    b1f = b1_ref[...].astype(F32)
    s1 = s1_ref[...]
    d_z1 = (b1f * n.astype(F32) * s1 * (1.0 - s1)).astype(BF16)
    z_scr[...] = d_z1
    sums_ref[0:1, :] = jnp.sum(d_z1.astype(F32), axis=0, keepdims=True)
    sums_ref[1:8, :] = jnp.zeros((7, sums_ref.shape[1]), F32)
    b1_left[...] = b1_ref[...].T
    left[...] = b2_ref[...].T
    w.wait()
    local_ref[...] = b1f * s1 + nt(d_z1, w.wide([(m, 0) for m in every]))
    need(att_ref, act_ref)
    ff_m = act_ref.shape[1] // mp_size
    for mx in every:
        m = jnp.bitwise_xor(me_m, mx)
        cols = pl.ds(col(m * LANE), LANE)
        put_blocks(downs, mx, me_d, chunks, 0, nn(n_left[...], z_scr[:, cols]).astype(BF16))
        put_blocks(downs, mx, me_d, chunks, 1, nn(b1_left[...], att_ref[:, cols]).astype(BF16))
        res = nn(left[...], act_ref[:, pl.ds(col(m * ff_m), ff_m)])
        put_blocks(downs, mx, me_d, chunks, 2, res.astype(BF16))


def weight_grad(
    me, n2, dcomb, b1, b2, att, act, s1, n_rows, wd, mp_size, chunks, mp_first, after=()
):
    rows, model = b1.shape
    gates = Parts(wd.arrays, wd.order, wd.first_rows, CHUNK)
    height = dcomb.shape[1] // mp_size // LANE * CHUNK
    return call(
        functools.partial(weight_grad_body, gates, mp_size, chunks, len(n_rows), mp_first),
        "weight_grad",
        [sds((mp_size // 2 * chunks, height, LANE), BF16)] * 2
        + [sds((mp_size // 2 * chunks, wd.rows, LANE), BF16)] * 2
        + [sds((rows, model), F32), sds((8, model), F32)],
        [me, Late(n2), dcomb, b1, b2, Late(att), Late(act), Late(s1)]
        + [Late(n) for n in n_rows],
        smem=1,
        parts=wd.arrays,
        scratch=[pltpu.VMEM((chunks * mp_size, CHUNK, LANE), BF16)]
        + [pltpu.VMEM((model, rows), BF16)] * 3
        + [pltpu.VMEM((rows, model), BF16), pltpu.SemaphoreType.DMA],
        after=after,
    )


def swap(value, axis, size, bits):
    return lax.ppermute(value, axis, [(i, i ^ bits) for i in range(size)])


def add_body(count, *refs):
    left, right = refs[:2]
    outs = refs[2:]
    size = outs[0].shape[0]

    def step(i, carry):
        for part, out in enumerate(outs):
            at = part * size + i
            out[i] = (left[at].astype(F32) + right[at].astype(F32)).astype(BF16)
        return carry

    lax.fori_loop(0, size, step, 0)


def add(left, right, count, name="add"):
    shape = (left.shape[0] // count,) + left.shape[1:]
    return call(
        functools.partial(add_body, count),
        name,
        [sds(shape, BF16)] * count,
        [left, right],
    )


def join_body(count, has_sums, me_ref, *refs):
    pairs = [(refs[2 * i], refs[2 * i + 1]) for i in range(count)]
    refs = refs[2 * count :]
    if has_sums:
        sums_ref, refs = refs[0], refs[1:]
    for k, out in enumerate(refs):
        at = 0
        for left, right in pairs:
            rows = left.shape[1]
            out[at : at + rows, :] = (left[k].astype(F32) + right[k].astype(F32)).astype(BF16)
            at += rows
        if has_sums:
            tile = jnp.bitwise_xor(me_ref[1], k) // (LANE // CHUNK)
            out[at:, :] = sums_ref[:, pl.ds(col(tile * LANE), LANE)].astype(BF16)


def join(me, pairs, sums=None, name="add"):
    width = 4
    rows = sum(p[0].shape[1] for p in pairs) + (0 if sums is None else sums.shape[0])
    flat = [a for pair in pairs for a in pair]
    return call(
        functools.partial(join_body, len(pairs), sums is not None),
        name,
        [sds((rows, LANE), BF16)] * width,
        [me] + flat + ([] if sums is None else [sums]),
        smem=1,
    )


def total_body(*refs):
    value = refs[0][...].astype(F32)
    for ref in refs[1:-1]:
        value += ref[...].astype(F32)
    refs[-1][...] = value


def total(parts, name="add"):
    return call(total_body, name, [sds(parts[0].shape, F32)], parts)[0]


def stack_body(cuts, *refs):
    ins, outs = refs[: -len(cuts)], refs[-len(cuts) :]
    for i, ref in enumerate(ins):
        at = 0
        for out, rows in zip(outs, cuts):
            out[i] = ref[at : at + rows, :]
            at += rows


def stack(arrays, cuts=None, after=()):
    cuts = cuts or [arrays[0].shape[0]]
    return call(
        functools.partial(stack_body, cuts),
        "stack",
        [sds((len(arrays), rows, LANE), BF16) for rows in cuts],
        arrays,
        after=after,
    )


def copy_body(rows, *refs):
    half = len(refs) // 2
    for (first, count), a_ref, b_ref in zip(rows, refs[:half], refs[half:]):
        b_ref[...] = a_ref[:, first : first + count, :]


def copied(*pieces):
    return call(
        functools.partial(copy_body, [p[1:] for p in pieces]),
        "stack",
        [sds((a.shape[0], count, a.shape[2]), a.dtype) for a, _, count in pieces],
        [p[0] for p in pieces],
    )


def relay_body(*refs):
    pass


def relay(arrays, name="relay"):
    call(relay_body, name, [], [], after=arrays)


def pack_q_body(me_ref, qkv_ref, gains_ref, biases_ref, out_ref, scr):
    per = qkv_ref.shape[2]
    for c in range(3):
        out_ref[c * per : (c + 1) * per, :] = qkv_ref[0, c]
    scr[...] = jnp.zeros_like(scr)
    for l in range(gains_ref.shape[0]):
        for first, ref in ((0, gains_ref), (2, biases_ref)):
            rows = slice(8 * l + first, 8 * l + first + ref.shape[1])
            for lane in range(0, LANE, per):
                scr[rows, lane : lane + per] = ref[l].astype(F32)
    share = lax.broadcasted_iota(jnp.int32, scr.shape, 1) // per
    mine = jnp.where(share == me_ref[1] % (LANE // per), scr[...], 0.0)
    out_ref[3 * per :, :] = mine.astype(BF16)


def pack_q(me, qkv, gains, biases):
    per, rows = qkv.shape[2], 8 * gains.shape[0]
    return call(
        pack_q_body,
        "pack",
        [sds((3 * per + rows, LANE), BF16)],
        [me, qkv, gains, biases],
        smem=1,
        scratch=[pltpu.VMEM((rows, LANE), F32)],
    )[0]


def pack_body(layer, with_q, qkv_ref, gate_ref, out_ref, up_ref, down_ref, shard_ref):
    per = gate_ref.shape[2]
    at = 0
    if with_q:
        for c in range(3):
            shard_ref[at : at + per, :] = qkv_ref[layer, c]
            at += per
    refs = (gate_ref.at[layer, 0], out_ref.at[layer], down_ref.at[layer])
    for ref in refs + (gate_ref.at[layer, 1], up_ref.at[layer]):
        for b in range(ref.shape[1] // LANE):
            shard_ref[at : at + per, :] = ref[:, b * LANE : (b + 1) * LANE]
            at += per


def pack(layer, with_q, w_qkv, w_gate, w_out, w_up, w_down):
    per = w_gate.shape[2]
    cols = 2 * w_gate.shape[3] + w_out.shape[2] + w_up.shape[2] + w_down.shape[2]
    rows = (cols // LANE + 3 * with_q) * per
    return call(
        functools.partial(pack_body, layer, with_q),
        "pack",
        [sds((rows, LANE), BF16)],
        [w_qkv, w_gate, w_out, w_up, w_down],
    )[0]


def finish_body(counts, names, me_ref, *refs):
    ins, outs = refs[: sum(counts)], refs[sum(counts) :]
    d_qkv, d_out, d_gate, d_up, d_down, d_gains, d_norm_biases, d_gate_biases = outs
    per = CHUNK
    at = 0
    for count, pieces in zip(counts, names):
        value = ins[at][...].astype(F32)
        for ref in ins[at + 1 : at + count]:
            value += ref[...].astype(F32)
        at += count
        row = 0
        for name, l in pieces:
            if name == "p":
                low, high = value[row:, :CHUNK], value[row:, CHUNK:]
                value = jnp.where(me_ref[1] % 2 == 0, low, high)
                for i in range(value.shape[0] // 8):
                    for out, first in ((d_gains, 0), (d_norm_biases, 2), (d_gate_biases, 3)):
                        step = 1 if out is d_gains else 2
                        for j in range(2):
                            at_row = 8 * i + first + j * step
                            out[i, j : j + 1, :] = value[at_row : at_row + 1]
                continue
            blocks = {"q": 3, "u": 1 + d_up.shape[2] // LANE, "d": 2 + d_down.shape[2] // LANE}
            for b in range(blocks[name]):
                block = value[row : row + per]
                row += per
                if name == "q":
                    d_qkv[l, b] = block
                elif name == "u" and b == 0:
                    d_gate[l, 1] = block
                elif name == "u":
                    d_up[l, :, (b - 1) * LANE : b * LANE] = block
                elif b == 0:
                    d_gate[l, 0] = block
                elif b == 1:
                    d_out[l] = block
                else:
                    d_down[l, :, (b - 2) * LANE : (b - 1) * LANE] = block


def finish(me, layers, ff_m, groups):
    shapes = [(3, CHUNK, LANE), (CHUNK, LANE), (2, CHUNK, LANE), (CHUNK, ff_m), (CHUNK, ff_m)]
    out = [sds((layers,) + shape, F32) for shape in shapes] + [sds((layers, 2, CHUNK), F32)] * 3
    return call(
        functools.partial(finish_body, [len(g[0]) for g in groups], [g[1] for g in groups]),
        "finish",
        out,
        [me] + [a for g in groups for a in g[0]],
        smem=1,
    )


def solution(mesh):
    dp_size, mp_size, width_size = (mesh.shape[a] for a in ("dp", "mp", "width"))
    all_axes = ("mp", "dp", "width")
    direct = (dp_size, mp_size, width_size) == (2, 4, 4)

    def mp_swap(value, bits):
        return swap(value, "mp", mp_size, bits)

    def dp_swap(value):
        return swap(value, "dp", dp_size, 1)

    def spread(value):
        return [value, mp_swap(value, 1), mp_swap(value, 2)]

    def spread_last(values):
        return values + [mp_swap(values[2], 1)]

    def exchange(own, near, far):
        far = mp_swap(far, 2)
        return [own, mp_swap(near, 1), far, mp_swap(far, 1)]

    def send_width(value):
        return [value] + [swap(value, "width", width_size, k) for k in range(1, width_size)]

    def swap_width(values):
        return [values[0]] + [
            swap(values[k], "width", width_size, k) for k in range(1, width_size)
        ]

    def on_device(
        tokens, segments, cotangent, norm_gains, biases, w_qkv, w_out, w_gate, w_up, w_down
    ):
        ORDER.token = None
        batch, part, model = tokens.shape
        layers = w_qkv.shape[0]
        per = w_qkv.shape[1]
        chunks = model // CHUNK
        half = chunks // 2
        ff_m = w_up.shape[2]
        ff_blocks = ff_m // LANE
        ff = ff_m * mp_size
        me_m = lax.axis_index("mp")
        me_d = lax.axis_index("dp") * width_size + lax.axis_index("width")
        rows = [jnp.where(segments[0, -1] < 0, 0, batch - 1)]
        rows += [batch - 1 - rows[0]] if batch == 2 else []
        me = jnp.stack([me_m, me_d] + rows).astype(jnp.int32)
        me_pack, me_att = me, me
        if not direct:
            me_pack = jnp.stack([0 * me_m, 0 * me_d] + rows).astype(jnp.int32)
            me_att = jnp.stack([me_m, 0 * me_d] + rows).astype(jnp.int32)

        def blocks_of(matrix):
            return jnp.swapaxes(matrix.reshape(per, -1, LANE), 0, 1).reshape(-1, LANE)

        qkv_t, out_t, down_t = (jnp.swapaxes(w, 1, 2) for w in (w_qkv, w_out, w_down))

        def param_block():
            params = jnp.concatenate([norm_gains, biases], axis=1)
            params = jnp.pad(params, ((0, 0), (0, 2), (0, 0))).reshape(layers * 8, per)
            rows = jnp.concatenate([params] * (LANE // per), axis=1)
            share = lax.broadcasted_iota(jnp.int32, rows.shape, 1) // per
            return jnp.where(share == me_d % (LANE // per), rows, 0)

        q_rows, d_rows, u_rows = 3 * CHUNK, (2 + ff_blocks) * CHUNK, (1 + ff_blocks) * CHUNK

        def shard(l, q):
            mats = [w_gate[l, 0], out_t[l], blocks_of(down_t[l]), w_gate[l, 1], blocks_of(w_up[l])]
            return jnp.concatenate(([qkv_t[l].reshape(-1, LANE)] if q else []) + mats, axis=0)

        def gather_whole(shard, extra):
            full = lax.all_gather(shard, all_axes, axis=0, tiled=False)
            if per == CHUNK:
                return full
            count = (shard.shape[0] - extra) // per
            full = full.reshape(mp_size, chunks, CHUNK // per, shard.shape[0], LANE)
            mats = full[:, :, :, : count * per]
            mats = mats.reshape(mp_size, chunks, CHUNK // per, count, per, LANE)
            mats = jnp.swapaxes(mats, 2, 3).reshape(mp_size * chunks, count * CHUNK, LANE)
            if not extra:
                return mats
            pars = jnp.sum(full[:, :, :, count * per :].astype(F32), axis=2).astype(BF16)
            return jnp.concatenate([mats, pars.reshape(mp_size * chunks, extra, LANE)], axis=1)

        def reduce_whole(even, odd):
            full = jnp.stack([even, odd], axis=1)
            full = full.reshape(2, mp_size // 2, half, 2, -1, CHUNK // per, per, LANE)
            full = jnp.transpose(full, (1, 3, 0, 2, 5, 4, 6, 7)).reshape(-1, LANE).astype(F32)
            return lax.psum_scatter(full, all_axes, scatter_dimension=0, tiled=True)

        def reduce_q_whole(grad):
            full = grad.reshape(chunks, -1, CHUNK // per, per, LANE)
            full = jnp.swapaxes(full, 1, 2).reshape(-1, LANE).astype(F32)
            return lax.psum_scatter(full, ("dp", "width"), scatter_dimension=0, tiled=True)

        seg = jnp.where(rows[0] == 0, segments, segments[::-1]) if batch == 2 else segments
        segs = (seg, seg[:, None, :].astype(F32))

        q_all = q_rows + layers * 8
        weights = [None] * layers
        if direct:
            mats = (qkv_t, w_gate, out_t, w_up, down_t)
            q_steps = send_width(pack_q(me, qkv_t, norm_gains, biases))
            t_all = spread(tokens)
            w_steps = send_width(pack(0, False, *mats))
            relay([], "pack")
            (q_base,) = stack(q_steps)
            t_far = copied((t_all[2], 0, part))[0]
            wq = Parts([q_base, dp_swap(q_base)], [(0, 0), (0, 4)], 0, q_all)
            (base,) = stack(w_steps)
            got = {(0, 0): base, (0, 4): dp_swap(base), (2, 0): mp_swap(base, 2)}
            later = send_width(pack(1, True, *mats))
            relay([wq.arrays[1]])
            t_all = t_all + [mp_swap(t_far, 1)]
        else:
            t_all = spread_last(spread(tokens))
            q_sh = jnp.concatenate([qkv_t[0].reshape(-1, LANE), param_block()], axis=0)
            wq = Parts([gather_whole(q_sh, layers * 8)], None, 0, q_all)
            full = gather_whole(shard(0, False), 0)
            wd, wu = Parts([full], None, 0, d_rows), Parts([full], None, d_rows, u_rows)
            for l in range(1, layers):
                full = gather_whole(shard(l, True), 0)
                weights[l] = (
                    Parts([full], None, 0, q_rows),
                    Parts([full], None, q_rows, d_rows),
                    Parts([full], None, q_rows + d_rows, u_rows),
                )

        def last_step(got):
            d_last, u_last = copied((got[2, 0], 0, d_rows), (got[0, 4], d_rows, u_rows))
            return dp_swap(d_last), mp_swap(u_last, 2)

        def two_pieces(got, lasts):
            for m, d in list(got):
                got[m + 1, d] = mp_swap(got[m, d], 1)
            arrays, order = list(got.values()), list(got) + [(2, 4), (3, 4)]
            lasts = copied(*[(a, 0, a.shape[1]) for a in lasts])
            d_all, u_all = (arrays + [a, mp_swap(a, 1)] for a in lasts)
            return (
                Parts(d_all, order, 0, d_rows),
                Parts(u_all, order, [d_rows] * len(arrays) + [0, 0], u_rows),
            )

        x = tokens.reshape(batch * part, model)
        par = None
        saved = []
        t_parts = t_all
        for l in range(layers):
            if l and direct:
                wq = wq_next
            elif l:
                wq, wd, wu = weights[l]
            qkv, lse, own, near, far, *rest = attend(
                me, segs, t_parts, wq, l, layers, l == 0, chunks
            )
            kept = (qkv, lse)
            if l == 0:
                par = rest[0]
                n_parts = [rest[1 + r * mp_size : 1 + (r + 1) * mp_size] for r in range(batch)]
            else:
                n_parts = [t_parts[r::batch] for r in range(batch)]
            o_parts = exchange(own, near, far)
            if direct:
                if l == 0:
                    relay([got[0, 4], got[2, 0]] + later[1:])
                    lasts = last_step(got)
                    relay([o_parts[2]])
                wd, wu = two_pieces(got, lasts)
                if l == 0:
                    q_base, base = stack(later, [q_rows, d_rows + u_rows])
                    wq_next = Parts([q_base, dp_swap(q_base)], [(0, 0), (0, 4)], 0, q_rows)
                    got = {(0, 0): base, (0, 4): dp_swap(base), (2, 0): mp_swap(base, 2)}
                else:
                    wq = wq_next
                weights[l] = (wq, wd, wu)
            elif l == 0:
                weights[0] = (wq, wd, wu)
            n_rows = [n_parts[r][0] for r in range(batch)]
            att, s1, mid, n2, s2, act, slope, out, *following = second(
                me, x, par, n_rows, o_parts, wd, wu, l, chunks, ff, l + 1 < layers
            )
            saved.append((x, n_parts, kept, att, s1, mid, n2, s2, act, slope))
            x = out
            if following:
                t_rows = [spread(n) for n in following]
                if direct:
                    relay([got[0, 4], got[2, 0], wq_next.arrays[1]] + [t[2] for t in t_rows])
                    lasts = last_step(got)
                t_rows = [spread_last(t) for t in t_rows]
                t_parts = [t_rows[r][mx] for mx in range(mp_size) for r in range(batch)]
        output = x.reshape(batch, part, model)

        own = lax.dynamic_slice_in_dim(segments, me_m * part, part, 1)
        g = cotangent.astype(F32) * (own >= 0).astype(F32)[:, :, None]
        g = g.reshape(batch * part, model)
        reduced = [None] * layers
        all_sums = [None] * layers
        moving = {}

        def reduce_2(name, mp_first=False):
            if name in moving:
                keep, send = add(*moving[name], 2)
                moving[name] = (keep, mp_swap(send, 2) if mp_first else dp_swap(send))

        def reduce_3(name, mp_first=False):
            if name in moving:
                keep, send = add(*moving[name], 2, "sum" if mp_first or name == ("d", 0) else "add")
                moving[name] = (keep, dp_swap(send) if mp_first else mp_swap(send, 2))

        def reduce_4(names, sums=None):
            if direct:
                pairs = [moving.pop(name) for name in names]
                moving[names[0]] = swap_width(join(me, pairs, sums, "sum" if names[0][1] == 0 else "add"))

        def reduce_5(name):
            return total(moving.pop(name), "sum" if name[1] == 0 else "add") if direct else None

        for l in reversed(range(layers)):
            wq, wd, wu = weights[l]
            x, n_parts, kept, att, s1, mid, n2, s2, act, slope = saved[l]
            n_rows = [n_parts[r][0] for r in range(batch)]
            final, first_of_two = l == 0, l + 1 < layers
            b2, dcomb, gmid, b1, sums2, *o_parts = second_back(
                me, g, mid, n2, s2, slope, par, wd, wu, l, mp_size, chunks, batch
            )
            d_parts = exchange(*o_parts)
            if first_of_two:
                reduce_4([("q", l + 1), ("u", l + 1)])
            reduce_3(("d", l + 1))
            *grads, local, sums1 = weight_grad(
                me_pack, n2, dcomb, b1, b2, att, act, s1, n_rows, wd, mp_size, chunks,
                final and direct,
            )
            relay([d_parts[2]])
            if direct:
                moving["u", l] = (grads[0], mp_swap(grads[1], 1))
                moving["d", l] = (grads[2], mp_swap(grads[3], 1))
            keeps, gots = [], []
            q_grad = None
            for r in range(batch):
                keep, send, q_grad = attend_back(
                    me_att, *segs, *kept, d_parts, n_parts[r], wq, r, chunks, q_grad
                )
                if r == 0:
                    if first_of_two:
                        reduce_4([("d", l + 1)])
                    reduce_2(("d", l))
                    reduce_2(("u", l), final)
                    if first_of_two:
                        moving["q", l + 1] = [reduce_5(("q", l + 1))] if direct else None
                else:
                    reduce_3(("u", l), final)
                    if final:
                        reduce_3(("d", l))
                keep, send = add(keep, mp_swap(send, 1), 2)
                keeps.append(keep.reshape(keep.shape[1:]))
                gots.append(mp_swap(send, 2).reshape(keep.shape[1:]))
            if direct and first_of_two:
                moving["d", l + 1] = [reduce_5(("d", l + 1))]
            if direct:
                moving["q", l] = (q_grad[:half], dp_swap(q_grad[half:]))
                if final:
                    reduce_4([("u", l)])
            g, all_sums[l] = first_back(me, x, gmid, local, par, sums2, sums1, keeps, gots, l)
            if direct and final:
                reduce_4([("q", l), ("d", l)])
                moving["u", l] = [reduce_5(("u", l))]
            if not direct:
                reduced[l] = (reduce_q_whole(q_grad), reduce_whole(*grads[:2]), reduce_whole(*grads[2:]))
        d_tokens = g.reshape(batch, part, model)
        sums = jnp.concatenate(all_sums, axis=0)
        if direct:
            sums = sums + mp_swap(sums, 1)
            sums = sums + mp_swap(sums, 2)
            sums = sums + dp_swap(sums)
            moving["p", 0] = swap_width(join(me, [], sums))
            groups = [
                (moving["q", 1], [("q", 1), ("u", 1)]),
                (moving["d", 1], [("d", 1)]),
                (moving["u", 0], [("u", 0)]),
                (moving["q", 0], [("q", 0), ("d", 0)]),
                (moving["p", 0], [("p", 0)]),
            ]
            stacked = finish(me, layers, ff_m, groups)
            stacked, small = stacked[:5], stacked[5:]
        else:
            params = lax.dynamic_slice_in_dim(lax.psum(sums, all_axes), me_d * per, per, 1)
            params = params.reshape(layers, 8, per)
            small = [params[:, 0:2], params[:, 2:6:2], params[:, 3:6:2]]

        def unblocks(rows, count):
            return jnp.swapaxes(rows.reshape(count, per, LANE), 0, 1).reshape(per, count * LANE)

        if not direct:
            grads = []
            for q_sum, up_sum, down_sum in reduced:
                grads.append(
                    (
                        q_sum.reshape(3, per, LANE),
                        down_sum[per : 2 * per],
                        jnp.stack([down_sum[:per], up_sum[:per]]),
                        unblocks(up_sum[per:], ff_blocks),
                        unblocks(down_sum[2 * per :], ff_blocks),
                    )
                )
            stacked = [jnp.stack([grads[l][i] for l in range(layers)]) for i in range(5)]
        for i in (0, 1, 4):
            stacked[i] = jnp.swapaxes(stacked[i], 1, 2)
        return (
            output,
            d_tokens,
            *small,
            *stacked,
        )

    placed = (
        P(("dp", "width"), "mp", None),
        P(("dp", "width"), None),
        P(("dp", "width"), "mp", None),
        P(None, None, ("dp", "width")),
        P(None, None, ("dp", "width")),
        P(None, ("dp", "width"), None, "mp"),
        P(None, "mp", ("dp", "width")),
        P(None, None, ("dp", "width"), "mp"),
        P(None, ("dp", "width"), "mp"),
        P(None, "mp", ("dp", "width")),
    )
    return jax.shard_map(
        on_device,
        mesh=mesh,
        in_specs=placed,
        out_specs=(
            placed[0],
            placed[0],
            placed[3],
            placed[3],
            placed[3],
            placed[5],
            placed[6],
            placed[7],
            placed[8],
            placed[9],
        ),
        check_vma=False,
    )
```

```python
import functools

import jax
import jax.numpy as jnp
from jax import lax
from jax.experimental import pallas as pl
from jax.experimental.pallas import tpu as pltpu
from jax.sharding import PartitionSpec as P

HEAD_DIM = 64
LANE = 128
NORM_EPS = 1e-05
SPAN = 256
CHUNK = 64

VALUES_MB = {
    "attend": 6,
    "second": 10,
    "second_back": 10,
    "attend_back": 8,
    "first_back": 6,
    "weight_grad": 8,
    "relay": 1,
    "sum": 2,
    "stack": 2,
    "add": 2,
    "pack": 2,
    "finish": 4,
}

KERNEL_US = {
    "attend": 8,
    "second": 12,
    "second_back": 10,
    "attend_back": 9,
    "first_back": 4,
    "weight_grad": 8,
    "relay": 1,
    "sum": 0.1,
    "stack": 0.1,
    "add": 1,
    "pack": 10,
    "finish": 2,
}

F32 = jnp.float32
BF16 = jnp.bfloat16


def nn(a, b):
    return jnp.dot(a, b, preferred_element_type=F32)


def nt(a, b):
    return lax.dot_general(a, b, (((1,), (1,)), ((), ())), preferred_element_type=F32)


def tn(a, b):
    return lax.dot_general(a, b, (((0,), (0,)), ((), ())), preferred_element_type=F32)


def sds(shape, dtype):
    return jax.ShapeDtypeStruct(shape, dtype)


class Late:
    def __init__(self, array):
        self.array = array


class Copies:
    def __init__(self, pairs, first_out, sems):
        self.first_out = first_out
        self.all = [
            (ref, pltpu.make_async_copy(*pair, sems.at[i]))
            for i, (ref, *pair) in enumerate(pairs)
        ]
        self.waiting = []
        self.unsent = list(self.all[first_out:])
        for ref, copy in self.all[:first_out]:
            copy.start()
            self.waiting.append((ref, copy))

    def need(self, *refs):
        for ref in refs:
            for i, entry in enumerate(self.waiting):
                if entry[0] is ref:
                    entry[1].wait()
                    del self.waiting[i]
                    break

    def send(self, *refs):
        for ref in refs:
            for i, entry in enumerate(self.unsent):
                if entry[0] is ref:
                    entry[1].start()
                    del self.unsent[i]
                    break

    def finish(self):
        for _, copy in self.waiting:
            copy.wait()
        for _, copy in self.unsent:
            copy.start()
        for _, copy in self.all[self.first_out :]:
            copy.wait()


class Chain:
    def __init__(self):
        self.token = None
        self.copies = None


ORDER = Chain()


def need(*refs):
    ORDER.copies.need(*refs)


def send(*refs):
    ORDER.copies.send(*refs)


def in_hbm(a):
    return pltpu.with_memory_space_constraint(a, pltpu.HBM)


def size_of(a):
    return a.size * a.dtype.itemsize


def call(body, name, out_shape, args, smem=0, parts=(), scratch=(), after=()):
    after = list(after) + ([] if ORDER.token is None else [ORDER.token])
    late_in = [i for i, a in enumerate(args) if isinstance(a, Late)]
    late_out = [i for i, o in enumerate(out_shape) if isinstance(o, Late)]
    args = [in_hbm(a.array) if isinstance(a, Late) else a for a in args]
    out_shape = [o.array if isinstance(o, Late) else o for o in out_shape]
    parts = [in_hbm(a) for a in parts]
    hbm, vmem = (pl.BlockSpec(memory_space=space) for space in (pltpu.HBM, pltpu.VMEM))
    specs = [pl.BlockSpec(memory_space=pltpu.SMEM)] * smem
    specs += [hbm if i in late_in else vmem for i in range(smem, len(args))]
    specs += [hbm] * len(parts)
    specs += [pl.BlockSpec(memory_space=pl.ANY)] * len(after)
    used = len(args) + len(parts)
    given = used + len(after)
    outs = len(out_shape)
    late = [args[i] for i in late_in] + [out_shape[i] for i in late_out]
    room = [pltpu.VMEM(a.shape, a.dtype) for a in late]
    sems = [pltpu.SemaphoreType.DMA((len(late),))] if late else []

    def inner(*refs):
        ins, results = list(refs[:used]), list(refs[given : given + outs])
        rest = refs[given + outs + 1 :]
        own = rest[: len(scratch)]
        places = rest[len(scratch) : len(scratch) + len(late)]
        pairs = []
        for i, place in zip(late_in, places):
            pairs.append((place, ins[i], place))
            ins[i] = place
        for i, place in zip(late_out, places[len(late_in) :]):
            pairs.append((place, place, results[i]))
            results[i] = place
        copies = ORDER.copies = Copies(pairs, len(late_in), rest[-1] if late else None)
        body(*ins, *results, *own)
        copies.finish()

    nbytes = sum(size_of(a) for a in args + out_shape)
    for s in scratch:
        if hasattr(s, "shape") and len(s.shape) > 1:
            nbytes += size_of(jax.ShapeDtypeStruct(s.shape, s.dtype))
    *result, ORDER.token = pl.pallas_call(
        inner,
        name=name,
        out_shape=[
            pltpu.HBM(o.shape, o.dtype) if i in late_out else o for i, o in enumerate(out_shape)
        ]
        + [sds((8, LANE), F32)],
        in_specs=specs,
        out_specs=[hbm if i in late_out else vmem for i in range(outs)]
        + [pl.BlockSpec(memory_space=pl.ANY)],
        scratch_shapes=list(scratch) + room + sems,
        cost_estimate=pl.CostEstimate(
            flops=int(5 * KERNEL_US[name] * 1.1e9),
            bytes_accessed=int(5 * KERNEL_US[name] * 3.6e6),
            transcendentals=0,
        ),
        compiler_params=pltpu.CompilerParams(
            vmem_limit_bytes=int(1.02 * nbytes) + VALUES_MB[name] * 2**20
        ),
    )(*args, *parts, *after)
    return result


def col(start):
    return pl.multiple_of(start, LANE)


class Parts:
    def __init__(self, arrays, order, first_rows, rows):
        self.arrays = arrays
        self.order = order
        self.first_rows = first_rows if isinstance(first_rows, list) else [first_rows] * len(arrays)
        self.rows = rows

    def open(self, refs, me_ref, dst, sem, chunks, own_only=False):
        if self.order is None:
            rows = pl.ds(self.first_rows[0], self.rows)
            src = refs[0].at[:, rows, :]
            if own_only:
                src = refs[0].at[pl.ds(me_ref[0] * chunks, chunks), rows, :]
            pltpu.make_async_copy(src, dst, sem).start()
            return Blocks(dst, sem, chunks, 0, 0)
        for ref, first_row, (mx, dx) in zip(refs, self.first_rows, self.order):
            rows = pl.ds(first_row, self.rows)
            at = pl.ds((0 if own_only else mx * chunks) + dx, ref.shape[0])
            pltpu.make_async_copy(ref.at[:, rows, :], dst.at[at], sem).start()
        return Blocks(dst, sem, chunks, 0 if own_only else me_ref[0], me_ref[1])


def others(wd, wu):
    return [a for a in wu.arrays if not any(a is b for b in wd.arrays)]


def shared(wd, wu, d_refs, refs):
    more = iter(refs)
    found, count = [], 0
    for a in wu.arrays:
        at = [i for i, b in enumerate(wd.arrays) if a is b]
        count += not at
        found.append(d_refs[at[0]] if at else next(more))
    return found, refs[count:]


class Blocks:
    def __init__(self, ref, sem, chunks, turn_m, turn_d):
        self.ref, self.sem, self.chunks = ref, sem, chunks
        self.turn_m, self.turn_d = turn_m, turn_d

    def wait(self):
        pltpu.make_async_copy(self.ref, self.ref, self.sem).wait()

    def place(self, m, d):
        if isinstance(self.turn_d, int):
            return m * self.chunks + d
        return jnp.bitwise_xor(m, self.turn_m) * self.chunks + jnp.bitwise_xor(d, self.turn_d)

    def block(self, m, b, lo=0, hi=None):
        rows = pl.ds(b * CHUNK, CHUNK)
        hi = self.chunks if hi is None else hi
        return jnp.concatenate([self.ref[self.place(m, d), rows, :] for d in range(lo, hi)], axis=0)

    def wide(self, which, lo=0, hi=None):
        return jnp.concatenate([self.block(m, b, lo, hi) for m, b in which], axis=1)

    def params(self, first_row, layer):
        rows = slice(first_row + 8 * layer, first_row + 8 * layer + 8)
        share = LANE // CHUNK
        tiles = []
        for i in range(self.chunks // share):
            tile = self.ref[self.place(0, i * share), rows, :].astype(F32)
            for j in range(1, share):
                tile += self.ref[self.place(0, i * share + j), rows, :].astype(F32)
            tiles.append(tile)
        return jnp.concatenate(tiles, axis=1)


def norm_parts(x):
    mean = jnp.mean(x, axis=1, keepdims=True)
    centred = x - mean
    rstd = lax.rsqrt(jnp.mean(centred * centred, axis=1, keepdims=True) + NORM_EPS)
    return centred * rstd, rstd


def sigmoid(v):
    return 1.0 / (1.0 + jnp.exp(-v))


def rows_at(me_ref, at, part):
    return pl.ds(pl.multiple_of(me_ref[2 + at] * part, part), part)


def seg_bounds(seg_ref, row, q_at, q_spans):
    first_id = seg_ref[row, q_at * SPAN]
    first_id = jnp.where(first_id < 0, 1 << 20, first_id)
    low = jnp.int32(0)
    for kb in range(q_spans - 1):
        last_id = seg_ref[row, (kb + 1) * SPAN - 1]
        last_id = jnp.where(last_id < 0, 1 << 20, last_id)
        low += jnp.where((kb < q_at) & (last_id < first_id), 1, 0)
    return low


def allowed_t(segc_ref, segr_ref, row, k0, q0, spans):
    keys = spans * SPAN
    seg_k = segc_ref[pl.ds(k0, keys), :]
    seg_q = segr_ref[row, :, pl.ds(q0, SPAN)]
    same = jnp.concatenate([seg_k == seg_q[:, :LANE], seg_k == seg_q[:, LANE:]], axis=1)
    tri = lax.broadcasted_iota(jnp.int32, (SPAN, SPAN), 0) <= (
        lax.broadcasted_iota(jnp.int32, (SPAN, SPAN), 1)
    )
    if spans == 1:
        return same & tri
    return jnp.concatenate([same[: keys - SPAN], same[keys - SPAN :] & tri], axis=0)


def attend_body(
    wq, layer, norm_here, mp_size, chunks, batch, me_ref, seg_ref, segr_ref, *refs
):
    given = mp_size if norm_here else mp_size * batch
    t_refs, refs = refs[:given], refs[given:]
    w_refs, refs = refs[: len(wq.arrays)], refs[len(wq.arrays) :]
    qkv_ref, lse_ref = refs[:2]
    o_refs, refs = [refs[2], refs[3], refs[4].at[0], refs[4].at[1]], refs[5:]
    if norm_here:
        par_ref, n_refs, refs = refs[0], refs[1 : 1 + mp_size * batch], refs[1 + mp_size * batch :]
    w_scr, o_scr, segc_ref, sem = refs
    part = o_refs[0].shape[1]
    me_m = me_ref[0]
    w = wq.open(w_refs, me_ref, w_scr, sem, chunks, own_only=True)
    w.wait()
    if norm_here:
        for l in range(par_ref.shape[0]):
            par_ref[l] = w.params(3 * CHUNK, l)
    weights = w.wide([(0, 0), (0, 1), (0, 2)])
    q_spans = qkv_ref.shape[1] // SPAN
    for r in range(batch):
        for mx in range(mp_size):
            at = pl.ds(pl.multiple_of(jnp.bitwise_xor(me_m, mx) * part, part), part)
            if norm_here:
                xhat, _ = norm_parts(t_refs[mx][me_ref[2 + r]].astype(F32))
                n = (xhat * par_ref[layer, 0:1] + par_ref[layer, 2:3]).astype(BF16)
                n_refs[r * mp_size + mx][...] = n
                send(n_refs[r * mp_size + mx])
            else:
                n = t_refs[mx * batch + r][...]
            qkv_ref[r, at, :] = nn(n, weights).astype(BF16)
    send(qkv_ref)

    for r in range(batch):
        length = qkv_ref.shape[1]
        segc_ref[pl.ds(r * length, length), :] = jnp.broadcast_to(segr_ref[r], (LANE, length)).T

    def step(i, carry):
        r, q_at = i // q_spans, i % q_spans
        low = seg_bounds(seg_ref, r, q_at, q_spans)
        q0 = pl.multiple_of(q_at * SPAN, SPAN)
        k0 = pl.multiple_of(low * SPAN, SPAN)
        k_abs = pl.multiple_of((r * q_spans + low) * SPAN, SPAN)
        for spans in range(1, q_spans + 1):

            @pl.when(q_at - low + 1 == spans)
            def _():
                keys = spans * SPAN
                mask = allowed_t(segc_ref, segr_ref, r, k_abs, q0, spans)
                outs = []
                for h in range(2):
                    lo = h * HEAD_DIM
                    q = qkv_ref[r, pl.ds(q0, SPAN), lo : lo + HEAD_DIM] * jnp.asarray(
                        HEAD_DIM**-0.5, BF16
                    )
                    k = qkv_ref[r, pl.ds(k0, keys), 128 + lo : 128 + lo + HEAD_DIM]
                    v = qkv_ref[r, pl.ds(k0, keys), 256 + lo : 256 + lo + HEAD_DIM]
                    s = jnp.where(mask, nt(k, q), -1e30)
                    top = jnp.max(s, axis=0, keepdims=True)
                    p = jnp.exp(s - top)
                    total = jnp.sum(p, axis=0, keepdims=True)
                    lse_ref[r * 2 + h, :, pl.ds(q0, SPAN)] = top + jnp.log(total)
                    outs.append(tn(v, p.astype(BF16)) / total)
                o_scr[r, pl.ds(q0, SPAN), :] = jnp.concatenate(outs, axis=0).T.astype(BF16)

        return carry

    lax.fori_loop(0, batch * q_spans, step, 0)
    for mx in range(mp_size):
        at = pl.multiple_of(jnp.bitwise_xor(me_m, mx) * part, part)
        for r in range(batch):
            o_refs[mx][r] = o_scr[r, pl.ds(at, part), :]


def attend(me, segs, t_parts, wq, layer, layers, norm_here, chunks):
    seg, segr = segs
    batch, length = seg.shape
    mp_size = 4
    part, model = t_parts[0].shape[-2:]
    out = [sds((batch, length, 384), BF16), sds((batch * 2, 1, length), F32)]
    if norm_here:
        out = [Late(o) for o in out]
    out += [sds((batch, part, LANE), BF16)] * 2 + [sds((2, batch, part, LANE), BF16)]
    if norm_here:
        out += [sds((layers, 8, model), F32)] + [Late(sds((part, model), BF16))] * mp_size * batch
    return call(
        functools.partial(attend_body, wq, layer, norm_here, mp_size, chunks, batch),
        "attend",
        out,
        [me, seg, segr] + t_parts,
        smem=2,
        parts=wq.arrays,
        scratch=[
            pltpu.VMEM((chunks, wq.rows, LANE), BF16),
            pltpu.VMEM((batch, length, LANE), BF16),
            pltpu.VMEM((batch * length, LANE), F32),
            pltpu.SemaphoreType.DMA,
        ],
    )


def second_body(
    wd, wu, layer, mp_size, chunks, batch, has_next, me_ref, x_ref, par_ref, *refs
):
    n_refs, refs = refs[:batch], refs[batch:]
    t_refs, refs = refs[:mp_size], refs[mp_size:]
    t_refs = [t_refs[0], t_refs[1], t_refs[2].at[0], t_refs[3].at[1]]
    d_refs, refs = refs[: len(wd.arrays)], refs[len(wd.arrays) :]
    u_refs, refs = shared(wd, wu, d_refs, refs)
    att_ref, s1_ref, mid_ref, n2_ref, s2_ref, act_ref, slope_ref, out_ref = refs[:8]
    refs = refs[8:]
    if has_next:
        next_refs, refs = refs[:batch], refs[batch:]
    n_scr, d_scr, u_scr, d_sem, u_sem = refs
    w_d = wd.open(d_refs, me_ref, d_scr, d_sem, chunks)
    w_u = wu.open(u_refs, me_ref, u_scr, u_sem, chunks)
    me_m = me_ref[0]
    part = n_refs[0].shape[0]
    par = par_ref.at[layer]
    for r in range(batch):
        for mx in range(mp_size):
            m = jnp.bitwise_xor(me_m, mx)
            att_ref[rows_at(me_ref, r, part), pl.ds(col(m * LANE), LANE)] = t_refs[mx][r]
    send(att_ref)
    need(*n_refs)
    for r in range(batch):
        n_scr[rows_at(me_ref, r, part), :] = n_refs[r][...]
    n = n_scr[...]
    every = range(mp_size)
    w_d.wait()
    s1 = sigmoid(nn(n, w_d.wide([(m, 0) for m in every])) + par[3:4])
    s1_ref[...] = s1
    send(s1_ref)
    need(x_ref)
    mid = (
        x_ref[...].astype(F32)
        + nt(att_ref[...], w_d.wide([(m, 1) for m in every]))
        + s1 * n.astype(F32)
    )
    mid_ref[...] = mid
    send(mid_ref)
    xhat, _ = norm_parts(mid)
    n2_ref[...] = (xhat * par[1:2] + par[4:5]).astype(BF16)
    send(n2_ref)
    w_u.wait()
    s2_ref[...] = sigmoid(nn(n2_ref[...], w_u.wide([(m, 0) for m in every])) + par[5:6])
    send(s2_ref)
    ff_blocks = act_ref.shape[1] // (mp_size * LANE)
    for m in every:
        for b in range(0, ff_blocks, 2):
            at = (m * ff_blocks + b) * LANE
            cols = slice(at, at + 2 * LANE)
            hidden = nn(n2_ref[...], w_u.wide([(m, 1 + b), (m, 2 + b)]))
            square = hidden * hidden
            inner = 0.7978845608 + (0.7978845608 * 0.044715) * square
            th = jnp.tanh(hidden * inner)
            half = 0.5 + 0.5 * th
            act = hidden * half
            act_ref[:, cols] = act.astype(BF16)
            slope = half + act * (1.0 - th) * (3.0 * inner - 2 * 0.7978845608)
            slope_ref[:, cols] = slope.astype(BF16)
    send(act_ref, slope_ref)
    share = chunks // 2
    for j in range(2):
        cols = slice(j * share * CHUNK, (j + 1) * share * CHUNK)
        down = [(m, 2 + b) for m in every for b in range(ff_blocks)]
        out_ref[:, cols] = (
            mid_ref[:, cols]
            + s2_ref[:, cols] * n2_ref[:, cols].astype(F32)
            + nt(act_ref[...], w_d.wide(down, j * share, (j + 1) * share))
        )
    send(out_ref)
    if has_next:
        xhat, _ = norm_parts(out_ref[...])
        n_scr[...] = (xhat * par_ref[layer + 1, 0:1] + par_ref[layer + 1, 2:3]).astype(BF16)
        for r in range(batch):
            next_refs[r][...] = n_scr[rows_at(me_ref, r, part), :]


def second(me, x, par, n_rows, t_parts, wd, wu, layer, chunks, ff, has_next, after=()):
    rows, model = x.shape
    mp_size = len(t_parts)
    out = [
        sds((rows, model), BF16),
        sds((rows, model), F32),
        sds((rows, model), F32),
        sds((rows, model), BF16),
        sds((rows, model), F32),
        sds((rows, ff), BF16),
        sds((rows, ff), BF16),
        sds((rows, model), F32),
    ]
    out = [Late(o) for o in out]
    if has_next:
        out += [sds(n_rows[0].shape, BF16)] * len(n_rows)
    return call(
        functools.partial(
            second_body, wd, wu, layer, mp_size, chunks, len(n_rows), has_next
        ),
        "second",
        out,
        [me, Late(x), par] + [Late(n) for n in n_rows] + t_parts,
        smem=1,
        parts=wd.arrays + others(wd, wu),
        scratch=[
            pltpu.VMEM((rows, model), BF16),
            pltpu.VMEM((chunks * mp_size, wd.rows, LANE), BF16),
            pltpu.VMEM((chunks * mp_size, wu.rows, LANE), BF16),
            pltpu.SemaphoreType.DMA,
            pltpu.SemaphoreType.DMA,
        ],
        after=after,
    )


def norm_back(x, gain, d_normed):
    xhat, rstd = norm_parts(x)
    e = d_normed * gain
    mean_e = jnp.mean(e, axis=1, keepdims=True)
    mean_ex = jnp.mean(e * xhat, axis=1, keepdims=True)
    d_gain = jnp.sum(d_normed * xhat, axis=0, keepdims=True)
    d_bias = jnp.sum(d_normed, axis=0, keepdims=True)
    return (e - mean_e - xhat * mean_ex) * rstd, d_gain, d_bias


def second_back_body(
    wd, wu, layer, mp_size, chunks, batch, me_ref, g_ref, mid_ref, n2_ref, s2_ref, slope_ref,
    par_ref, *refs, before=None
):
    d_refs, refs = refs[: len(wd.arrays)], refs[len(wd.arrays) :]
    u_refs, refs = shared(wd, wu, d_refs, refs)
    b2_ref, dcomb_ref, gmid_ref, b1_ref, sums_ref = refs[:5]
    refs = refs[5:]
    o_refs, refs = [refs[0], refs[1], refs[2].at[0], refs[2].at[1]], refs[3:]
    o_scr, d_scr, u_scr, d_sem, u_sem = refs
    w_d = wd.open(d_refs, me_ref, d_scr, d_sem, chunks)
    if before is not None:
        before()
    ff = slope_ref.shape[1]
    model = g_ref.shape[1]
    ff_m = ff // mp_size
    ff_blocks = ff_m // LANE
    stride = LANE + ff_m
    part = g_ref.shape[0] // batch
    me_m = me_ref[0]
    every = range(mp_size)
    g = g_ref[...]
    b2_ref[...] = g.astype(BF16)
    need(n2_ref, s2_ref)
    s2 = s2_ref[...]
    b2f = b2_ref[...].astype(F32)
    d_z2 = (b2f * n2_ref[...].astype(F32) * s2 * (1.0 - s2)).astype(BF16)
    sums_ref[2:3, :] = jnp.sum(d_z2.astype(F32), axis=0, keepdims=True)
    for m in every:
        dcomb_ref[:, m * stride : m * stride + LANE] = d_z2[:, m * LANE : (m + 1) * LANE]
    w_d.wait()
    w_u = wu.open(u_refs, me_ref, u_scr, u_sem, chunks)
    need(slope_ref)
    for m in every:
        for b in range(0, ff_blocks, 2):
            at = m * ff_m + b * LANE
            d_act = nn(b2_ref[...], w_d.wide([(m, 2 + b), (m, 3 + b)]))
            slope = slope_ref[:, at : at + 2 * LANE].astype(F32)
            at = m * stride + (1 + b) * LANE
            dcomb_ref[:, at : at + 2 * LANE] = (d_act * slope).astype(BF16)
    w_u.wait()
    share = chunks // 2
    cols_of = [(m, b) for m in every for b in range(1 + ff_blocks)]
    for j in range(2):
        cols = slice(j * share * CHUNK, (j + 1) * share * CHUNK)
        gmid_ref[:, cols] = b2_ref[:, cols].astype(F32) * s2_ref[:, cols] + nt(
            dcomb_ref[...], w_u.wide(cols_of, j * share, (j + 1) * share)
        )
    need(mid_ref)
    d_mid, d_gain, d_bias = norm_back(mid_ref[...], par_ref[layer, 1:2], gmid_ref[...])
    sums_ref[0:1, :] = d_gain
    sums_ref[1:2, :] = d_bias
    sums_ref[3:8, :] = jnp.zeros((5, model), F32)
    g_mid = g_ref[...] + d_mid
    gmid_ref[...] = g_mid
    b1_ref[...] = g_mid.astype(BF16)
    for mx in every:
        m = jnp.bitwise_xor(me_m, mx)
        o_scr[...] = nn(b1_ref[...], w_d.block(m, 1)).astype(BF16)
        for r in range(batch):
            o_refs[mx][r] = o_scr[rows_at(me_ref, r, part), :]


def second_back(me, g, mid, n2, s2, slope, par, wd, wu, layer, mp_size, chunks, batch, after=()):
    rows, model = g.shape
    ff = slope.shape[1]
    out = [
        sds((rows, model), BF16),
        sds((rows, ff + LANE * mp_size), BF16),
        sds((rows, model), F32),
        sds((rows, model), BF16),
        sds((8, model), F32),
    ]
    out += [sds((batch, rows // batch, LANE), BF16)] * 2
    out += [sds((2, batch, rows // batch, LANE), BF16)]
    return call(
        functools.partial(second_back_body, wd, wu, layer, mp_size, chunks, batch),
        "second_back",
        out,
        [me, g, Late(mid), Late(n2), Late(s2), Late(slope), par],
        smem=1,
        parts=wd.arrays + others(wd, wu),
        scratch=[
            pltpu.VMEM((rows, LANE), BF16),
            pltpu.VMEM((chunks * mp_size, wd.rows, LANE), BF16),
            pltpu.VMEM((chunks * mp_size, wu.rows, LANE), BF16),
            pltpu.SemaphoreType.DMA,
            pltpu.SemaphoreType.DMA,
        ],
        after=after,
    )


def attend_back_body(wq, row, mp_size, chunks, last, me_ref, seg_ref, segr_ref, *refs):
    qkv_ref, lse_ref = refs[:2]
    d_in, refs = refs[2 : 2 + mp_size], refs[2 + mp_size :]
    d_in = [d_in[0].at[row], d_in[1].at[row], d_in[2].at[0, row], d_in[3].at[1, row]]
    n_refs, refs = refs[:mp_size], refs[mp_size:]
    if last:
        before_ref, refs = refs[0], refs[1:]
    w_refs, refs = refs[: len(wq.arrays)], refs[len(wq.arrays) :]
    keep_ref, send_ref, dw_ref = refs[:3]
    w_scr, do_scr, dqkv_scr, dk_scr, dv_scr, segc_ref, sem = refs[3:]
    w = wq.open(w_refs, me_ref, w_scr, sem, chunks, own_only=True)
    length = qkv_ref.shape[1]
    part = d_in[0].shape[0]
    me_m, me_d = me_ref[0], me_ref[1]
    for mx in range(mp_size):
        at = pl.multiple_of(jnp.bitwise_xor(me_m, mx) * part, part)
        do_scr[pl.ds(at, part), :] = d_in[mx][...]
    dqkv_scr[...] = jnp.zeros_like(dqkv_scr)
    dk_scr[...] = jnp.zeros_like(dk_scr)
    segc_ref[...] = jnp.broadcast_to(segr_ref[row], (LANE, length)).T
    dv_scr[...] = jnp.zeros_like(dv_scr)
    q_spans = length // SPAN

    def step(q_at, carry):
        low = seg_bounds(seg_ref, row, q_at, q_spans)
        real = seg_ref[row, q_at * SPAN] >= 0
        q0 = pl.multiple_of(q_at * SPAN, SPAN)
        k0 = pl.multiple_of(low * SPAN, SPAN)
        for spans in range(1, q_spans + 1):

            @pl.when(real & (q_at - low + 1 == spans))
            def _():
                keys = spans * SPAN
                mask = allowed_t(segc_ref, segr_ref, row, k0, q0, spans)
                dqs, dks, dvs = [], [], []
                for h in range(2):
                    lo = h * HEAD_DIM
                    q = qkv_ref[row, pl.ds(q0, SPAN), lo : lo + HEAD_DIM] * jnp.asarray(
                        HEAD_DIM**-0.5, BF16
                    )
                    k = qkv_ref[row, pl.ds(k0, keys), 128 + lo : 128 + lo + HEAD_DIM]
                    v = qkv_ref[row, pl.ds(k0, keys), 256 + lo : 256 + lo + HEAD_DIM]
                    do = do_scr[pl.ds(q0, SPAN), lo : lo + HEAD_DIM]
                    lse = lse_ref[row * 2 + h, :, pl.ds(q0, SPAN)]
                    p = jnp.where(mask, jnp.exp(nt(k, q) - lse), 0.0)
                    dvs.append(nn(p.astype(BF16), do))
                    dp = nt(v, do)
                    delta = jnp.sum(p * dp, axis=0, keepdims=True)
                    ds = (p * (dp - delta)).astype(BF16)
                    dks.append(nn(ds, q))
                    dqs.append(tn(k, ds))
                dqkv_scr[pl.ds(q0, SPAN), 0:128] = (
                    jnp.concatenate(dqs, axis=0).T * HEAD_DIM**-0.5
                ).astype(BF16)
                dk_scr[pl.ds(k0, keys), :] += jnp.concatenate(dks, axis=1)
                dv_scr[pl.ds(k0, keys), :] += jnp.concatenate(dvs, axis=1)

        return carry

    lax.fori_loop(0, q_spans, step, 0)
    dqkv_scr[:, 128:256] = dk_scr[...].astype(BF16)
    dqkv_scr[:, 256:384] = dv_scr[...].astype(BF16)
    w.wait()
    weights = w.wide([(0, 0), (0, 1), (0, 2)])
    need(*n_refs)
    grad = jnp.zeros((n_refs[0].shape[1], 384), F32)
    if last:
        grad = before_ref[...]
    for mx in range(mp_size):
        at = pl.multiple_of(jnp.bitwise_xor(me_m, mx) * part, part)
        d_here = dqkv_scr[pl.ds(at, part), :]
        d_n = nt(d_here, weights).astype(BF16)
        (send_ref if mx % 2 else keep_ref)[mx // 2] = d_n
        grad += tn(n_refs[mx][...], d_here)
    if not last:
        dw_ref[...] = grad
        return
    grad = grad.astype(BF16)
    for d in range(chunks):
        for b in range(3):
            dw_ref[jnp.bitwise_xor(d, me_d), b * CHUNK : (b + 1) * CHUNK, :] = grad[
                d * CHUNK : (d + 1) * CHUNK, b * LANE : (b + 1) * LANE
            ]


def attend_back(
    me, seg, segr, qkv, lse, d_parts, n_parts, wq, row, chunks, before=None, after=()
):
    mp_size = len(d_parts)
    length = seg.shape[1]
    part, model = n_parts[0].shape
    last = before is not None
    out = [sds((mp_size // 2, part, model), BF16)] * 2
    out += [sds((chunks, 3 * CHUNK, LANE), BF16) if last else sds((model, 384), F32)]
    return call(
        functools.partial(attend_back_body, wq, row, mp_size, chunks, last),
        "attend_back",
        out,
        [me, seg, segr, qkv, lse]
        + d_parts
        + [Late(n) for n in n_parts]
        + ([before] if last else []),
        smem=2,
        parts=wq.arrays,
        scratch=[
            pltpu.VMEM((chunks, wq.rows, LANE), BF16),
            pltpu.VMEM((length, LANE), BF16),
            pltpu.VMEM((length, 384), BF16),
            pltpu.VMEM((length, LANE), F32),
            pltpu.VMEM((length, LANE), F32),
            pltpu.VMEM((length, LANE), F32),
            pltpu.SemaphoreType.DMA,
        ],
        after=after,
    )


def first_back_body(
    layer, batch, me_ref, x_ref, gmid_ref, local_ref, par_ref, sums2_ref, sums1_ref, *refs
):
    kept, got = refs[:batch], refs[batch : 2 * batch]
    g_ref, sums_ref = refs[2 * batch :]
    part = kept[0].shape[0]
    for r in range(batch):
        at = rows_at(me_ref, r, part)
        g_ref[at, :] = local_ref[at, :] + kept[r][...].astype(F32) + got[r][...].astype(F32)
    need(x_ref)
    d_x, d_gain, d_bias = norm_back(x_ref[...].astype(F32), par_ref[layer, 0:1], g_ref[...])
    g_ref[...] = gmid_ref[...] + d_x
    sums_ref[0:1, :] = d_gain
    sums_ref[1:2, :] = sums2_ref[0:1, :]
    sums_ref[2:3, :] = d_bias
    sums_ref[3:4, :] = sums1_ref[0:1, :]
    sums_ref[4:5, :] = sums2_ref[1:2, :]
    sums_ref[5:6, :] = sums2_ref[2:3, :]
    sums_ref[6:8, :] = sums2_ref[6:8, :]


def first_back(me, x, gmid, local, par, sums2, sums1, kept, got, layer, after=()):
    rows, model = x.shape
    return call(
        functools.partial(first_back_body, layer, len(kept)),
        "first_back",
        [sds((rows, model), F32), sds((8, model), F32)],
        [me, Late(x), gmid, local, par, sums2, sums1] + kept + got,
        smem=1,
        after=after,
    )


def turn_body(wd, wu, layer, mp_size, chunks, batch, me_ref, *refs):
    count = 6 + 2 * batch
    upper, refs = refs[:count], refs[count:]
    lower, refs = refs[:4], refs[4:]
    arrays = len(wd.arrays) + len(others(wd, wu))
    parts, refs = refs[:arrays], refs[arrays:]
    sums_ref, refs = refs[0], refs[1:]
    g_scr, rest = refs[-6], refs[:-6] + refs[-5:]

    def before():
        first_back_body(layer + 1, batch, me_ref, *upper, g_scr, sums_ref)

    second_back_body(
        wd, wu, layer, mp_size, chunks, batch, me_ref, g_scr, *lower, upper[3], *parts, *rest,
        before=before,
    )


def turn(me, upper, kept, got, lower, wd, wu, layer, mp_size, chunks):
    x, gmid, local, par, sums2, sums1 = upper
    mid, n2, s2, slope = lower
    batch = len(kept)
    rows, model = x.shape
    ff = slope.shape[1]
    out = [
        sds((8, model), F32),
        sds((rows, model), BF16),
        sds((rows, ff + LANE * mp_size), BF16),
        sds((rows, model), F32),
        sds((rows, model), BF16),
        sds((8, model), F32),
    ]
    out += [sds((batch, rows // batch, LANE), BF16)] * 2
    out += [sds((2, batch, rows // batch, LANE), BF16)]
    return call(
        functools.partial(turn_body, wd, wu, layer, mp_size, chunks, batch),
        "second_back",
        out,
        [me, Late(x), gmid, local, par, sums2, sums1]
        + kept
        + got
        + [Late(mid), Late(n2), Late(s2), Late(slope)],
        smem=1,
        parts=wd.arrays + others(wd, wu),
        scratch=[
            pltpu.VMEM((rows, model), F32),
            pltpu.VMEM((rows, LANE), BF16),
            pltpu.VMEM((chunks * mp_size, wd.rows, LANE), BF16),
            pltpu.VMEM((chunks * mp_size, wu.rows, LANE), BF16),
            pltpu.SemaphoreType.DMA,
            pltpu.SemaphoreType.DMA,
        ],
    )


def put_blocks(outs, mx, me_d, chunks, at_block, res, mp_first=False):
    half = chunks // 2
    for d in range(chunks):
        at = jnp.bitwise_xor(d, me_d)
        if mp_first:
            at = (mx // 2) * chunks + at
        else:
            at = (at // half) * chunks + (mx // 2) * half + at % half
        for b in range(res.shape[1] // LANE):
            rows = slice((at_block + b) * CHUNK, (at_block + b + 1) * CHUNK)
            outs[mx % 2][at, rows, :] = res[d * CHUNK : (d + 1) * CHUNK, b * LANE : (b + 1) * LANE]


def weight_grad_body(
    wd, mp_size, chunks, batch, mp_first, me_ref, n2_ref, dcomb_ref, b1_ref, b2_ref, att_ref,
    act_ref, s1_ref, *refs
):
    n_refs, refs = refs[:batch], refs[batch:]
    d_refs, refs = refs[: len(wd.arrays)], refs[len(wd.arrays) :]
    ups, downs, (local_ref, sums_ref), refs = refs[:2], refs[2:4], refs[4:6], refs[6:]
    w_scr, left, n_left, b1_left, z_scr, sem = refs
    w = wd.open(d_refs, me_ref, w_scr, sem, chunks)
    me_m, me_d = me_ref[0], me_ref[1]
    every = range(mp_size)
    need(n2_ref)
    left[...] = n2_ref[...].T
    stride = dcomb_ref.shape[1] // mp_size
    for mx in every:
        m = jnp.bitwise_xor(me_m, mx)
        res = nn(left[...], dcomb_ref[:, pl.ds(col(m * stride), stride)])
        put_blocks(ups, mx, me_d, chunks, 0, res.astype(BF16), mp_first)
    need(s1_ref, *n_refs)
    for r in range(batch):
        z_scr[rows_at(me_ref, r, n_refs[r].shape[0]), :] = n_refs[r][...]
    n = z_scr[...]
    n_left[...] = n.T
    b1f = b1_ref[...].astype(F32)
    s1 = s1_ref[...]
    d_z1 = (b1f * n.astype(F32) * s1 * (1.0 - s1)).astype(BF16)
    z_scr[...] = d_z1
    sums_ref[0:1, :] = jnp.sum(d_z1.astype(F32), axis=0, keepdims=True)
    sums_ref[1:8, :] = jnp.zeros((7, sums_ref.shape[1]), F32)
    b1_left[...] = b1_ref[...].T
    left[...] = b2_ref[...].T
    w.wait()
    local_ref[...] = b1f * s1 + nt(d_z1, w.wide([(m, 0) for m in every]))
    need(att_ref, act_ref)
    ff_m = act_ref.shape[1] // mp_size
    for mx in every:
        m = jnp.bitwise_xor(me_m, mx)
        cols = pl.ds(col(m * LANE), LANE)
        put_blocks(downs, mx, me_d, chunks, 0, nn(n_left[...], z_scr[:, cols]).astype(BF16))
        put_blocks(downs, mx, me_d, chunks, 1, nn(b1_left[...], att_ref[:, cols]).astype(BF16))
        res = nn(left[...], act_ref[:, pl.ds(col(m * ff_m), ff_m)])
        put_blocks(downs, mx, me_d, chunks, 2, res.astype(BF16))


def weight_grad(
    me, n2, dcomb, b1, b2, att, act, s1, n_rows, wd, mp_size, chunks, mp_first, after=()
):
    rows, model = b1.shape
    gates = Parts(wd.arrays, wd.order, wd.first_rows, CHUNK)
    height = dcomb.shape[1] // mp_size // LANE * CHUNK
    return call(
        functools.partial(weight_grad_body, gates, mp_size, chunks, len(n_rows), mp_first),
        "weight_grad",
        [sds((mp_size // 2 * chunks, height, LANE), BF16)] * 2
        + [sds((mp_size // 2 * chunks, wd.rows, LANE), BF16)] * 2
        + [sds((rows, model), F32), sds((8, model), F32)],
        [me, Late(n2), dcomb, b1, b2, Late(att), Late(act), Late(s1)]
        + [Late(n) for n in n_rows],
        smem=1,
        parts=wd.arrays,
        scratch=[pltpu.VMEM((chunks * mp_size, CHUNK, LANE), BF16)]
        + [pltpu.VMEM((model, rows), BF16)] * 3
        + [pltpu.VMEM((rows, model), BF16), pltpu.SemaphoreType.DMA],
        after=after,
    )


def swap(value, axis, size, bits):
    return lax.ppermute(value, axis, [(i, i ^ bits) for i in range(size)])


def add_body(count, *refs):
    left, right = refs[:2]
    outs = refs[2:]
    size = outs[0].shape[0]

    def step(i, carry):
        for part, out in enumerate(outs):
            at = part * size + i
            out[i] = (left[at].astype(F32) + right[at].astype(F32)).astype(BF16)
        return carry

    lax.fori_loop(0, size, step, 0)


def add(left, right, count, name="add"):
    shape = (left.shape[0] // count,) + left.shape[1:]
    return call(
        functools.partial(add_body, count),
        name,
        [sds(shape, BF16)] * count,
        [left, right],
    )


def join_body(count, has_sums, me_ref, *refs):
    pairs = [(refs[2 * i], refs[2 * i + 1]) for i in range(count)]
    refs = refs[2 * count :]
    if has_sums:
        sums_ref, refs = refs[0], refs[1:]
    for k, out in enumerate(refs):
        at = 0
        for left, right in pairs:
            rows = left.shape[1]
            out[at : at + rows, :] = (left[k].astype(F32) + right[k].astype(F32)).astype(BF16)
            at += rows
        if has_sums:
            tile = jnp.bitwise_xor(me_ref[1], k) // (LANE // CHUNK)
            out[at:, :] = sums_ref[:, pl.ds(col(tile * LANE), LANE)].astype(BF16)


def join(me, pairs, sums=None, name="add"):
    width = 4
    rows = sum(p[0].shape[1] for p in pairs) + (0 if sums is None else sums.shape[0])
    flat = [a for pair in pairs for a in pair]
    return call(
        functools.partial(join_body, len(pairs), sums is not None),
        name,
        [sds((rows, LANE), BF16)] * width,
        [me] + flat + ([] if sums is None else [sums]),
        smem=1,
    )


def total_body(*refs):
    value = refs[0][...].astype(F32)
    for ref in refs[1:-1]:
        value += ref[...].astype(F32)
    refs[-1][...] = value


def total(parts, name="add"):
    return call(total_body, name, [sds(parts[0].shape, F32)], parts)[0]


def stack_body(cuts, *refs):
    ins, outs = refs[: -len(cuts)], refs[-len(cuts) :]
    for i, ref in enumerate(ins):
        at = 0
        for out, rows in zip(outs, cuts):
            out[i] = ref[at : at + rows, :]
            at += rows


def stack(arrays, cuts=None, after=()):
    cuts = cuts or [arrays[0].shape[0]]
    return call(
        functools.partial(stack_body, cuts),
        "stack",
        [sds((len(arrays), rows, LANE), BF16) for rows in cuts],
        arrays,
        after=after,
    )


def copy_body(rows, *refs):
    half = len(refs) // 2
    for (first, count), a_ref, b_ref in zip(rows, refs[:half], refs[half:]):
        b_ref[...] = a_ref[:, first : first + count, :]


def copied(*pieces):
    return call(
        functools.partial(copy_body, [p[1:] for p in pieces]),
        "stack",
        [sds((a.shape[0], count, a.shape[2]), a.dtype) for a, _, count in pieces],
        [p[0] for p in pieces],
    )


def relay_body(*refs):
    pass


def relay(arrays, name="relay"):
    call(relay_body, name, [], [], after=arrays)


def pack_q_body(me_ref, qkv_ref, gains_ref, biases_ref, out_ref, scr):
    per = qkv_ref.shape[2]
    for c in range(3):
        out_ref[c * per : (c + 1) * per, :] = qkv_ref[0, c]
    scr[...] = jnp.zeros_like(scr)
    for l in range(gains_ref.shape[0]):
        for first, ref in ((0, gains_ref), (2, biases_ref)):
            rows = slice(8 * l + first, 8 * l + first + ref.shape[1])
            for lane in range(0, LANE, per):
                scr[rows, lane : lane + per] = ref[l].astype(F32)
    share = lax.broadcasted_iota(jnp.int32, scr.shape, 1) // per
    mine = jnp.where(share == me_ref[1] % (LANE // per), scr[...], 0.0)
    out_ref[3 * per :, :] = mine.astype(BF16)


def pack_q(me, qkv, gains, biases):
    per, rows = qkv.shape[2], 8 * gains.shape[0]
    return call(
        pack_q_body,
        "pack",
        [sds((3 * per + rows, LANE), BF16)],
        [me, qkv, gains, biases],
        smem=1,
        scratch=[pltpu.VMEM((rows, LANE), F32)],
    )[0]


def pack_body(layer, with_q, qkv_ref, gate_ref, out_ref, up_ref, down_ref, shard_ref):
    per = gate_ref.shape[2]
    at = 0
    if with_q:
        for c in range(3):
            shard_ref[at : at + per, :] = qkv_ref[layer, c]
            at += per
    refs = (gate_ref.at[layer, 0], out_ref.at[layer], down_ref.at[layer])
    for ref in refs + (gate_ref.at[layer, 1], up_ref.at[layer]):
        for b in range(ref.shape[1] // LANE):
            shard_ref[at : at + per, :] = ref[:, b * LANE : (b + 1) * LANE]
            at += per


def pack(layer, with_q, w_qkv, w_gate, w_out, w_up, w_down):
    per = w_gate.shape[2]
    cols = 2 * w_gate.shape[3] + w_out.shape[2] + w_up.shape[2] + w_down.shape[2]
    rows = (cols // LANE + 3 * with_q) * per
    return call(
        functools.partial(pack_body, layer, with_q),
        "pack",
        [sds((rows, LANE), BF16)],
        [w_qkv, w_gate, w_out, w_up, w_down],
    )[0]


def finish_body(counts, names, me_ref, *refs):
    ins, outs = refs[: sum(counts)], refs[sum(counts) :]
    d_qkv, d_out, d_gate, d_up, d_down, d_gains, d_norm_biases, d_gate_biases = outs
    per = CHUNK
    at = 0
    for count, pieces in zip(counts, names):
        value = ins[at][...].astype(F32)
        for ref in ins[at + 1 : at + count]:
            value += ref[...].astype(F32)
        at += count
        row = 0
        for name, l in pieces:
            if name == "p":
                low, high = value[row:, :CHUNK], value[row:, CHUNK:]
                value = jnp.where(me_ref[1] % 2 == 0, low, high)
                for i in range(value.shape[0] // 8):
                    for out, first in ((d_gains, 0), (d_norm_biases, 2), (d_gate_biases, 3)):
                        step = 1 if out is d_gains else 2
                        for j in range(2):
                            at_row = 8 * i + first + j * step
                            out[i, j : j + 1, :] = value[at_row : at_row + 1]
                continue
            blocks = {"q": 3, "u": 1 + d_up.shape[2] // LANE, "d": 2 + d_down.shape[2] // LANE}
            for b in range(blocks[name]):
                block = value[row : row + per]
                row += per
                if name == "q":
                    d_qkv[l, b] = block
                elif name == "u" and b == 0:
                    d_gate[l, 1] = block
                elif name == "u":
                    d_up[l, :, (b - 1) * LANE : b * LANE] = block
                elif b == 0:
                    d_gate[l, 0] = block
                elif b == 1:
                    d_out[l] = block
                else:
                    d_down[l, :, (b - 2) * LANE : (b - 1) * LANE] = block


def finish(me, layers, ff_m, groups):
    shapes = [(3, CHUNK, LANE), (CHUNK, LANE), (2, CHUNK, LANE), (CHUNK, ff_m), (CHUNK, ff_m)]
    out = [sds((layers,) + shape, F32) for shape in shapes] + [sds((layers, 2, CHUNK), F32)] * 3
    return call(
        functools.partial(finish_body, [len(g[0]) for g in groups], [g[1] for g in groups]),
        "finish",
        out,
        [me] + [a for g in groups for a in g[0]],
        smem=1,
    )


def solution(mesh):
    dp_size, mp_size, width_size = (mesh.shape[a] for a in ("dp", "mp", "width"))
    all_axes = ("mp", "dp", "width")
    direct = (dp_size, mp_size, width_size) == (2, 4, 4)

    def mp_swap(value, bits):
        return swap(value, "mp", mp_size, bits)

    def dp_swap(value):
        return swap(value, "dp", dp_size, 1)

    def spread(value):
        return [value, mp_swap(value, 1), mp_swap(value, 2)]

    def spread_last(values):
        return values + [mp_swap(values[2], 1)]

    def exchange(own, near, far):
        far = mp_swap(far, 2)
        return [own, mp_swap(near, 1), far, mp_swap(far, 1)]

    def send_width(value):
        return [value] + [swap(value, "width", width_size, k) for k in range(1, width_size)]

    def swap_width(values):
        return [values[0]] + [
            swap(values[k], "width", width_size, k) for k in range(1, width_size)
        ]

    def on_device(
        tokens, segments, cotangent, norm_gains, biases, w_qkv, w_out, w_gate, w_up, w_down
    ):
        ORDER.token = None
        batch, part, model = tokens.shape
        layers = w_qkv.shape[0]
        per = w_qkv.shape[1]
        chunks = model // CHUNK
        half = chunks // 2
        ff_m = w_up.shape[2]
        ff_blocks = ff_m // LANE
        ff = ff_m * mp_size
        me_m = lax.axis_index("mp")
        me_d = lax.axis_index("dp") * width_size + lax.axis_index("width")
        rows = [jnp.where(segments[0, -1] < 0, 0, batch - 1)]
        rows += [batch - 1 - rows[0]] if batch == 2 else []
        me = jnp.stack([me_m, me_d] + rows).astype(jnp.int32)
        me_pack, me_att = me, me
        if not direct:
            me_pack = jnp.stack([0 * me_m, 0 * me_d] + rows).astype(jnp.int32)
            me_att = jnp.stack([me_m, 0 * me_d] + rows).astype(jnp.int32)

        def blocks_of(matrix):
            return jnp.swapaxes(matrix.reshape(per, -1, LANE), 0, 1).reshape(-1, LANE)

        qkv_t, out_t, down_t = (jnp.swapaxes(w, 1, 2) for w in (w_qkv, w_out, w_down))

        def param_block():
            params = jnp.concatenate([norm_gains, biases], axis=1)
            params = jnp.pad(params, ((0, 0), (0, 2), (0, 0))).reshape(layers * 8, per)
            rows = jnp.concatenate([params] * (LANE // per), axis=1)
            share = lax.broadcasted_iota(jnp.int32, rows.shape, 1) // per
            return jnp.where(share == me_d % (LANE // per), rows, 0)

        q_rows, d_rows, u_rows = 3 * CHUNK, (2 + ff_blocks) * CHUNK, (1 + ff_blocks) * CHUNK

        def shard(l, q):
            mats = [w_gate[l, 0], out_t[l], blocks_of(down_t[l]), w_gate[l, 1], blocks_of(w_up[l])]
            return jnp.concatenate(([qkv_t[l].reshape(-1, LANE)] if q else []) + mats, axis=0)

        def gather_whole(shard, extra):
            full = lax.all_gather(shard, all_axes, axis=0, tiled=False)
            if per == CHUNK:
                return full
            count = (shard.shape[0] - extra) // per
            full = full.reshape(mp_size, chunks, CHUNK // per, shard.shape[0], LANE)
            mats = full[:, :, :, : count * per]
            mats = mats.reshape(mp_size, chunks, CHUNK // per, count, per, LANE)
            mats = jnp.swapaxes(mats, 2, 3).reshape(mp_size * chunks, count * CHUNK, LANE)
            if not extra:
                return mats
            pars = jnp.sum(full[:, :, :, count * per :].astype(F32), axis=2).astype(BF16)
            return jnp.concatenate([mats, pars.reshape(mp_size * chunks, extra, LANE)], axis=1)

        def reduce_whole(even, odd):
            full = jnp.stack([even, odd], axis=1)
            full = full.reshape(2, mp_size // 2, half, 2, -1, CHUNK // per, per, LANE)
            full = jnp.transpose(full, (1, 3, 0, 2, 5, 4, 6, 7)).reshape(-1, LANE).astype(F32)
            return lax.psum_scatter(full, all_axes, scatter_dimension=0, tiled=True)

        def reduce_q_whole(grad):
            full = grad.reshape(chunks, -1, CHUNK // per, per, LANE)
            full = jnp.swapaxes(full, 1, 2).reshape(-1, LANE).astype(F32)
            return lax.psum_scatter(full, ("dp", "width"), scatter_dimension=0, tiled=True)

        seg = jnp.where(rows[0] == 0, segments, segments[::-1]) if batch == 2 else segments
        segs = (seg, seg[:, None, :].astype(F32))

        q_all = q_rows + layers * 8
        weights = [None] * layers
        if direct:
            mats = (qkv_t, w_gate, out_t, w_up, down_t)
            q_steps = send_width(pack_q(me, qkv_t, norm_gains, biases))
            t_all = spread(tokens)
            w_steps = send_width(pack(0, False, *mats))
            relay([], "pack")
            (q_base,) = stack(q_steps)
            t_far = copied((t_all[2], 0, part))[0]
            wq = Parts([q_base, dp_swap(q_base)], [(0, 0), (0, 4)], 0, q_all)
            (base,) = stack(w_steps)
            got = {(0, 0): base, (0, 4): dp_swap(base), (2, 0): mp_swap(base, 2)}
            later = send_width(pack(1, True, *mats))
            relay([wq.arrays[1]])
            t_all = t_all + [mp_swap(t_far, 1)]
        else:
            t_all = spread_last(spread(tokens))
            q_sh = jnp.concatenate([qkv_t[0].reshape(-1, LANE), param_block()], axis=0)
            wq = Parts([gather_whole(q_sh, layers * 8)], None, 0, q_all)
            full = gather_whole(shard(0, False), 0)
            wd, wu = Parts([full], None, 0, d_rows), Parts([full], None, d_rows, u_rows)
            for l in range(1, layers):
                full = gather_whole(shard(l, True), 0)
                weights[l] = (
                    Parts([full], None, 0, q_rows),
                    Parts([full], None, q_rows, d_rows),
                    Parts([full], None, q_rows + d_rows, u_rows),
                )

        def last_step(got):
            d_last, u_last = copied((got[2, 0], 0, d_rows), (got[0, 4], d_rows, u_rows))
            return dp_swap(d_last), mp_swap(u_last, 2)

        def two_pieces(got, lasts):
            for m, d in list(got):
                got[m + 1, d] = mp_swap(got[m, d], 1)
            arrays, order = list(got.values()), list(got) + [(2, 4), (3, 4)]
            lasts = copied(*[(a, 0, a.shape[1]) for a in lasts])
            d_all, u_all = (arrays + [a, mp_swap(a, 1)] for a in lasts)
            return (
                Parts(d_all, order, 0, d_rows),
                Parts(u_all, order, [d_rows] * len(arrays) + [0, 0], u_rows),
            )

        x = tokens.reshape(batch * part, model)
        par = None
        saved = []
        t_parts = t_all
        for l in range(layers):
            if l and direct:
                wq = wq_next
            elif l:
                wq, wd, wu = weights[l]
            qkv, lse, own, near, far, *rest = attend(
                me, segs, t_parts, wq, l, layers, l == 0, chunks
            )
            kept = (qkv, lse)
            if l == 0:
                par = rest[0]
                n_parts = [rest[1 + r * mp_size : 1 + (r + 1) * mp_size] for r in range(batch)]
            else:
                n_parts = [t_parts[r::batch] for r in range(batch)]
            o_parts = exchange(own, near, far)
            if direct:
                if l == 0:
                    relay([got[0, 4], got[2, 0]] + later[1:])
                    lasts = last_step(got)
                    relay([o_parts[2]])
                wd, wu = two_pieces(got, lasts)
                if l == 0:
                    q_base, base = stack(later, [q_rows, d_rows + u_rows])
                    wq_next = Parts([q_base, dp_swap(q_base)], [(0, 0), (0, 4)], 0, q_rows)
                    got = {(0, 0): base, (0, 4): dp_swap(base), (2, 0): mp_swap(base, 2)}
                else:
                    wq = wq_next
                weights[l] = (wq, wd, wu)
            elif l == 0:
                weights[0] = (wq, wd, wu)
            n_rows = [n_parts[r][0] for r in range(batch)]
            att, s1, mid, n2, s2, act, slope, out, *following = second(
                me, x, par, n_rows, o_parts, wd, wu, l, chunks, ff, l + 1 < layers
            )
            saved.append((x, n_parts, kept, att, s1, mid, n2, s2, act, slope))
            x = out
            if following:
                t_rows = [spread(n) for n in following]
                if direct:
                    relay([got[0, 4], got[2, 0], wq_next.arrays[1]] + [t[2] for t in t_rows])
                    lasts = last_step(got)
                t_rows = [spread_last(t) for t in t_rows]
                t_parts = [t_rows[r][mx] for mx in range(mp_size) for r in range(batch)]
        output = x.reshape(batch, part, model)

        own = lax.dynamic_slice_in_dim(segments, me_m * part, part, 1)
        g = cotangent.astype(F32) * (own >= 0).astype(F32)[:, :, None]
        g = g.reshape(batch * part, model)
        reduced = [None] * layers
        all_sums = [None] * layers
        moving = {}

        def reduce_2(name, mp_first=False):
            if name in moving:
                keep, send = add(*moving[name], 2)
                moving[name] = (keep, mp_swap(send, 2) if mp_first else dp_swap(send))

        def reduce_3(name, mp_first=False):
            if name in moving:
                keep, send = add(*moving[name], 2, "sum" if mp_first or name == ("d", 0) else "add")
                moving[name] = (keep, dp_swap(send) if mp_first else mp_swap(send, 2))

        def reduce_4(names, sums=None):
            if direct:
                pairs = [moving.pop(name) for name in names]
                moving[names[0]] = swap_width(join(me, pairs, sums, "sum" if names[0][1] == 0 else "add"))

        def reduce_5(name):
            return total(moving.pop(name), "sum" if name[1] == 0 else "add") if direct else None

        for l in reversed(range(layers)):
            wq, wd, wu = weights[l]
            x, n_parts, kept, att, s1, mid, n2, s2, act, slope = saved[l]
            n_rows = [n_parts[r][0] for r in range(batch)]
            final, first_of_two = l == 0, l + 1 < layers
            if first_of_two:
                all_sums[l + 1], b2, dcomb, gmid, b1, sums2, *o_parts = turn(
                    me, upper, keeps, gots, (mid, n2, s2, slope), wd, wu, l, mp_size, chunks
                )
            else:
                b2, dcomb, gmid, b1, sums2, *o_parts = second_back(
                    me, g, mid, n2, s2, slope, par, wd, wu, l, mp_size, chunks, batch
                )
            d_parts = exchange(*o_parts)
            if first_of_two:
                reduce_4([("q", l + 1), ("u", l + 1)])
            reduce_3(("d", l + 1))
            *grads, local, sums1 = weight_grad(
                me_pack, n2, dcomb, b1, b2, att, act, s1, n_rows, wd, mp_size, chunks,
                final and direct,
            )
            relay([d_parts[2]])
            if direct:
                moving["u", l] = (grads[0], mp_swap(grads[1], 1))
                moving["d", l] = (grads[2], mp_swap(grads[3], 1))
            keeps, gots = [], []
            q_grad = None
            for r in range(batch):
                keep, send, q_grad = attend_back(
                    me_att, *segs, *kept, d_parts, n_parts[r], wq, r, chunks, q_grad
                )
                if r == 0:
                    if first_of_two:
                        reduce_4([("d", l + 1)])
                    reduce_2(("d", l))
                    reduce_2(("u", l), final)
                    if first_of_two:
                        moving["q", l + 1] = [reduce_5(("q", l + 1))] if direct else None
                else:
                    reduce_3(("u", l), final)
                    if final:
                        reduce_3(("d", l))
                keep, send = add(keep, mp_swap(send, 1), 2)
                keeps.append(keep.reshape(keep.shape[1:]))
                gots.append(mp_swap(send, 2).reshape(keep.shape[1:]))
            if direct and first_of_two:
                moving["d", l + 1] = [reduce_5(("d", l + 1))]
            if direct:
                moving["q", l] = (q_grad[:half], dp_swap(q_grad[half:]))
                if final:
                    reduce_4([("u", l)])
            upper = (x, gmid, local, par, sums2, sums1)
            if final:
                g, all_sums[l] = first_back(me, *upper, keeps, gots, l)
            if direct and final:
                reduce_4([("q", l), ("d", l)])
                moving["u", l] = [reduce_5(("u", l))]
            if not direct:
                reduced[l] = (reduce_q_whole(q_grad), reduce_whole(*grads[:2]), reduce_whole(*grads[2:]))
        d_tokens = g.reshape(batch, part, model)
        sums = jnp.concatenate(all_sums, axis=0)
        if direct:
            sums = sums + mp_swap(sums, 1)
            sums = sums + mp_swap(sums, 2)
            sums = sums + dp_swap(sums)
            moving["p", 0] = swap_width(join(me, [], sums))
            groups = [
                (moving["q", 1], [("q", 1), ("u", 1)]),
                (moving["d", 1], [("d", 1)]),
                (moving["u", 0], [("u", 0)]),
                (moving["q", 0], [("q", 0), ("d", 0)]),
                (moving["p", 0], [("p", 0)]),
            ]
            stacked = finish(me, layers, ff_m, groups)
            stacked, small = stacked[:5], stacked[5:]
        else:
            params = lax.dynamic_slice_in_dim(lax.psum(sums, all_axes), me_d * per, per, 1)
            params = params.reshape(layers, 8, per)
            small = [params[:, 0:2], params[:, 2:6:2], params[:, 3:6:2]]

        def unblocks(rows, count):
            return jnp.swapaxes(rows.reshape(count, per, LANE), 0, 1).reshape(per, count * LANE)

        if not direct:
            grads = []
            for q_sum, up_sum, down_sum in reduced:
                grads.append(
                    (
                        q_sum.reshape(3, per, LANE),
                        down_sum[per : 2 * per],
                        jnp.stack([down_sum[:per], up_sum[:per]]),
                        unblocks(up_sum[per:], ff_blocks),
                        unblocks(down_sum[2 * per :], ff_blocks),
                    )
                )
            stacked = [jnp.stack([grads[l][i] for l in range(layers)]) for i in range(5)]
        for i in (0, 1, 4):
            stacked[i] = jnp.swapaxes(stacked[i], 1, 2)
        return (
            output,
            d_tokens,
            *small,
            *stacked,
        )

    placed = (
        P(("dp", "width"), "mp", None),
        P(("dp", "width"), None),
        P(("dp", "width"), "mp", None),
        P(None, None, ("dp", "width")),
        P(None, None, ("dp", "width")),
        P(None, ("dp", "width"), None, "mp"),
        P(None, "mp", ("dp", "width")),
        P(None, None, ("dp", "width"), "mp"),
        P(None, ("dp", "width"), "mp"),
        P(None, "mp", ("dp", "width")),
    )
    return jax.shard_map(
        on_device,
        mesh=mesh,
        in_specs=placed,
        out_specs=(
            placed[0],
            placed[0],
            placed[3],
            placed[3],
            placed[3],
            placed[5],
            placed[6],
            placed[7],
            placed[8],
            placed[9],
        ),
        check_vma=False,
    )
```
